32 devices in a mesh: vis: 2 (over x), grp: 8 (over z, core), enc: 2 (over y).
Axes of the slice: x: 2, y: 2, z: 4, core: 2. Of those that a mesh axis runs over, the one named last changes fastest.
Arguments:
- image_tokens: bfloat16 [8, 256, 6144], P('grp', None, 'enc'), may hold values from -8 to 8
- vision_gain: float32 [6144], P('enc'), may hold values from 0.1 to 1.9
- up_weight: bfloat16 [6144, 12288], P('enc', ('vis', 'grp')), may hold values from -0.078125 to 0.078125
- down_weight: bfloat16 [12288, 6144], P(('vis', 'grp'), 'enc'), may hold values from -0.0546875 to 0.0546875
- project_weight: bfloat16 [6144, 4096], P('enc', 'vis'), may hold values from -0.078125 to 0.078125
- encoder_gain: float32 [4096], P('vis'), may hold values from 0.1 to 1.9
- qkv_weight: bfloat16 [3, 4096, 2048], P(None, 'vis', 'enc'), may hold values from -0.6 to 0.6
- out_weight: bfloat16 [2048, 4096], P('enc', 'vis'), may hold values from -0.5 to 0.5
- captions: bfloat16 [32, 16, 4096], P('grp', 'enc', 'vis'), may hold values from -8 to 8
- cand_counts: int32 [8], replicated, may hold values from 1 to 12, 32 in all
- caption_lengths: int32 [32], P('grp'), may hold values from 1 to 16
Outputs:
- vision_out: bfloat16 [8, 256, 6144], P('grp', None, 'enc')
- caption_out: bfloat16 [32, 16, 4096], P('grp', 'enc', 'vis')
The draws below stay inside these ranges and needn't reach their ends.
Inputs may be any that keep to these rules, and one draw needn't show every extreme that they name: `cand_counts`: every image has at least one candidate, the counts sum to 32 and the largest is 12.
All inputs are finite; a program needn't handle non-finite values.
Results may differ from the reference program's by a relative error of at most 0.035.
Values may be sent and summed in bfloat16 or wider, within the bound.
No kernel may reach another device: no remote copies, remote signals or barrier semaphores. Data moves between devices by JAX's collectives and lax.ppermute only.
A program may use at most 192 MiB of HBM per device.

```python
import math
import jax
import jax.numpy as jnp
import numpy as np
from jax import lax

D = 6144
FFW = 12288
R = 256
DE = 4096
HE = 8
DH = 256
CAP = 16
IMAGES = 8
CANDS = 32
MOSTC = 12
INNER = 2048


def rising_scale(count, lowest, highest):
    fraction = jnp.arange(count, dtype=jnp.float32) / (count - 1)
    return lowest * (highest / lowest) ** fraction


def draw_image_tokens(key, part):
    key = jax.random.fold_in(key, 21)
    values = jax.random.normal(key, (IMAGES, R, D), jnp.float32) * rising_scale(D, 0.5, 2.0)
    return jnp.clip(values, -8.0, 8.0).astype(jnp.bfloat16)


def draw_captions(key, part):
    key = jax.random.fold_in(key, 23)
    values = jax.random.normal(key, (CANDS, CAP, DE), jnp.float32) * rising_scale(DE, 0.5, 2.0)
    return jnp.clip(values, -8.0, 8.0).astype(jnp.bfloat16)


def draw_qkv_weight(key, part):
    key = jax.random.fold_in(key, 11)
    first = jax.random.fold_in(key, 0)
    base = jax.random.normal(first, (3, DE, HE * DH), jnp.float32) * DE ** (-0.5)
    base = base * (rising_scale(DE, 0.125, 8.0) / 2.77)[None, :, None]
    return jnp.clip(base, -0.59375, 0.59375).astype(jnp.bfloat16)


def place_ends(values, key, least, largest):
    index_at = [jax.random.randint(jax.random.fold_in(key, axis), (), 0, length) for axis, length in enumerate(values.shape)]
    widest = values.shape.index(max(values.shape))
    neighbour = index_at[:widest] + [(index_at[widest] + 1) % values.shape[widest]] + index_at[widest + 1:]
    return values.at[tuple(index_at)].set(least).at[tuple(neighbour)].set(largest)


def steps_of(own_key, dims, cuts, low, high):
    gain, own = 1.0, jax.random.fold_in(own_key, 6)
    for axis_at, blocks in cuts:
        steps = jnp.exp(jax.random.uniform(jax.random.fold_in(own, axis_at), (blocks,), jnp.float32, low / len(cuts), high / len(cuts)))
        gain = gain * jnp.repeat(steps, dims[axis_at] // blocks).reshape([-1 if axis == axis_at else 1 for axis in range(len(dims))])
    return gain


def split_up(count, total, reach, lean):
    portions = [(1 << 20) // math.isqrt(grade ** lean) + 1 for grade in range(2, count + 1)]
    surplus, given = total - reach - (count - 1), [1] * (count - 1)
    while surplus > 0:
        free = [i for i in range(count - 1) if given[i] < reach]
        whole, remaining = sum([portions[i] for i in free]), surplus
        for i in free:
            addition = min(reach - given[i], max(1, remaining * portions[i] // whole), surplus)
            given[i] = given[i] + addition
            surplus = surplus - addition
    return np.array([reach] + given)


def uneven(key, amount, total, most, slope):
    if amount == 2:
        one = jax.random.randint(key, (), max(1, total - most), min(most, total - 1) + 1)
        return jnp.stack([one, total - one])
    lengths = jnp.asarray(split_up(amount, total, most, slope), jnp.int32)
    couples = (amount - 1) // 2
    giver, taker = lengths[1:1 + 2 * couples:2], lengths[2:2 + 2 * couples:2]
    room = jnp.minimum(giver - 1, most - taker)
    shifted = jax.random.randint(jax.random.fold_in(key, 1), (couples,), 0, 1 << 20) % (room + 1)
    lengths = lengths.at[1:1 + 2 * couples:2].set(giver - shifted).at[2:2 + 2 * couples:2].set(taker + shifted)
    return lengths[jax.random.permutation(jax.random.fold_in(key, 2), amount)]


def bell_draw(key, shape, scale, limit, shards=(), kind=jnp.bfloat16):
    loudness = steps_of(key, shape, shards, -0.22, 0.18) if shards else 1.0
    result = jax.random.normal(key, shape, jnp.float32) * scale * loudness
    return jnp.minimum(jnp.maximum(result, -limit), limit).astype(kind)


def setup_inputs(seed: int = 0) -> dict:
    keys = jax.random.split(jax.random.key(seed), 12)
    return {
        "image_tokens": draw_image_tokens(jax.random.fold_in(keys[11], 71), 0),
        "vision_gain": jnp.clip(1.0 + 0.18 * jax.random.normal(keys[1], (D,), jnp.float32), 0.1, 1.9),
        "up_weight": bell_draw(keys[2], (D, FFW), D ** -0.5, 0.078125, ((0, 2), (1, 16))),
        "down_weight": bell_draw(keys[3], (FFW, D), FFW ** -0.5, 0.0546875, ((0, 16), (1, 2))),
        "project_weight": bell_draw(keys[4], (D, DE), D ** -0.5, 0.078125, ((0, 2), (1, 2))),
        "encoder_gain": jnp.clip(1.0 + 0.18 * jax.random.normal(keys[5], (DE,), jnp.float32), 0.1, 1.9),
        "qkv_weight": draw_qkv_weight(jax.random.fold_in(keys[11], 71), 0),
        "out_weight": bell_draw(keys[7], (INNER, DE), (INNER // 16) ** -0.5, 0.5, ((0, 2), (1, 2))),
        "captions": draw_captions(jax.random.fold_in(keys[11], 71), 0),
        "cand_counts": uneven(keys[9], IMAGES, CANDS, MOSTC, 2).astype(jnp.int32),
        "caption_lengths": place_ends(jax.random.randint(keys[10], (CANDS,), 1, CAP + 1), jax.random.fold_in(keys[10], 1), 1, CAP).astype(jnp.int32),
    }


EPSILON = 1e-06
FLOOR = -1e+30

def image_of(counts, total):
    ends = jnp.cumsum(counts)
    index = jnp.arange(total, dtype=jnp.int32)
    return lax.optimization_barrier(jnp.sum((index[:, None] >= ends[None, :]).astype(jnp.int32), axis=1))

def reference(image_tokens, vision_gain, up_weight, down_weight, project_weight, encoder_gain, qkv_weight, out_weight, captions, cand_counts, caption_lengths):
    tokens = image_tokens.astype(jnp.float32)
    mean = lax.optimization_barrier(jnp.mean(tokens, axis=-1, keepdims=True))
    spread = lax.optimization_barrier(jnp.mean(tokens * tokens, axis=-1, keepdims=True)) - mean * mean
    normed = ((tokens - mean) * lax.rsqrt(spread + EPSILON) * vision_gain).astype(jnp.bfloat16)

    def vision_layer(pair):
        rows_in, rows_normed = pair
        pre = jnp.dot(rows_normed, up_weight, preferred_element_type=jnp.float32)
        hidden = jax.nn.gelu(pre, approximate=False).astype(jnp.bfloat16)
        return (rows_in + jnp.dot(hidden, down_weight, preferred_element_type=jnp.float32)).astype(jnp.bfloat16)
    vision_out = lax.map(vision_layer, (tokens, normed))
    flat_rows = vision_out.reshape(IMAGES * R, D)
    embedded = jnp.dot(flat_rows, project_weight, preferred_element_type=jnp.float32)
    image_normed = (embedded * lax.rsqrt(lax.optimization_barrier(jnp.mean(embedded * embedded, axis=-1, keepdims=True)) + EPSILON) * encoder_gain).astype(jnp.bfloat16)
    image_keys = jnp.dot(image_normed, qkv_weight[1], preferred_element_type=jnp.float32).astype(jnp.bfloat16).reshape(IMAGES, R, HE, DH)
    image_values = jnp.dot(image_normed, qkv_weight[2], preferred_element_type=jnp.float32).astype(jnp.bfloat16).reshape(IMAGES, R, HE, DH)
    words = captions.astype(jnp.float32)
    word_normed = (words * lax.rsqrt(lax.optimization_barrier(jnp.mean(words * words, axis=-1, keepdims=True)) + EPSILON) * encoder_gain).astype(jnp.bfloat16)
    word_flat = word_normed.reshape(CANDS * CAP, DE)
    word_query = jnp.dot(word_flat, qkv_weight[0], preferred_element_type=jnp.float32).astype(jnp.bfloat16).reshape(CANDS, CAP, HE, DH)
    word_keys = jnp.dot(word_flat, qkv_weight[1], preferred_element_type=jnp.float32).astype(jnp.bfloat16).reshape(CANDS, CAP, HE, DH)
    word_values = jnp.dot(word_flat, qkv_weight[2], preferred_element_type=jnp.float32).astype(jnp.bfloat16).reshape(CANDS, CAP, HE, DH)
    owner = image_of(cand_counts, CANDS)
    positions = jnp.arange(CAP, dtype=jnp.int32)

    def attend(args):
        query, own_keys, own_values, image, length = args
        keys_here = lax.dynamic_index_in_dim(image_keys, image, 0, keepdims=False)
        values_here = lax.dynamic_index_in_dim(image_values, image, 0, keepdims=False)
        all_keys = jnp.concatenate([keys_here, own_keys], axis=0).astype(jnp.float32)
        all_values = jnp.concatenate([values_here, own_values], axis=0).astype(jnp.float32)
        scores = jnp.einsum('qhd,khd->hqk', query.astype(jnp.float32), all_keys) * DH ** (-0.5)
        live = jnp.concatenate([jnp.ones((R,), dtype=bool), positions < length])
        scores = jnp.where(live[None, None, :], scores, FLOOR)
        top = lax.optimization_barrier(jnp.max(scores, axis=-1, keepdims=True))
        weights = jnp.where(live[None, None, :], jnp.exp(scores - top), 0.0)
        total = lax.optimization_barrier(jnp.sum(weights, axis=-1))
        rounded = lax.optimization_barrier(weights.astype(jnp.bfloat16)).astype(jnp.float32)
        mixed = jnp.einsum('hqk,khd->qhd', rounded, all_values) / jnp.transpose(total)[:, :, None]
        return mixed.astype(jnp.bfloat16).reshape(CAP, HE * DH)
    attended = lax.map(attend, (word_query, word_keys, word_values, owner, caption_lengths))
    branch = jnp.dot(attended.reshape(CANDS * CAP, HE * DH), out_weight, preferred_element_type=jnp.float32)
    caption_out = (words + branch.reshape(CANDS, CAP, DE)).astype(jnp.bfloat16)
    return (vision_out, caption_out)
```

```python
import jax
import jax.numpy as jnp
from jax import lax
from jax.sharding import PartitionSpec as P

DH = 256
CAP = 16
MOSTC = 12


EPSILON = 1e-06
FLOOR = -1e30


def image_of(counts, candidate):
    ends = jnp.cumsum(counts)
    return jnp.sum((candidate[:, None] >= ends[None, :]).astype(jnp.int32), axis=1)


def dot(a, b):
    return jnp.dot(a, b, preferred_element_type=jnp.float32)


def wide(a):
    return a.astype(jnp.float32)


def slim(a):
    return a.astype(jnp.bfloat16)


def shifted(value, axis, step):
    count = lax.axis_size(axis)
    return lax.ppermute(value, axis, [(i, (i + step) % count) for i in range(count)])


def summed(value, axis):
    if lax.axis_size(axis) != 2:
        return lax.psum(value, axis)
    return value + shifted(value, axis, 1)


def joined(value, axis, dim):
    if lax.axis_size(axis) != 2:
        return lax.all_gather(value, axis, axis=dim, tiled=True)
    other = shifted(value, axis, 1)
    first = lax.axis_index(axis) == 0
    return jnp.concatenate(
        [jnp.where(first, value, other), jnp.where(first, other, value)], axis=dim
    )


def on_device(
    image_tokens,
    vision_gain,
    up_weight,
    down_weight,
    project_weight,
    encoder_gain,
    qkv_weight,
    out_weight,
    captions,
    cand_counts,
    caption_lengths,
):
    vis_count = lax.axis_size("vis")
    enc_count = lax.axis_size("enc")
    groups = lax.axis_size("grp")
    vis = lax.axis_index("vis")
    group = lax.axis_index("grp")
    rows, features = image_tokens.shape[1:]
    all_features = features * enc_count
    width = captions.shape[2] * vis_count
    pair = vis_count == 2
    part_rows = rows // vis_count

    cores = 2 if groups % 2 == 0 else 1
    places = groups // cores
    up_parts, down_parts = [up_weight], [down_weight]
    if cores == 2:
        swap = [(i, i ^ 1) for i in range(groups)]
        up_parts.append(lax.ppermute(up_weight, "grp", swap))
        down_parts.append(lax.ppermute(down_weight, "grp", swap))

    def to_place(value, step):
        return lax.ppermute(
            value, "grp", [(i, (i + step * cores) % groups) for i in range(groups)]
        )

    def mine_of(value):
        return lax.dynamic_slice_in_dim(value, vis * part_rows, part_rows, axis=0)

    def by_halves(value):
        if not pair:
            return value
        return jnp.concatenate(
            [mine_of(value), lax.dynamic_slice_in_dim(value, (1 - vis) * part_rows, part_rows, axis=0)]
        )

    def all_rows(mine):
        if not pair:
            return lax.all_gather(mine, "vis", axis=0, tiled=True)
        return jnp.concatenate([mine, shifted(mine, "vis", 1)])

    def my_rows_sum(value):
        if not pair:
            return lax.psum_scatter(value, "vis", scatter_dimension=0, tiled=True)
        return value[:part_rows] + wide(shifted(slim(value[part_rows:]), "vis", 1))

    tokens = wide(image_tokens[0])
    row_total, row_squares = summed(
        jnp.stack([jnp.sum(tokens, axis=-1), jnp.sum(tokens * tokens, axis=-1)]), "enc"
    )
    mean = row_total / all_features
    spread = row_squares / all_features - mean * mean
    normed = slim(
        (tokens - mean[:, None]) * lax.rsqrt(spread + EPSILON)[:, None] * vision_gain
    )
    my_normed = mine_of(normed)

    def pre_of(block):
        return [dot(block, weight) for weight in up_parts]

    def out_of(pre):
        total = None
        for part, weight in zip(pre, down_parts):
            if enc_count == 2:
                full = part + wide(shifted(slim(part), "enc", 1))
            else:
                full = lax.psum(part, "enc")
            term = dot(slim(jax.nn.gelu(full, approximate=False)), weight)
            total = term if total is None else total + term
        return total

    order = [0] + list(range(1, places))
    my_out = None
    blocks = [by_halves(normed)]
    blocks += [all_rows(to_place(my_normed, step)) for step in order[1:]]
    for step, block in zip(order, blocks):
        partial = my_rows_sum(out_of(pre_of(block)))
        if step:
            partial = wide(to_place(slim(partial), -step))
        my_out = partial if my_out is None else my_out + partial
    my_vision = slim(mine_of(tokens) + my_out)

    inner = qkv_weight.shape[2]
    heads = inner // DH
    shares = vis_count if heads % vis_count == 0 else 1
    share = inner // shares
    words = wide(captions)
    all_words = wide(joined(captions, "enc", 1))
    word_power = summed(jnp.sum(all_words * all_words, axis=-1), "vis")
    word_normed = slim(
        all_words * lax.rsqrt(word_power / width + EPSILON)[..., None] * encoder_gain
    )
    cand_local = word_normed.shape[0]
    word_rows = cand_local * CAP
    flat_words = word_normed.reshape(word_rows, word_normed.shape[2])

    def head_weights(which):
        return lax.dynamic_slice_in_dim(qkv_weight, which * share, share, axis=2)

    def head_sum(values, scale=None):
        if shares == 1:
            return lax.psum(values, "vis")
        return lax.psum_scatter(values, "vis", scatter_dimension=2, tiled=True)

    if pair and shares == 2:
        my_heads, other_heads = head_weights(vis), head_weights(1 - vis)

        def project_heads(block, first):
            sent = jnp.einsum(
                "rd,kdh->rkh", block, other_heads[first:], preferred_element_type=jnp.float32
            )
            kept = jnp.einsum(
                "rd,kdh->rkh", block, my_heads[first:], preferred_element_type=jnp.float32
            )
            return kept, slim(sent)

        kept, sent = project_heads(flat_words, 0)
        word_qkv = slim(kept + wide(shifted(sent, "vis", 1)))
    else:
        word_qkv = slim(
            head_sum(
                jnp.einsum(
                    "rd,kdh->rkh", flat_words, qkv_weight, preferred_element_type=jnp.float32
                )
            )
        )
    every_word = lax.all_gather(word_qkv, "grp", axis=0, tiled=True)
    every_length = lax.all_gather(wide(caption_lengths), "grp", axis=0, tiled=True)

    def embed(block):
        partial = dot(block, project_weight)
        if enc_count == 2:
            full = partial + wide(shifted(slim(partial), "enc", 1))
        else:
            full = lax.psum(partial, "enc")
        return slim(full * encoder_gain), jnp.sum(full * full, axis=-1)

    if pair and shares == 2:
        other_vision = shifted(my_vision, "vis", 1)
        vision_rows = jnp.where(
            vis == 0,
            jnp.concatenate([my_vision, other_vision]),
            jnp.concatenate([other_vision, my_vision]),
        )
        pieces = []
        for block in (my_vision, other_vision):
            scaled, power = embed(block)
            pieces.append(project_heads(scaled, 1) + (power,))
        image_kv = []
        for here, there in ((0, 1), (1, 0)):
            total = pieces[here][0] + wide(shifted(pieces[there][1], "vis", 1))
            power = pieces[here][2] + shifted(pieces[there][2], "vis", 1)
            image_kv.append(
                slim(total * lax.rsqrt(power / width + EPSILON)[:, None, None])
            )
        image_kv = jnp.concatenate(image_kv)
    else:
        vision_rows = joined(my_vision, "vis", 0)
        scaled, power = embed(vision_rows)
        total = head_sum(
            jnp.einsum(
                "rd,kdh->rkh", scaled, qkv_weight[1:], preferred_element_type=jnp.float32
            )
        )
        power = lax.psum(power, "vis")
        image_kv = slim(total * lax.rsqrt(power / width + EPSILON)[:, None, None])

    cands = every_length.shape[0]
    most = min(MOSTC, cands)
    ends = jnp.cumsum(cand_counts)
    start = jnp.minimum(ends[group] - cand_counts[group], cands - most)
    near = lax.dynamic_slice_in_dim(every_word, start * CAP, most * CAP, axis=0)
    near = near.reshape(most * CAP, 3, share // DH, DH)
    lengths = lax.dynamic_slice_in_dim(every_length, start, most, axis=0)
    row_cand = jnp.arange(most * CAP, dtype=jnp.int32) // CAP
    owned = image_of(cand_counts, start + row_cand) == group
    live = wide(jnp.arange(most * CAP, dtype=jnp.int32) % CAP) < jnp.repeat(lengths, CAP)
    own_allowed = (row_cand[:, None] == row_cand[None, :]) & live[None, :]
    image_kv = image_kv.reshape(rows, 2, share // DH, DH)
    query = near[:, 0]

    def scores_of(keys):
        return jnp.einsum(
            "qhd,khd->hqk", query, keys, preferred_element_type=jnp.float32
        ) * DH ** (-0.5)

    def mixed(weights, values):
        return jnp.einsum(
            "hqk,khd->hqd", slim(weights), values, preferred_element_type=jnp.float32
        )

    image_scores = scores_of(image_kv[:, 0])
    own_scores = jnp.where(own_allowed[None], scores_of(near[:, 1]), FLOOR)
    top = jnp.maximum(
        jnp.max(image_scores, axis=-1, keepdims=True), jnp.max(own_scores, axis=-1, keepdims=True)
    )
    image_weights = jnp.exp(image_scores - top)
    own_weights = jnp.where(own_allowed[None], jnp.exp(own_scores - top), 0.0)
    total = jnp.sum(image_weights, axis=-1, keepdims=True) + jnp.sum(
        own_weights, axis=-1, keepdims=True
    )
    result = (mixed(image_weights, image_kv[:, 1]) + mixed(own_weights, near[:, 2])) / total
    result = jnp.where(owned[:, None, None], slim(result).transpose(1, 0, 2), 0)
    spread_out = lax.dynamic_update_slice_in_dim(
        jnp.zeros((cands * CAP, share), jnp.bfloat16),
        result.reshape(most * CAP, share),
        start * CAP,
        axis=0,
    )
    attended = lax.psum_scatter(spread_out, "grp", scatter_dimension=0, tiled=True)
    if shares > 1:
        attended = joined(attended, "vis", 1)
    partial_words = dot(attended, out_weight).reshape(cand_local, CAP, out_weight.shape[1])
    words_out = lax.psum_scatter(partial_words, "enc", scatter_dimension=1, tiled=True)
    caption_out = slim(words + words_out)
    return (vision_rows[None], caption_out)


def solution(mesh):
    return jax.shard_map(
        on_device,
        mesh=mesh,
        in_specs=(
            P("grp", None, "enc"),
            P("enc"),
            P("enc", ("vis", "grp")),
            P(("vis", "grp"), "enc"),
            P("enc", "vis"),
            P("vis"),
            P(None, "vis", "enc"),
            P("enc", "vis"),
            P("grp", "enc", "vis"),
            P(),
            P("grp"),
        ),
        out_specs=(P("grp", None, "enc"), P("grp", "enc", "vis")),
        check_vma=False,
    )
```

```python
import jax
import jax.numpy as jnp
from jax import lax
from jax.sharding import PartitionSpec as P

DH = 256
CAP = 16
MOSTC = 12


EPSILON = 1e-06
FLOOR = -1e30


def image_of(counts, candidate):
    ends = jnp.cumsum(counts)
    return jnp.sum((candidate[:, None] >= ends[None, :]).astype(jnp.int32), axis=1)


def dot(a, b):
    return jnp.dot(a, b, preferred_element_type=jnp.float32)


def wide(a):
    return a.astype(jnp.float32)


def slim(a):
    return a.astype(jnp.bfloat16)


def shifted(value, axis, step):
    count = lax.axis_size(axis)
    return lax.ppermute(value, axis, [(i, (i + step) % count) for i in range(count)])


def summed(value, axis):
    if lax.axis_size(axis) != 2:
        return lax.psum(value, axis)
    return value + shifted(value, axis, 1)


def ordered(value, first):
    return lax.optimization_barrier((value, first))[0]


def joined(value, axis, dim):
    if lax.axis_size(axis) != 2:
        return lax.all_gather(value, axis, axis=dim, tiled=True)
    other = shifted(value, axis, 1)
    first = lax.axis_index(axis) == 0
    return jnp.concatenate(
        [jnp.where(first, value, other), jnp.where(first, other, value)], axis=dim
    )


def on_device(
    image_tokens,
    vision_gain,
    up_weight,
    down_weight,
    project_weight,
    encoder_gain,
    qkv_weight,
    out_weight,
    captions,
    cand_counts,
    caption_lengths,
):
    vis_count = lax.axis_size("vis")
    enc_count = lax.axis_size("enc")
    groups = lax.axis_size("grp")
    vis = lax.axis_index("vis")
    group = lax.axis_index("grp")
    rows, features = image_tokens.shape[1:]
    all_features = features * enc_count
    width = captions.shape[2] * vis_count
    pair = vis_count == 2
    part_rows = rows // vis_count

    cores = 2 if groups % 2 == 0 else 1
    places = groups // cores
    place, core = group // cores, group % cores
    core_swap = [(i, i ^ 1) for i in range(groups)]
    up_parts, down_parts = [up_weight], [down_weight]
    if cores == 2:
        up_parts.append(lax.ppermute(up_weight, "grp", core_swap))
        down_parts.append(lax.ppermute(down_weight, "grp", core_swap))

    def to_place(value, step):
        return lax.ppermute(
            value, "grp", [(i, (i + step * cores) % groups) for i in range(groups)]
        )

    def mine_of(value):
        return lax.dynamic_slice_in_dim(value, vis * part_rows, part_rows, axis=0)

    def by_halves(value):
        if not pair:
            return value
        return jnp.concatenate(
            [mine_of(value), lax.dynamic_slice_in_dim(value, (1 - vis) * part_rows, part_rows, axis=0)]
        )

    def all_rows(mine):
        if not pair:
            return lax.all_gather(mine, "vis", axis=0, tiled=True)
        return jnp.concatenate([mine, shifted(mine, "vis", 1)])

    def my_rows_sum(value):
        if not pair:
            return lax.psum_scatter(value, "vis", scatter_dimension=0, tiled=True)
        return value[:part_rows] + wide(shifted(slim(value[part_rows:]), "vis", 1))

    my_tokens = mine_of(image_tokens[0])
    my_blocks = {}
    gate = my_tokens
    for step in range(1, places):
        my_blocks[step] = to_place(gate, step)
        if step == 1:
            gate = ordered(my_tokens, my_blocks[1])

    tokens = wide(image_tokens[0])
    row_total, row_squares = summed(
        jnp.stack([jnp.sum(tokens, axis=-1), jnp.sum(tokens * tokens, axis=-1)]), "enc"
    )
    mean = row_total / all_features
    spread = row_squares / all_features - mean * mean
    stats = jnp.stack([mean, lax.rsqrt(spread + EPSILON)])

    def normalized(block, step):
        moved = by_halves(jnp.transpose(to_place(stats, step) if step else stats))
        return slim((wide(block) - moved[:, :1]) * moved[:, 1:] * vision_gain)

    def pre_of(block):
        return jnp.concatenate([dot(block, weight) for weight in up_parts], axis=1)

    def out_of(pre):
        if enc_count == 2:
            full = pre + wide(shifted(slim(pre), "enc", 1))
        else:
            full = lax.psum(pre, "enc")
        hidden = slim(jax.nn.gelu(full, approximate=False))
        units = down_weight.shape[0]
        terms = [
            dot(hidden[:, at * units : (at + 1) * units], weight)
            for at, weight in enumerate(down_parts)
        ]
        return sum(terms[1:], terms[0])

    my_out = wide(my_tokens)
    for step in range(places):
        if step:
            block = all_rows(my_blocks[step])
            block = ordered(block, up_parts[-1])
        else:
            block = by_halves(image_tokens[0])
        partial = my_rows_sum(out_of(pre_of(normalized(block, step))))
        if step:
            partial = wide(to_place(slim(partial), -step))
        my_out = my_out + partial
    my_vision = slim(my_out)

    inner = qkv_weight.shape[2]
    heads = inner // DH
    shares = vis_count if heads % vis_count == 0 else 1
    share = inner // shares
    words = wide(captions)
    all_words = wide(joined(captions, "enc", 1))
    word_power = summed(jnp.sum(all_words * all_words, axis=-1), "vis")
    word_normed = slim(
        all_words * lax.rsqrt(word_power / width + EPSILON)[..., None] * encoder_gain
    )
    cand_local = word_normed.shape[0]
    word_rows = cand_local * CAP
    flat_words = word_normed.reshape(word_rows, word_normed.shape[2])

    def head_weights(which):
        return lax.dynamic_slice_in_dim(qkv_weight, which * share, share, axis=2)

    def head_sum(values, scale=None):
        if shares == 1:
            return lax.psum(values, "vis")
        return lax.psum_scatter(values, "vis", scatter_dimension=2, tiled=True)

    if pair and shares == 2:
        my_heads, other_heads = head_weights(vis), head_weights(1 - vis)

        def project_heads(block, first):
            sent = jnp.einsum(
                "rd,kdh->rkh", block, other_heads[first:], preferred_element_type=jnp.float32
            )
            kept = jnp.einsum(
                "rd,kdh->rkh", block, my_heads[first:], preferred_element_type=jnp.float32
            )
            return kept, slim(sent)

        kept, sent = project_heads(flat_words, 0)
        word_qkv = slim(kept + wide(shifted(sent, "vis", 1)))
    else:
        word_qkv = slim(
            head_sum(
                jnp.einsum(
                    "rd,kdh->rkh", flat_words, qkv_weight, preferred_element_type=jnp.float32
                )
            )
        )
    row_at = jnp.arange(word_rows, dtype=jnp.int32) % CAP
    word_live = row_at < jnp.repeat(caption_lengths, CAP)
    flags = jnp.broadcast_to(word_live[:, None].astype(jnp.bfloat16), (word_rows, 128))
    message = jnp.concatenate([word_qkv.reshape(word_rows, 3 * share), flags], axis=1)
    if cores == 2:
        other = lax.ppermute(message, "grp", core_swap)
        message = jnp.concatenate(
            [jnp.where(core == 0, message, other), jnp.where(core == 0, other, message)]
        )
    place_rows = cores * word_rows
    every_word = jnp.zeros((groups * word_rows, message.shape[1]), jnp.bfloat16)
    for step in range(places):
        moved = to_place(message, step) if step else message
        every_word = lax.dynamic_update_slice_in_dim(
            every_word, moved, (place - step) % places * place_rows, axis=0
        )

    def embed(block):
        partial = dot(block, project_weight)
        if enc_count == 2:
            full = partial + wide(shifted(slim(partial), "enc", 1))
        else:
            full = lax.psum(partial, "enc")
        return slim(full * encoder_gain), jnp.sum(full * full, axis=-1)

    if pair and shares == 2:
        other_vision = shifted(my_vision, "vis", 1)
        vision_rows = jnp.where(
            vis == 0,
            jnp.concatenate([my_vision, other_vision]),
            jnp.concatenate([other_vision, my_vision]),
        )
        pieces = []
        for block in (my_vision, other_vision):
            scaled, power = embed(block)
            pieces.append(project_heads(scaled, 1) + (power,))
        image_kv = []
        for here, there in ((0, 1), (1, 0)):
            total = pieces[here][0] + wide(shifted(pieces[there][1], "vis", 1))
            power = pieces[here][2] + shifted(pieces[there][2], "vis", 1)
            image_kv.append(
                slim(total * lax.rsqrt(power / width + EPSILON)[:, None, None])
            )
        image_kv = jnp.concatenate(image_kv)
    else:
        vision_rows = joined(my_vision, "vis", 0)
        scaled, power = embed(vision_rows)
        total = head_sum(
            jnp.einsum(
                "rd,kdh->rkh", scaled, qkv_weight[1:], preferred_element_type=jnp.float32
            )
        )
        power = lax.psum(power, "vis")
        image_kv = slim(total * lax.rsqrt(power / width + EPSILON)[:, None, None])

    cands = groups * cand_local
    most = min(MOSTC, cands)
    ends = jnp.cumsum(cand_counts)
    start = jnp.minimum(ends[group] - cand_counts[group], cands - most)
    near = lax.dynamic_slice_in_dim(every_word, start * CAP, most * CAP, axis=0)
    live = near[:, 3 * share] > 0
    near = near[:, : 3 * share].reshape(most * CAP, 3, share // DH, DH)
    row_cand = jnp.arange(most * CAP, dtype=jnp.int32) // CAP
    owned = image_of(cand_counts, start + row_cand) == group
    own_allowed = (row_cand[:, None] == row_cand[None, :]) & live[None, :]
    image_kv = image_kv.reshape(rows, 2, share // DH, DH)
    query = near[:, 0]

    def scores_of(keys):
        return jnp.einsum(
            "qhd,khd->hqk", query, keys, preferred_element_type=jnp.float32
        ) * DH ** (-0.5)

    def mixed(weights, values):
        return jnp.einsum(
            "hqk,khd->hqd", slim(weights), values, preferred_element_type=jnp.float32
        )

    image_scores = scores_of(image_kv[:, 0])
    own_scores = jnp.where(own_allowed[None], scores_of(near[:, 1]), FLOOR)
    top = jnp.maximum(
        jnp.max(image_scores, axis=-1, keepdims=True), jnp.max(own_scores, axis=-1, keepdims=True)
    )
    image_weights = jnp.exp(image_scores - top)
    own_weights = jnp.where(own_allowed[None], jnp.exp(own_scores - top), 0.0)
    total = jnp.sum(image_weights, axis=-1, keepdims=True) + jnp.sum(
        own_weights, axis=-1, keepdims=True
    )
    result = (mixed(image_weights, image_kv[:, 1]) + mixed(own_weights, near[:, 2])) / total
    result = jnp.where(owned[:, None, None], slim(result).transpose(1, 0, 2), 0)
    spread_out = lax.dynamic_update_slice_in_dim(
        jnp.zeros((cands * CAP, share), jnp.bfloat16),
        result.reshape(most * CAP, share),
        start * CAP,
        axis=0,
    )
    landed = None
    for step in range(places):
        part = lax.dynamic_slice_in_dim(
            spread_out, (place + step) % places * place_rows, place_rows, axis=0
        )
        part = to_place(part, step) if step else part
        landed = part if landed is None else landed + part
    if cores == 2:
        kept = lax.dynamic_slice_in_dim(landed, core * word_rows, word_rows, axis=0)
        given = lax.dynamic_slice_in_dim(landed, (1 - core) * word_rows, word_rows, axis=0)
        attended = kept + lax.ppermute(given, "grp", core_swap)
    else:
        kept, attended = landed, landed
    if pair and shares == 2:
        other = shifted(kept, "vis", 1)
        if cores == 2:
            across = [
                (v * groups + i, (1 - v) * groups + (i ^ 1)) for v in range(2) for i in range(groups)
            ]
            other = other + lax.ppermute(given, ("vis", "grp"), across)
        attended = jnp.concatenate([attended, other], axis=1)
        final_weight = jnp.concatenate(
            [
                lax.dynamic_slice_in_dim(out_weight, vis * share, share, axis=0),
                lax.dynamic_slice_in_dim(out_weight, (1 - vis) * share, share, axis=0),
            ]
        )
    else:
        if shares > 1:
            attended = lax.all_gather(attended, "vis", axis=1, tiled=True)
        final_weight = out_weight
    if enc_count == 2:
        enc = lax.axis_index("enc")
        slots = CAP // enc_count
        attended = attended.reshape(cand_local, CAP, inner)

        def branch(which):
            part = lax.dynamic_slice_in_dim(attended, which * slots, slots, axis=1)
            return dot(part.reshape(cand_local * slots, inner), final_weight)

        given = shifted(slim(branch(1 - enc)), "enc", 1)
        words_out = (branch(enc) + wide(given)).reshape(words.shape)
    else:
        partial_words = dot(attended, final_weight).reshape(cand_local, CAP, out_weight.shape[1])
        words_out = lax.psum_scatter(partial_words, "enc", scatter_dimension=1, tiled=True)
    caption_out = slim(words + words_out)
    return (vision_rows[None], caption_out)


def solution(mesh):
    return jax.shard_map(
        on_device,
        mesh=mesh,
        in_specs=(
            P("grp", None, "enc"),
            P("enc"),
            P("enc", ("vis", "grp")),
            P(("vis", "grp"), "enc"),
            P("enc", "vis"),
            P("vis"),
            P(None, "vis", "enc"),
            P("enc", "vis"),
            P("grp", "enc", "vis"),
            P(),
            P("grp"),
        ),
        out_specs=(P("grp", None, "enc"), P("grp", "enc", "vis")),
        check_vma=False,
    )
```

```python
import jax
import jax.numpy as jnp
from jax import lax
from jax.sharding import PartitionSpec as P

DH = 256
CAP = 16
MOSTC = 12


EPSILON = 1e-06
FLOOR = -1e30


def image_of(counts, candidate):
    ends = jnp.cumsum(counts)
    return jnp.sum((candidate[:, None] >= ends[None, :]).astype(jnp.int32), axis=1)


def dot(a, b):
    return jnp.dot(a, b, preferred_element_type=jnp.float32)


def wide(a):
    return a.astype(jnp.float32)


def slim(a):
    return a.astype(jnp.bfloat16)


def shifted(value, axis, step):
    count = lax.axis_size(axis)
    return lax.ppermute(value, axis, [(i, (i + step) % count) for i in range(count)])


def summed(value, axis):
    if lax.axis_size(axis) != 2:
        return lax.psum(value, axis)
    return value + shifted(value, axis, 1)


def ordered(value, first):
    return lax.optimization_barrier((value, first))[0]


def joined(value, axis, dim):
    if lax.axis_size(axis) != 2:
        return lax.all_gather(value, axis, axis=dim, tiled=True)
    other = shifted(value, axis, 1)
    first = lax.axis_index(axis) == 0
    return jnp.concatenate(
        [jnp.where(first, value, other), jnp.where(first, other, value)], axis=dim
    )


def on_device(
    image_tokens,
    vision_gain,
    up_weight,
    down_weight,
    project_weight,
    encoder_gain,
    qkv_weight,
    out_weight,
    captions,
    cand_counts,
    caption_lengths,
):
    vis_count = lax.axis_size("vis")
    enc_count = lax.axis_size("enc")
    groups = lax.axis_size("grp")
    vis = lax.axis_index("vis")
    group = lax.axis_index("grp")
    rows, features = image_tokens.shape[1:]
    all_features = features * enc_count
    width = captions.shape[2] * vis_count
    pair = vis_count == 2
    part_rows = rows // vis_count

    cores = 2 if groups % 2 == 0 else 1
    places = groups // cores
    place, core = group // cores, group % cores
    core_swap = [(i, i ^ 1) for i in range(groups)]
    up_parts, down_parts = [up_weight], [down_weight]
    if cores == 2:
        up_parts.append(lax.ppermute(up_weight, "grp", core_swap))
        down_parts.append(lax.ppermute(down_weight, "grp", core_swap))

    def to_place(value, step):
        return lax.ppermute(
            value, "grp", [(i, (i + step * cores) % groups) for i in range(groups)]
        )

    def mine_of(value):
        return lax.dynamic_slice_in_dim(value, vis * part_rows, part_rows, axis=0)

    def by_halves(value):
        if not pair:
            return value
        return jnp.concatenate(
            [mine_of(value), lax.dynamic_slice_in_dim(value, (1 - vis) * part_rows, part_rows, axis=0)]
        )

    def all_rows(mine):
        if not pair:
            return lax.all_gather(mine, "vis", axis=0, tiled=True)
        return jnp.concatenate([mine, shifted(mine, "vis", 1)])

    def my_rows_sum(value):
        if not pair:
            return lax.psum_scatter(value, "vis", scatter_dimension=0, tiled=True)
        return value[:part_rows] + wide(shifted(slim(value[part_rows:]), "vis", 1))

    last = []

    def gated(*values):
        if not last:
            return values if len(values) > 1 else values[0]
        held = lax.optimization_barrier((*values, *last))[: len(values)]
        return held if len(values) > 1 else held[0]

    def marked(*values):
        last[:] = values

    my_tokens = mine_of(image_tokens[0])
    arrived = {1: to_place(my_tokens, 1)} if places > 1 else {}
    words = wide(captions)
    word_power = summed(jnp.sum(words * words, axis=-1), "vis")
    tokens = wide(image_tokens[0])
    row_total, row_squares = summed(
        jnp.stack([jnp.sum(tokens, axis=-1), jnp.sum(tokens * tokens, axis=-1)]), "enc"
    )
    mean = row_total / all_features
    spread = row_squares / all_features - mean * mean
    stats = jnp.stack([mean, lax.rsqrt(spread + EPSILON)])
    moved_stats = [to_place(stats, step) if step else stats for step in range(places)]

    def normalized(block, step):
        moved = by_halves(jnp.transpose(moved_stats[step]))
        return slim((wide(block) - moved[:, :1]) * moved[:, 1:] * vision_gain)

    def exchanged(pre):
        if enc_count == 2:
            return pre, shifted(slim(pre), "enc", 1)
        return pre, lax.psum(pre, "enc") - pre

    def up_of(step):
        block = gated(blocks[step])
        block = normalized(block, step)
        pre = jnp.concatenate([dot(block, weight) for weight in up_parts], axis=1)
        marked(pre)
        return exchanged(pre)

    def down_of(pre, other):
        pre, other = gated(pre, other)
        hidden = slim(jax.nn.gelu(pre + wide(other), approximate=False))
        units = down_weight.shape[0]
        terms = [
            dot(hidden[:, at * units : (at + 1) * units], weight)
            for at, weight in enumerate(down_parts)
        ]
        out = sum(terms[1:], terms[0])
        marked(out)
        if pair:
            return out[:part_rows], shifted(slim(out[part_rows:]), "vis", 1)
        kept = lax.psum_scatter(out, "vis", scatter_dimension=0, tiled=True)
        return kept, jnp.zeros_like(kept, jnp.bfloat16)

    def returned(kept, other, step):
        kept, other = gated(kept, other)
        total = slim(kept + wide(other))
        marked(total)
        return to_place(total, -step)

    inner = qkv_weight.shape[2]
    heads = inner // DH
    shares = vis_count if heads % vis_count == 0 else 1
    share = inner // shares
    split_heads = pair and shares == 2
    word_normed = slim(words * lax.rsqrt(word_power / width + EPSILON)[..., None] * encoder_gain)
    all_words = joined(word_normed, "enc", 1)
    cand_local = all_words.shape[0]
    word_rows = cand_local * CAP
    flat_words = all_words.reshape(word_rows, all_words.shape[2])

    def head_weights(which):
        return lax.dynamic_slice_in_dim(qkv_weight, which * share, share, axis=2)

    def heads_of(block, weight):
        return jnp.einsum("rd,kdh->rkh", block, weight, preferred_element_type=jnp.float32)

    def head_sum(values):
        if shares == 1:
            return lax.psum(values, "vis")
        return lax.psum_scatter(values, "vis", scatter_dimension=2, tiled=True)

    own_normed = normalized(by_halves(image_tokens[0]), 0)
    own_pre = [dot(own_normed, up_parts[0])]
    marked(own_pre[0])

    blocks = {}

    def forwarded(step):
        here, tokens_next = gated(arrived[step], my_tokens)
        marked(here)
        if step + 1 < places:
            arrived[step + 1] = to_place(ordered(tokens_next, here), step + 1)
        blocks[step] = all_rows(here)

    if places > 1:
        forwarded(1)
    flat_words = gated(flat_words)
    if split_heads:
        my_heads, other_heads = head_weights(vis), head_weights(1 - vis)
        sent = slim(heads_of(flat_words, other_heads))
        word_other = shifted(sent, "vis", 1)
        word_kept = heads_of(flat_words, my_heads)
        marked(sent, word_kept)
    else:
        word_kept = head_sum(heads_of(flat_words, qkv_weight))
        marked(word_kept)
    if cores == 2:
        own_normed = gated(own_normed)
        own_pre.append(dot(own_normed, up_parts[1]))
        marked(own_pre[1])
    own_pre = exchanged(jnp.concatenate(own_pre, axis=1))

    pres, outs, backs = {}, {}, {}

    def up(step):
        if 0 < step < places:
            pres[step] = up_of(step)

    def down(step):
        if 0 < step < places:
            outs[step] = down_of(*pres[step])

    def back(step):
        if 0 < step < places:
            backs[step] = returned(*outs[step], step)

    up(1)
    if split_heads:
        word_kept, word_other = gated(word_kept, word_other)
        word_kept = word_kept + wide(word_other)
    row_at = jnp.arange(word_rows, dtype=jnp.int32) % CAP
    word_live = row_at < jnp.repeat(caption_lengths, CAP)
    flags = jnp.broadcast_to(word_live[:, None].astype(jnp.bfloat16), (word_rows, 128))
    message = jnp.concatenate([slim(word_kept).reshape(word_rows, 3 * share), flags], axis=1)
    marked(message)
    if split_heads:
        final_weight = jnp.concatenate(
            [
                lax.dynamic_slice_in_dim(gated(out_weight), vis * share, share, axis=0),
                lax.dynamic_slice_in_dim(out_weight, (1 - vis) * share, share, axis=0),
            ]
        )
        marked(final_weight)
    else:
        final_weight = out_weight
    for step in range(2, places):
        forwarded(step)
    message = ordered(message, last[0])
    messages = [to_place(message, step) if step else message for step in range(places)]
    up(2)
    down(1)
    up(3)
    down(2)
    back(1)
    for step in range(4, places):
        up(step)
        down(step - 1)
    down(places - 1)
    outs[0] = down_of(*own_pre)
    for step in range(2, places - 1):
        back(step)

    word_block = jnp.concatenate([m[None] for m in gated(*messages)])
    marked(word_block)
    if cores == 2:
        other = lax.ppermute(word_block, "grp", core_swap)
        word_block = jnp.stack(
            [jnp.where(core == 0, word_block, other), jnp.where(core == 0, other, word_block)],
            axis=1,
        )
    place_rows = cores * word_rows
    word_block = word_block.reshape(places, place_rows, message.shape[1])
    every_word = jnp.zeros((groups * word_rows, message.shape[1]), jnp.bfloat16)
    for step in range(places):
        every_word = lax.dynamic_update_slice_in_dim(
            every_word, word_block[step], (place - step) % places * place_rows, axis=0
        )

    cands = groups * cand_local
    most = min(MOSTC, cands)
    ends = jnp.cumsum(cand_counts)
    start = jnp.minimum(ends[group] - cand_counts[group], cands - most)
    near = lax.dynamic_slice_in_dim(every_word, start * CAP, most * CAP, axis=0)
    if places > 2:
        back(places - 1)
    near, kept, other = gated(near, *outs[0])
    my_out = wide(my_tokens) + (kept + wide(other))
    for step in backs:
        my_out = my_out + wide(backs[step])
    my_vision = slim(my_out)

    def embed(block):
        partial = dot(block, project_weight)
        if enc_count == 2:
            full = partial + wide(shifted(slim(partial), "enc", 1))
        else:
            full = lax.psum(partial, "enc")
        return slim(full * encoder_gain), jnp.sum(full * full, axis=-1)

    if split_heads:
        other_vision = shifted(my_vision, "vis", 1)
        vision_rows = jnp.where(
            vis == 0,
            jnp.concatenate([my_vision, other_vision]),
            jnp.concatenate([other_vision, my_vision]),
        )
        pieces = []
        for block in (my_vision, other_vision):
            scaled, power = embed(block)
            pieces.append(
                (heads_of(scaled, my_heads[1:]), slim(heads_of(scaled, other_heads[1:])), power)
            )
        image_kv = []
        for here, there in ((0, 1), (1, 0)):
            total = pieces[here][0] + wide(shifted(pieces[there][1], "vis", 1))
            power = pieces[here][2] + shifted(pieces[there][2], "vis", 1)
            image_kv.append(
                slim(total * lax.rsqrt(power / width + EPSILON)[:, None, None])
            )
        image_kv = jnp.concatenate(image_kv)
    else:
        vision_rows = joined(my_vision, "vis", 0)
        scaled, power = embed(vision_rows)
        total = head_sum(heads_of(scaled, qkv_weight[1:]))
        power = lax.psum(power, "vis")
        image_kv = slim(total * lax.rsqrt(power / width + EPSILON)[:, None, None])

    live = near[:, 3 * share] > 0
    near = near[:, : 3 * share].reshape(most * CAP, 3, share // DH, DH)
    row_cand = jnp.arange(most * CAP, dtype=jnp.int32) // CAP
    owned = image_of(cand_counts, start + row_cand) == group
    own_allowed = (row_cand[:, None] == row_cand[None, :]) & live[None, :]
    image_kv = image_kv.reshape(rows, 2, share // DH, DH)
    query = near[:, 0]

    def scores_of(keys):
        return jnp.einsum(
            "qhd,khd->hqk", query, keys, preferred_element_type=jnp.float32
        ) * DH ** (-0.5)

    def mixed(weights, values):
        return jnp.einsum(
            "hqk,khd->hqd", slim(weights), values, preferred_element_type=jnp.float32
        )

    image_scores = scores_of(image_kv[:, 0])
    own_scores = jnp.where(own_allowed[None], scores_of(near[:, 1]), FLOOR)
    top = jnp.maximum(
        jnp.max(image_scores, axis=-1, keepdims=True), jnp.max(own_scores, axis=-1, keepdims=True)
    )
    image_weights = jnp.exp(image_scores - top)
    own_weights = jnp.where(own_allowed[None], jnp.exp(own_scores - top), 0.0)
    total = jnp.sum(image_weights, axis=-1, keepdims=True) + jnp.sum(
        own_weights, axis=-1, keepdims=True
    )
    result = (mixed(image_weights, image_kv[:, 1]) + mixed(own_weights, near[:, 2])) / total
    result = jnp.where(owned[:, None, None], slim(result).transpose(1, 0, 2), 0)
    spread_out = lax.dynamic_update_slice_in_dim(
        jnp.zeros((cands * CAP, share), jnp.bfloat16),
        result.reshape(most * CAP, share),
        start * CAP,
        axis=0,
    )
    landed = None
    for step in range(places):
        part = lax.dynamic_slice_in_dim(
            spread_out, (place + step) % places * place_rows, place_rows, axis=0
        )
        part = to_place(part, step) if step else part
        landed = part if landed is None else landed + part
    if cores == 2:
        kept = lax.dynamic_slice_in_dim(landed, core * word_rows, word_rows, axis=0)
        given = lax.dynamic_slice_in_dim(landed, (1 - core) * word_rows, word_rows, axis=0)
        attended = kept + lax.ppermute(given, "grp", core_swap)
    else:
        kept, attended = landed, landed
    if split_heads:
        other = shifted(kept, "vis", 1)
        if cores == 2:
            across = [
                (v * groups + i, (1 - v) * groups + (i ^ 1)) for v in range(2) for i in range(groups)
            ]
            other = other + lax.ppermute(given, ("vis", "grp"), across)
        attended = jnp.concatenate([attended, other], axis=1)
    else:
        if shares > 1:
            attended = lax.all_gather(attended, "vis", axis=1, tiled=True)
    if enc_count == 2:
        enc = lax.axis_index("enc")
        slots = CAP // enc_count
        attended = attended.reshape(cand_local, CAP, inner)

        def branch(which):
            part = lax.dynamic_slice_in_dim(attended, which * slots, slots, axis=1)
            return dot(part.reshape(cand_local * slots, inner), final_weight)

        given = shifted(slim(branch(1 - enc)), "enc", 1)
        words_out = (branch(enc) + wide(given)).reshape(words.shape)
    else:
        partial_words = dot(attended, final_weight).reshape(cand_local, CAP, out_weight.shape[1])
        words_out = lax.psum_scatter(partial_words, "enc", scatter_dimension=1, tiled=True)
    caption_out = slim(words + words_out)
    return (vision_rows[None], caption_out)


def solution(mesh):
    return jax.shard_map(
        on_device,
        mesh=mesh,
        in_specs=(
            P("grp", None, "enc"),
            P("enc"),
            P("enc", ("vis", "grp")),
            P(("vis", "grp"), "enc"),
            P("enc", "vis"),
            P("vis"),
            P(None, "vis", "enc"),
            P("enc", "vis"),
            P("grp", "enc", "vis"),
            P(),
            P("grp"),
        ),
        out_specs=(P("grp", None, "enc"), P("grp", "enc", "vis")),
        check_vma=False,
    )
```

```python
import jax
import jax.numpy as jnp
from jax import lax
from jax.sharding import PartitionSpec as P

DH = 256
CAP = 16
MOSTC = 12


EPSILON = 1e-06
FLOOR = -1e30


def image_of(counts, candidate):
    ends = jnp.cumsum(counts)
    return jnp.sum((candidate[:, None] >= ends[None, :]).astype(jnp.int32), axis=1)


def dot(a, b):
    return jnp.dot(a, b, preferred_element_type=jnp.float32)


def wide(a):
    return a.astype(jnp.float32)


def slim(a):
    return a.astype(jnp.bfloat16)


def shifted(value, axis, step):
    count = lax.axis_size(axis)
    return lax.ppermute(value, axis, [(i, (i + step) % count) for i in range(count)])


def summed(value, axis):
    if lax.axis_size(axis) != 2:
        return lax.psum(value, axis)
    return value + shifted(value, axis, 1)


def joined(value, axis, dim):
    if lax.axis_size(axis) != 2:
        return lax.all_gather(value, axis, axis=dim, tiled=True)
    other = shifted(value, axis, 1)
    first = lax.axis_index(axis) == 0
    return jnp.concatenate(
        [jnp.where(first, value, other), jnp.where(first, other, value)], axis=dim
    )


def on_device(
    image_tokens,
    vision_gain,
    up_weight,
    down_weight,
    project_weight,
    encoder_gain,
    qkv_weight,
    out_weight,
    captions,
    cand_counts,
    caption_lengths,
):
    vis_count = lax.axis_size("vis")
    enc_count = lax.axis_size("enc")
    groups = lax.axis_size("grp")
    vis = lax.axis_index("vis")
    group = lax.axis_index("grp")
    rows, features = image_tokens.shape[1:]
    all_features = features * enc_count
    width = captions.shape[2] * vis_count
    pair = vis_count == 2
    part_rows = rows // vis_count

    cores = 2 if groups % 2 == 0 else 1
    places = groups // cores
    place, core = group // cores, group % cores
    core_swap = [(i, i ^ 1) for i in range(groups)]
    if cores == 2:
        pairs = [[i, i + 1] for i in range(0, groups, 2)]
        up_weight = lax.all_gather(
            up_weight, "grp", axis=1, tiled=True, axis_index_groups=pairs
        )
        down_weight = lax.all_gather(
            down_weight, "grp", axis=0, tiled=True, axis_index_groups=pairs
        )

    def to_place(value, step):
        return lax.ppermute(
            value, "grp", [(i, (i + step * cores) % groups) for i in range(groups)]
        )

    def mine_of(value):
        return lax.dynamic_slice_in_dim(value, vis * part_rows, part_rows, axis=0)

    def by_halves(value):
        if not pair:
            return value
        return jnp.concatenate(
            [mine_of(value), lax.dynamic_slice_in_dim(value, (1 - vis) * part_rows, part_rows, axis=0)]
        )

    def all_rows(mine):
        if not pair:
            return lax.all_gather(mine, "vis", axis=0, tiled=True)
        return jnp.concatenate([mine, shifted(mine, "vis", 1)])

    def my_rows_sum(value):
        if not pair:
            return lax.psum_scatter(value, "vis", scatter_dimension=0, tiled=True)
        return value[:part_rows] + wide(shifted(slim(value[part_rows:]), "vis", 1))

    last = []

    def gated(value):
        return value + last[0].astype(value.dtype) if last else value

    def marked(*values):
        corners = [lax.slice(v, (0,) * v.ndim, (1,) * v.ndim).reshape(()) for v in values]
        last[:] = [sum([wide(corner) for corner in corners]) * 0.0]

    my_tokens = mine_of(image_tokens[0])
    arrived = {1: to_place(my_tokens, 1)} if places > 1 else {}
    words = wide(captions)
    word_power = summed(jnp.sum(words * words, axis=-1), "vis")
    marked(my_tokens)
    tokens = gated(wide(image_tokens[0]))
    row_total, row_squares = summed(
        jnp.stack([jnp.sum(tokens, axis=-1), jnp.sum(tokens * tokens, axis=-1)]), "enc"
    )
    mean = row_total / all_features
    spread = row_squares / all_features - mean * mean
    stats = jnp.stack([mean, lax.rsqrt(spread + EPSILON)], axis=1)
    stats = stats.T
    moved_stats = [to_place(stats, step) if step else stats for step in range(places)]

    def normalized(block, step):
        moved = by_halves(gated(moved_stats[step]).T)
        return slim((wide(block) - moved[:, :1]) * moved[:, 1:] * vision_gain)

    def exchanged(pre):
        if enc_count == 2:
            return pre, shifted(slim(pre), "enc", 1)
        return pre, lax.psum(pre, "enc") - pre

    def up_of(block, step):
        pre = dot(normalized(block, step), up_weight)
        marked(pre)
        return exchanged(pre)

    def down_of(pre, other):
        full = gated(pre) + wide(other)
        out = dot(slim(jax.nn.gelu(full, approximate=False)), down_weight)
        marked(out)
        if pair:
            return out[:part_rows], shifted(slim(out[part_rows:]), "vis", 1)
        kept = lax.psum_scatter(out, "vis", scatter_dimension=0, tiled=True)
        return kept, jnp.zeros_like(kept, jnp.bfloat16)

    inner = qkv_weight.shape[2]
    heads = inner // DH
    shares = vis_count if heads % vis_count == 0 else 1
    share = inner // shares
    split_heads = pair and shares == 2
    word_normed = slim(words * lax.rsqrt(word_power / width + EPSILON)[..., None] * encoder_gain)
    all_words = joined(word_normed, "enc", 1)
    cand_local = all_words.shape[0]
    word_rows = cand_local * CAP
    flat_words = all_words.reshape(word_rows, all_words.shape[2])

    def head_weights(which):
        return lax.dynamic_slice_in_dim(qkv_weight, which * share, share, axis=2)

    def heads_of(block, weight):
        return jnp.einsum("rd,kdh->rkh", block, weight, preferred_element_type=jnp.float32)

    def head_sum(values):
        if shares == 1:
            return lax.psum(values, "vis")
        return lax.psum_scatter(values, "vis", scatter_dimension=2, tiled=True)

    blocks, pres, outs, backs = {}, {}, {}, {}

    def forwarded(step):
        if step < places:
            here = gated(arrived[step]) if step > 1 else arrived[step]
            marked(here)
            if step + 1 < places:
                arrived[step + 1] = to_place(here, 1)
            blocks[step] = all_rows(here)

    def up(step):
        if step < places:
            pres[step] = up_of(blocks[step], step)

    def down(step):
        if step < places:
            outs[step] = down_of(*pres[step])

    def back(step):
        if 0 < step < places:
            total = gated(outs[step][0]) + wide(outs[step][1])
            if step > 1:
                total = total + wide(backs[step - 1])
            total = slim(total)
            marked(total)
            backs[step] = to_place(total, 1)

    blocks[0] = by_halves(image_tokens[0])
    forwarded(1)
    marked(flat_words, *moved_stats[1:], *[arrived[step] for step in (1,) if places > 1])
    up(0)
    forwarded(2)
    up(1)
    forwarded(3)
    flat_words = gated(flat_words)
    if split_heads:
        my_heads, other_heads = head_weights(vis), head_weights(1 - vis)
        sent = slim(heads_of(flat_words, other_heads))
        word_other = shifted(sent, "vis", 1)
        word_kept = heads_of(flat_words, my_heads)
        marked(sent)
    else:
        word_kept = head_sum(heads_of(flat_words, qkv_weight))
    up(2)
    down(1)
    if split_heads:
        word_kept = gated(word_kept) + wide(word_other)
    row_at = jnp.arange(word_rows, dtype=jnp.int32) % CAP
    word_live = row_at < jnp.repeat(caption_lengths, CAP)
    flags = jnp.broadcast_to(word_live[:, None].astype(jnp.bfloat16), (word_rows, 128))
    message = jnp.concatenate([slim(word_kept).reshape(word_rows, 3 * share), flags], axis=1)
    marked(message)
    every_word = lax.all_gather(message, "grp", axis=0, tiled=True)
    if split_heads:
        final_weight = jnp.concatenate(
            [
                lax.dynamic_slice_in_dim(out_weight, vis * share, share, axis=0),
                lax.dynamic_slice_in_dim(out_weight, (1 - vis) * share, share, axis=0),
            ]
        )
        final_weight = gated(final_weight)
        marked(final_weight)
    else:
        final_weight = out_weight
    up(3)
    down(2)
    back(1)
    for step in range(4, places):
        forwarded(step)
        up(step)
        down(step - 1)
    down(places - 1)
    down(0)
    marked(outs[0][0], every_word)
    for step in range(2, places):
        back(step)
    place_rows = cores * word_rows

    cands = groups * cand_local
    most = min(MOSTC, cands)
    ends = jnp.cumsum(cand_counts)
    start = jnp.minimum(ends[group] - cand_counts[group], cands - most)
    near = lax.dynamic_slice_in_dim(every_word, start * CAP, most * CAP, axis=0)
    my_out = wide(my_tokens) + (outs[0][0] + wide(outs[0][1]))
    if places > 1:
        my_out = my_out + wide(backs[places - 1])
    my_vision = slim(my_out)

    def embed(block):
        partial = dot(block, project_weight)
        if enc_count == 2:
            full = partial + wide(shifted(slim(partial), "enc", 1))
        else:
            full = lax.psum(partial, "enc")
        return slim(full * encoder_gain), jnp.sum(full * full, axis=-1)

    if split_heads:
        other_vision = shifted(my_vision, "vis", 1)
        vision_rows = jnp.where(
            vis == 0,
            jnp.concatenate([my_vision, other_vision]),
            jnp.concatenate([other_vision, my_vision]),
        )
        pieces = []
        for block in (my_vision, other_vision):
            scaled, power = embed(block)
            pieces.append(
                (heads_of(scaled, my_heads[1:]), slim(heads_of(scaled, other_heads[1:])), power)
            )
        image_kv = []
        for here, there in ((0, 1), (1, 0)):
            total = pieces[here][0] + wide(shifted(pieces[there][1], "vis", 1))
            power = pieces[here][2] + shifted(pieces[there][2], "vis", 1)
            image_kv.append(
                slim(total * lax.rsqrt(power / width + EPSILON)[:, None, None])
            )
        image_kv = jnp.concatenate(image_kv)
    else:
        vision_rows = joined(my_vision, "vis", 0)
        scaled, power = embed(vision_rows)
        total = head_sum(heads_of(scaled, qkv_weight[1:]))
        power = lax.psum(power, "vis")
        image_kv = slim(total * lax.rsqrt(power / width + EPSILON)[:, None, None])

    live = near[:, 3 * share] > 0
    near = near[:, : 3 * share].reshape(most * CAP, 3, share // DH, DH)
    row_cand = jnp.arange(most * CAP, dtype=jnp.int32) // CAP
    owned = image_of(cand_counts, start + row_cand) == group
    own_allowed = (row_cand[:, None] == row_cand[None, :]) & live[None, :]
    image_kv = image_kv.reshape(rows, 2, share // DH, DH)
    query = near[:, 0]

    def scores_of(keys):
        return jnp.einsum(
            "qhd,khd->hqk", query, keys, preferred_element_type=jnp.float32
        ) * DH ** (-0.5)

    def mixed(weights, values):
        return jnp.einsum(
            "hqk,khd->hqd", slim(weights), values, preferred_element_type=jnp.float32
        )

    image_scores = scores_of(image_kv[:, 0])
    own_scores = jnp.where(own_allowed[None], scores_of(near[:, 1]), FLOOR)
    top = jnp.maximum(
        jnp.max(image_scores, axis=-1, keepdims=True), jnp.max(own_scores, axis=-1, keepdims=True)
    )
    image_weights = jnp.exp(image_scores - top)
    own_weights = jnp.where(own_allowed[None], jnp.exp(own_scores - top), 0.0)
    total = jnp.sum(image_weights, axis=-1, keepdims=True) + jnp.sum(
        own_weights, axis=-1, keepdims=True
    )
    result = (mixed(image_weights, image_kv[:, 1]) + mixed(own_weights, near[:, 2])) / total
    result = jnp.where(owned[:, None, None], slim(result).transpose(1, 0, 2), 0)
    spread_out = lax.dynamic_update_slice_in_dim(
        jnp.zeros((cands * CAP, share), jnp.bfloat16),
        result.reshape(most * CAP, share),
        start * CAP,
        axis=0,
    )
    landed = None
    for step in range(places):
        part = lax.dynamic_slice_in_dim(
            spread_out, (place + step) % places * place_rows, place_rows, axis=0
        )
        part = to_place(part, step) if step else part
        landed = part if landed is None else landed + part
    if cores == 2:
        kept = lax.dynamic_slice_in_dim(landed, core * word_rows, word_rows, axis=0)
        given = lax.dynamic_slice_in_dim(landed, (1 - core) * word_rows, word_rows, axis=0)
        attended = kept + lax.ppermute(given, "grp", core_swap)
    else:
        kept, attended = landed, landed
    if split_heads:
        other = shifted(kept, "vis", 1)
        if cores == 2:
            across = [
                (v * groups + i, (1 - v) * groups + (i ^ 1)) for v in range(2) for i in range(groups)
            ]
            other = other + lax.ppermute(given, ("vis", "grp"), across)
        attended = jnp.concatenate([attended, other], axis=1)
    else:
        if shares > 1:
            attended = lax.all_gather(attended, "vis", axis=1, tiled=True)
    if enc_count == 2:
        enc = lax.axis_index("enc")
        slots = CAP // enc_count
        attended = attended.reshape(cand_local, CAP, inner)

        def branch(which):
            part = lax.dynamic_slice_in_dim(attended, which * slots, slots, axis=1)
            return dot(part.reshape(cand_local * slots, inner), final_weight)

        given = shifted(slim(branch(1 - enc)), "enc", 1)
        words_out = (branch(enc) + wide(given)).reshape(words.shape)
    else:
        partial_words = dot(attended, final_weight).reshape(cand_local, CAP, out_weight.shape[1])
        words_out = lax.psum_scatter(partial_words, "enc", scatter_dimension=1, tiled=True)
    caption_out = slim(words + words_out)
    return (vision_rows[None], caption_out)


def solution(mesh):
    return jax.shard_map(
        on_device,
        mesh=mesh,
        in_specs=(
            P("grp", None, "enc"),
            P("enc"),
            P("enc", ("vis", "grp")),
            P(("vis", "grp"), "enc"),
            P("enc", "vis"),
            P("vis"),
            P(None, "vis", "enc"),
            P("enc", "vis"),
            P("grp", "enc", "vis"),
            P(),
            P("grp"),
        ),
        out_specs=(P("grp", None, "enc"), P("grp", "enc", "vis")),
        check_vma=False,
    )
```

```python
import functools

import jax
import jax.numpy as jnp
from jax import lax
from jax.experimental import pallas as pl
from jax.experimental.pallas import tpu as pltpu
from jax.sharding import PartitionSpec as P

DH = 256
CAP = 16
MOSTC = 12


EPSILON = 1e-06
FLOOR = -1e30


def dot(a, b):
    return jnp.dot(a, b, preferred_element_type=jnp.float32)


def wide(a):
    return a.astype(jnp.float32)


def slim(a):
    return a.astype(jnp.bfloat16)


def shifted(value, axis, step):
    count = lax.axis_size(axis)
    return lax.ppermute(value, axis, [(i, (i + step) % count) for i in range(count)])


def summed(value, axis):
    if lax.axis_size(axis) != 2:
        return lax.psum(value, axis)
    return value + shifted(value, axis, 1)


def joined(value, axis, dim):
    if lax.axis_size(axis) != 2:
        return lax.all_gather(value, axis, axis=dim, tiled=True)
    other = shifted(value, axis, 1)
    first = lax.axis_index(axis) == 0
    return jnp.concatenate(
        [jnp.where(first, value, other), jnp.where(first, other, value)], axis=dim
    )


TOKEN = (8, 128)
HBM = pl.BlockSpec(memory_space=pl.ANY)
LIGHT = pl.CostEstimate(flops=1024, bytes_accessed=1024, transcendentals=0)
PARAMS = pltpu.CompilerParams(vmem_limit_bytes=48 * 1024 * 1024)


def tile_of(size, most):
    return most if size % most == 0 else size


def up_kernel(cores, steps, mine_ref, theirs_ref, *refs):
    weights, (out_ref, token_ref, rows_ref) = refs[:cores], refs[-3:]
    at = pl.program_id(0)
    half = mine_ref.shape[0]

    @pl.when(at == 0)
    def _():
        rows_ref[:half] = mine_ref[...]
        rows_ref[half:] = theirs_ref[...]
        token_ref[...] = jnp.zeros(TOKEN, jnp.float32)

    for core in range(cores):

        @pl.when((at >= core * steps) & (at < (core + 1) * steps))
        def _(core=core):
            out_ref[...] = slim(dot(rows_ref[...], weights[core][...]))


def up_call(halves, weights, after):
    cores = len(weights)
    depth, units = weights[0].shape
    tile = tile_of(units, 256)
    steps = units // tile
    rows = 2 * halves[0].shape[0]
    whole = pl.BlockSpec(halves[0].shape, lambda i: (0, 0))

    def weight_spec(core):
        return pl.BlockSpec((depth, tile), lambda i: (0, jnp.clip(i - core * steps, 0, steps - 1)))

    return pl.pallas_call(
        functools.partial(up_kernel, cores, steps),
        grid=(cores * steps,),
        in_specs=[whole, whole] + [weight_spec(core) for core in range(cores)] + [HBM] * len(after),
        out_specs=[
            pl.BlockSpec((rows, tile), lambda i: (0, i)),
            pl.BlockSpec(TOKEN, lambda i: (0, 0)),
        ],
        out_shape=[
            jax.ShapeDtypeStruct((rows, cores * units), jnp.bfloat16),
            jax.ShapeDtypeStruct(TOKEN, jnp.float32),
        ],
        scratch_shapes=[pltpu.VMEM((rows, depth), jnp.bfloat16)],
        compiler_params=PARAMS,
        cost_estimate=LIGHT,
    )(*halves, *weights, *after)


def down_kernel(cores, steps, own_ref, other_ref, *refs):
    weights = refs[:cores]
    kept_ref, sent_ref, token_ref, rest_ref = refs[-4 - cores : -cores]
    hidden = refs[-cores:]
    at = pl.program_id(0)
    tile, columns = weights[0].shape
    half = kept_ref.shape[0]
    wide_tile = tile_of(columns, 512)

    def fill(core, step):
        first = core * steps + step if steps > 1 else core
        columns_at = pl.ds(pl.multiple_of(first * tile, tile) if steps > 1 else first * tile, tile)
        total = wide(own_ref[:, columns_at]) + wide(other_ref[:, columns_at])
        hidden[core][...] = slim(0.5 * total * (1.0 + lax.erf(total * 0.5**0.5)))

    @pl.when(at == 0)
    def _():
        fill(0, 0)
        kept_ref[...] = jnp.zeros_like(kept_ref)
        rest_ref[...] = jnp.zeros_like(rest_ref)
        token_ref[...] = jnp.zeros(TOKEN, jnp.float32)

    for core in range(cores):
        for start in range(0, columns, wide_tile):
            part = pl.ds(start, wide_tile)
            term = dot(hidden[core][...], weights[core][:, part])
            kept_ref[:, part] += term[:half]
            rest_ref[:, part] += term[half:]
        if core + 1 < cores:
            fill(core + 1, at)
        else:
            fill(0, jnp.minimum(at + 1, steps - 1))

    @pl.when(at == steps - 1)
    def _():
        sent_ref[...] = slim(rest_ref[...])


def down_call(own, other, weights, after):
    cores = len(weights)
    units, columns = weights[0].shape
    tile = tile_of(units, 256)
    steps = units // tile
    rows = own.shape[0]
    whole = pl.BlockSpec(own.shape, lambda i: (0, 0))
    half_spec = pl.BlockSpec((rows // 2, columns), lambda i: (0, 0))
    return pl.pallas_call(
        functools.partial(down_kernel, cores, steps),
        grid=(steps,),
        in_specs=[whole, whole]
        + [pl.BlockSpec((tile, columns), lambda i: (i, 0))] * cores
        + [HBM] * len(after),
        out_specs=[half_spec, half_spec, pl.BlockSpec(TOKEN, lambda i: (0, 0))],
        out_shape=[
            jax.ShapeDtypeStruct((rows // 2, columns), jnp.float32),
            jax.ShapeDtypeStruct((rows // 2, columns), jnp.bfloat16),
            jax.ShapeDtypeStruct(TOKEN, jnp.float32),
        ],
        scratch_shapes=[pltpu.VMEM((rows // 2, columns), jnp.float32)]
        + [pltpu.VMEM((rows, tile), jnp.bfloat16) for _ in range(cores)],
        compiler_params=PARAMS,
        cost_estimate=LIGHT,
    )(own, other, *weights, *after)


def on_device(
    image_tokens,
    vision_gain,
    up_weight,
    down_weight,
    project_weight,
    encoder_gain,
    qkv_weight,
    out_weight,
    captions,
    cand_counts,
    caption_lengths,
):
    vis_count = lax.axis_size("vis")
    enc_count = lax.axis_size("enc")
    groups = lax.axis_size("grp")
    vis = lax.axis_index("vis")
    group = lax.axis_index("grp")
    rows, features = image_tokens.shape[1:]
    all_features = features * enc_count
    width = captions.shape[2] * vis_count
    pair = vis_count == 2
    part_rows = rows // vis_count

    cores = 2 if groups % 2 == 0 else 1
    places = groups // cores
    place, core = group // cores, group % cores
    core_swap = [(i, i ^ 1) for i in range(groups)]
    up_weights, down_weights = [up_weight], [down_weight]
    if cores == 2:
        up_weights.append(lax.ppermute(up_weight, "grp", core_swap))
        down_weights.append(lax.ppermute(down_weight, "grp", core_swap))
        if up_weight.shape[1] % 128:
            up_weights = [jnp.concatenate(up_weights, axis=1)]
            down_weights = [jnp.concatenate(down_weights)]

    def to_place(value, step):
        return lax.ppermute(
            value, "grp", [(i, (i + step * cores) % groups) for i in range(groups)]
        )

    def mine_of(value):
        return lax.dynamic_slice_in_dim(value, vis * part_rows, part_rows, axis=0)

    def halves_of(mine, value):
        if pair and value is None:
            return [mine, shifted(mine, "vis", 1)]
        if pair:
            return [mine, lax.dynamic_slice_in_dim(value, (1 - vis) * part_rows, part_rows, axis=0)]
        if value is None:
            value = lax.all_gather(mine, "vis", axis=0, tiled=True)
        return [value[: rows // 2], value[rows // 2 :]]

    token = []

    def gated(value):
        return value + token[0][0, 0].astype(value.dtype) if token else value

    words = wide(captions)
    word_power = summed(jnp.sum(words * words, axis=-1), "vis")
    tokens = wide(image_tokens[0])
    row_total, row_squares = summed(
        jnp.stack([jnp.sum(tokens, axis=-1), jnp.sum(tokens * tokens, axis=-1)]), "enc"
    )
    mean = row_total / all_features
    spread = row_squares / all_features - mean * mean
    normed = slim(
        (tokens - mean[:, None]) * lax.rsqrt(spread + EPSILON)[:, None] * vision_gain
    )
    my_tokens = mine_of(image_tokens[0])
    my_normed = mine_of(normed)

    inner = qkv_weight.shape[2]
    heads = inner // DH
    shares = vis_count if heads % vis_count == 0 else 1
    share = inner // shares
    split_heads = pair and shares == 2
    word_normed = slim(words * lax.rsqrt(word_power / width + EPSILON)[..., None] * encoder_gain)
    all_words = joined(word_normed, "enc", 1)
    cand_local = all_words.shape[0]
    word_rows = cand_local * CAP
    flat_words = all_words.reshape(word_rows, all_words.shape[2])

    def head_weights(which):
        return lax.dynamic_slice_in_dim(qkv_weight, which * share, share, axis=2)

    def heads_of(block, weight):
        return jnp.einsum("rd,kdh->rkh", block, weight, preferred_element_type=jnp.float32)

    def head_sum(values):
        if shares == 1:
            return lax.psum(values, "vis")
        return lax.psum_scatter(values, "vis", scatter_dimension=2, tiled=True)

    arrived, blocks, pres, outs, backs = {}, {}, {}, {}, {}

    def forwarded(step):
        if step < places:
            here = arrived[step] if step == 1 else gated(arrived[step])
            if step + 1 < places:
                arrived[step + 1] = to_place(here, 1)
            blocks[step] = halves_of(here, None)

    def up(step, *after):
        if step < places:
            pre, token[:] = (lambda got: (got[0], [got[1]]))(
                up_call(blocks[step], up_weights, [*token, *after])
            )
            if enc_count == 2:
                pres[step] = pre, shifted(pre, "enc", 1)
            else:
                pres[step] = pre, slim(lax.psum(wide(pre), "enc") - wide(pre))

    def down(step, *after):
        if step < places:
            kept, sent, next_token = down_call(*pres[step], down_weights, [*token, *after])
            token[:] = [next_token]
            if pair:
                outs[step] = kept, shifted(sent, "vis", 1)
            else:
                out = jnp.concatenate([kept, wide(sent)])
                kept = lax.psum_scatter(out, "vis", scatter_dimension=0, tiled=True)
                outs[step] = kept, jnp.zeros_like(kept, jnp.bfloat16)

    def back(step):
        if 0 < step < places:
            total = gated(outs[step][0]) + wide(outs[step][1])
            if step > 1:
                total = total + wide(backs[step - 1])
            backs[step] = to_place(slim(total), 1)

    if places > 1:
        arrived[1] = to_place(my_normed, 1)
    forwarded(1)
    row_at = jnp.arange(word_rows, dtype=jnp.int32) % CAP
    word_live = row_at < jnp.repeat(caption_lengths, CAP)
    flags = jnp.broadcast_to(word_live[:, None].astype(jnp.bfloat16), (word_rows, 128))
    blocks[0] = halves_of(my_normed, normed)
    up(0)
    flat_words = gated(flat_words)
    if split_heads:
        my_heads, other_heads = head_weights(vis), head_weights(1 - vis)
        sent = slim(heads_of(flat_words, other_heads))
        word_kept = heads_of(flat_words, my_heads) + wide(shifted(sent, "vis", 1))
    else:
        word_kept = head_sum(heads_of(flat_words, qkv_weight))
    forwarded(2)
    up(1, down_weights[-1], word_kept)
    message = jnp.concatenate([slim(word_kept).reshape(word_rows, 3 * share), flags], axis=1)
    messages = [gated(message)]
    for _ in range(1, places):
        messages.append(to_place(messages[-1], 1))
    final_weight = out_weight
    if split_heads:
        final_weight = gated(
            jnp.concatenate(
                [
                    lax.dynamic_slice_in_dim(out_weight, vis * share, share, axis=0),
                    lax.dynamic_slice_in_dim(out_weight, (1 - vis) * share, share, axis=0),
                ]
            )
        )
    forwarded(3)
    up(2, pres[0][1])
    down(1, messages[min(1, places - 1)])
    up(3, messages[min(2, places - 1)], final_weight)
    down(2, messages[min(3, places - 1)])
    back(1)
    for step in range(4, places):
        forwarded(step)
        up(step)
        down(step - 1)
    word_block = jnp.concatenate(messages)
    if cores == 2:
        word_blocks = [word_block, lax.ppermute(word_block, "grp", core_swap)]
    else:
        word_blocks = [word_block]
    down(places - 1)
    down(0, word_blocks[-1])
    for step in range(2, places):
        back(step)

    cands = groups * cand_local
    most = min(MOSTC, cands)
    ends = jnp.cumsum(cand_counts)
    start = ends[group] - cand_counts[group]
    near_ids = start * CAP + jnp.arange(most * CAP, dtype=jnp.int32)
    owned = near_ids < ends[group] * CAP

    def ids_of(core_at, sign):
        steps = jnp.arange(places, dtype=jnp.int32)[:, None]
        first = ((place + sign * steps) % places * cores + core_at) * word_rows
        return (first + jnp.arange(word_rows, dtype=jnp.int32)[None]).reshape(-1)

    core_order = [core, 1 - core][:cores]
    near = 0.0
    for core_at, block in zip(core_order, word_blocks):
        pick = near_ids[:, None] == ids_of(core_at, -1)[None, :]
        near = near + dot(pick.astype(jnp.bfloat16), block)
    near = slim(near)
    place_ids = jnp.concatenate(
        [ids_of(core_at, 1).reshape(places, word_rows) for core_at in core_order], axis=1
    ).reshape(-1)
    put = slim((place_ids[:, None] == near_ids[None, :]) & owned[None, :])
    my_out = wide(my_tokens) + (outs[0][0] + wide(outs[0][1]))
    if places > 1:
        my_out = my_out + wide(backs[places - 1])
    my_vision = slim(my_out)

    def embed(block):
        partial = dot(block, project_weight)
        if enc_count == 2:
            full = partial + wide(shifted(slim(partial), "enc", 1))
        else:
            full = lax.psum(partial, "enc")
        return slim(full * encoder_gain), jnp.sum(full * full, axis=-1)

    if split_heads:
        other_vision = shifted(my_vision, "vis", 1)
        vision_rows = jnp.where(
            vis == 0,
            jnp.concatenate([my_vision, other_vision]),
            jnp.concatenate([other_vision, my_vision]),
        )
        pieces = []
        for block in (my_vision, other_vision):
            scaled, power = embed(block)
            pieces.append(
                (heads_of(scaled, my_heads[1:]), slim(heads_of(scaled, other_heads[1:])), power)
            )
        image_kv = []
        for here, there in ((0, 1), (1, 0)):
            total = pieces[here][0] + wide(shifted(pieces[there][1], "vis", 1))
            power = pieces[here][2] + shifted(pieces[there][2], "vis", 1)
            image_kv.append(
                slim(total * lax.rsqrt(power / width + EPSILON)[:, None, None])
            )
        image_kv = jnp.concatenate(image_kv)
    else:
        vision_rows = joined(my_vision, "vis", 0)
        scaled, power = embed(vision_rows)
        total = head_sum(heads_of(scaled, qkv_weight[1:]))
        power = lax.psum(power, "vis")
        image_kv = slim(total * lax.rsqrt(power / width + EPSILON)[:, None, None])

    live = near[:, 3 * share] > 0
    near = near[:, : 3 * share].reshape(most * CAP, 3, share // DH, DH)
    row_cand = jnp.arange(most * CAP, dtype=jnp.int32) // CAP
    own_allowed = (row_cand[:, None] == row_cand[None, :]) & live[None, :]
    image_kv = image_kv.reshape(rows, 2, share // DH, DH)
    query = near[:, 0]

    def scores_of(keys):
        return jnp.einsum(
            "qhd,khd->hqk", query, keys, preferred_element_type=jnp.float32
        ) * DH ** (-0.5)

    def mixed(weights, values):
        return jnp.einsum(
            "hqk,khd->hqd", slim(weights), values, preferred_element_type=jnp.float32
        )

    image_scores = scores_of(image_kv[:, 0])
    own_scores = jnp.where(own_allowed[None], scores_of(near[:, 1]), FLOOR)
    top = jnp.maximum(
        jnp.max(image_scores, axis=-1, keepdims=True), jnp.max(own_scores, axis=-1, keepdims=True)
    )
    image_weights = jnp.exp(image_scores - top)
    own_weights = jnp.where(own_allowed[None], jnp.exp(own_scores - top), 0.0)
    total = jnp.sum(image_weights, axis=-1, keepdims=True) + jnp.sum(
        own_weights, axis=-1, keepdims=True
    )
    result = (mixed(image_weights, image_kv[:, 1]) + mixed(own_weights, near[:, 2])) / total
    result = slim(result).transpose(1, 0, 2).reshape(most * CAP, share)
    spread_out = slim(dot(put, result)).reshape(places, cores * word_rows, share)
    landed = spread_out[0]
    for step in range(1, places):
        landed = landed + to_place(spread_out[step], step)
    kept = landed[:word_rows]
    attended = kept
    if cores == 2:
        given = landed[word_rows:]
        attended = kept + lax.ppermute(given, "grp", core_swap)
    if split_heads:
        other = shifted(kept, "vis", 1)
        if cores == 2:
            across = [
                (v * groups + i, (1 - v) * groups + (i ^ 1)) for v in range(2) for i in range(groups)
            ]
            other = other + lax.ppermute(given, ("vis", "grp"), across)
        attended = jnp.concatenate([attended, other], axis=1)
    else:
        if shares > 1:
            attended = lax.all_gather(attended, "vis", axis=1, tiled=True)
    if enc_count == 2:
        enc = lax.axis_index("enc")
        slots = CAP // enc_count
        attended = attended.reshape(cand_local, CAP, inner)

        def branch(which):
            part = lax.dynamic_slice_in_dim(attended, which * slots, slots, axis=1)
            return dot(part.reshape(cand_local * slots, inner), final_weight)

        given = shifted(slim(branch(1 - enc)), "enc", 1)
        words_out = (branch(enc) + wide(given)).reshape(words.shape)
    else:
        partial_words = dot(attended, final_weight).reshape(cand_local, CAP, out_weight.shape[1])
        words_out = lax.psum_scatter(partial_words, "enc", scatter_dimension=1, tiled=True)
    caption_out = slim(words + words_out)
    return (vision_rows[None], caption_out)


def solution(mesh):
    return jax.shard_map(
        on_device,
        mesh=mesh,
        in_specs=(
            P("grp", None, "enc"),
            P("enc"),
            P("enc", ("vis", "grp")),
            P(("vis", "grp"), "enc"),
            P("enc", "vis"),
            P("vis"),
            P(None, "vis", "enc"),
            P("enc", "vis"),
            P("grp", "enc", "vis"),
            P(),
            P("grp"),
        ),
        out_specs=(P("grp", None, "enc"), P("grp", "enc", "vis")),
        check_vma=False,
    )
```

```python
import functools

import jax
import jax.numpy as jnp
from jax import lax
from jax.experimental import pallas as pl
from jax.experimental.pallas import tpu as pltpu
from jax.sharding import PartitionSpec as P

DH = 256
CAP = 16
MOSTC = 12


EPSILON = 1e-06
FLOOR = -1e30


def dot(a, b):
    return jnp.dot(a, b, preferred_element_type=jnp.float32)


def wide(a):
    return a.astype(jnp.float32)


def slim(a):
    return a.astype(jnp.bfloat16)


def shifted(value, axis, step):
    count = lax.axis_size(axis)
    return lax.ppermute(value, axis, [(i, (i + step) % count) for i in range(count)])


def summed(value, axis):
    if lax.axis_size(axis) != 2:
        return lax.psum(value, axis)
    return value + shifted(value, axis, 1)


def joined(value, axis, dim):
    if lax.axis_size(axis) != 2:
        return lax.all_gather(value, axis, axis=dim, tiled=True)
    other = shifted(value, axis, 1)
    first = lax.axis_index(axis) == 0
    return jnp.concatenate(
        [jnp.where(first, value, other), jnp.where(first, other, value)], axis=dim
    )


TOKEN = (8, 128)
HBM = pl.BlockSpec(memory_space=pl.ANY)
VMEM = pl.BlockSpec(memory_space=pltpu.VMEM)
LIGHT = pl.CostEstimate(flops=1024, bytes_accessed=1024, transcendentals=0)
PARAMS = pltpu.CompilerParams(vmem_limit_bytes=32 * 1024 * 1024)


def tile_of(size, most):
    return most if size % most == 0 else size


def up_kernel(cores, steps, mine_ref, theirs_ref, *refs):
    weights, (out_ref, token_ref, rows_ref, held, sems) = refs[:cores], refs[-5:]
    half = mine_ref.shape[0]
    tile = held.shape[2]
    copies = [
        pltpu.make_async_copy(
            weights[core].at[:, pl.ds(step * tile, tile)],
            held.at[core * steps + step],
            sems.at[core * steps + step],
        )
        for core in range(cores)
        for step in range(steps)
    ]
    for copy in copies:
        copy.start()
    rows_ref[:half] = mine_ref[...]
    rows_ref[half:] = theirs_ref[...]
    token_ref[...] = jnp.zeros(TOKEN, jnp.float32)
    for at, copy in enumerate(copies):
        copy.wait()
        out_ref[:, at * tile : (at + 1) * tile] = slim(dot(rows_ref[...], held[at]))


def up_call(halves, weights, after):
    cores = len(weights)
    depth, units = weights[0].shape
    tile = tile_of(units, 256)
    steps = units // tile
    rows = 2 * halves[0].shape[0]
    return pl.pallas_call(
        functools.partial(up_kernel, cores, steps),
        in_specs=[VMEM, VMEM] + [HBM] * (cores + len(after)),
        out_specs=[VMEM, VMEM],
        out_shape=[
            jax.ShapeDtypeStruct((rows, cores * units), jnp.bfloat16),
            jax.ShapeDtypeStruct(TOKEN, jnp.float32),
        ],
        scratch_shapes=[
            pltpu.VMEM((rows, depth), jnp.bfloat16),
            pltpu.VMEM((cores * steps, depth, tile), jnp.bfloat16),
            pltpu.SemaphoreType.DMA((cores * steps,)),
        ],
        compiler_params=PARAMS,
        cost_estimate=LIGHT,
    )(*halves, *weights, *after)


def down_kernel(cores, steps, own_ref, other_ref, *refs):
    weights, (kept_ref, sent_ref, token_ref, held, total_ref, sems) = refs[:cores], refs[-6 - cores : -cores]
    hidden = refs[-cores:]
    tile, columns = held.shape[1:]
    half = kept_ref.shape[0]
    part = tile_of(columns, 512)
    copies = {
        (core, step): pltpu.make_async_copy(
            weights[core].at[pl.ds(step * tile, tile)],
            held.at[core * steps + step],
            sems.at[core * steps + step],
        )
        for step in range(steps)
        for core in range(cores)
    }
    for copy in copies.values():
        copy.start()
    token_ref[...] = jnp.zeros(TOKEN, jnp.float32)

    def fill(core, step):
        first = (core * steps + step) * tile
        total = wide(own_ref[:, first : first + tile]) + wide(other_ref[:, first : first + tile])
        hidden[core][...] = slim(0.5 * total * (1.0 + lax.erf(total * 0.5**0.5)))

    fill(0, 0)
    order = [(core, step) for step in range(steps) for core in range(cores)]
    for at, (core, step) in enumerate(order):
        copies[core, step].wait()
        for start in range(0, columns, part):
            term = dot(hidden[core][...], held[core * steps + step, :, start : start + part])
            if at:
                term = total_ref[:, start : start + part] + term
            if at + 1 < len(order):
                total_ref[:, start : start + part] = term
            else:
                kept_ref[:, start : start + part] = slim(term[:half])
                sent_ref[:, start : start + part] = slim(term[half:])
        if at + 1 < len(order):
            fill(*order[at + 1])


def down_call(own, other, weights, after):
    cores = len(weights)
    units, columns = weights[0].shape
    tile = tile_of(units, 256)
    steps = units // tile
    rows = own.shape[0]
    half = jax.ShapeDtypeStruct((rows // 2, columns), jnp.bfloat16)
    return pl.pallas_call(
        functools.partial(down_kernel, cores, steps),
        in_specs=[VMEM, VMEM] + [HBM] * (cores + len(after)),
        out_specs=[VMEM, VMEM, VMEM],
        out_shape=[half, half, jax.ShapeDtypeStruct(TOKEN, jnp.float32)],
        scratch_shapes=[
            pltpu.VMEM((cores * steps, tile, columns), jnp.bfloat16),
            pltpu.VMEM((rows, columns), jnp.float32),
            pltpu.SemaphoreType.DMA((cores * steps,)),
        ]
        + [pltpu.VMEM((rows, tile), jnp.bfloat16) for _ in range(cores)],
        compiler_params=PARAMS,
        cost_estimate=LIGHT,
    )(own, other, *weights, *after)


def heads_kernel(kinds, first, vis_ref, rows_ref, weight_ref, *refs):
    sent_ref, kept_ref, token_ref, held, sems = refs[-5:]
    share = held.shape[2]
    copies = []
    for at in range(2 * kinds):
        which = vis_ref[0] if at >= kinds else 1 - vis_ref[0]
        copies.append(
            pltpu.make_async_copy(
                weight_ref.at[first + at % kinds, :, pl.ds(pl.multiple_of(which * share, share), share)],
                held.at[at],
                sems.at[at],
            )
        )
    for copy in copies:
        copy.start()
    token_ref[...] = jnp.zeros(TOKEN, jnp.float32)
    for at, copy in enumerate(copies):
        copy.wait()
        term = dot(rows_ref[...], held[at])
        columns = slice(at % kinds * share, (at % kinds + 1) * share)
        if at < kinds:
            sent_ref[:, columns] = slim(term)
        else:
            kept_ref[:, columns] = term


def heads_call(block, weight, first, vis, after):
    kinds = weight.shape[0] - first
    depth, share = weight.shape[1], weight.shape[2] // 2
    shape = (block.shape[0], kinds * share)
    return pl.pallas_call(
        functools.partial(heads_kernel, kinds, first),
        in_specs=[pl.BlockSpec(memory_space=pltpu.SMEM), VMEM] + [HBM] * (1 + len(after)),
        out_specs=[VMEM, VMEM, VMEM],
        out_shape=[
            jax.ShapeDtypeStruct(shape, jnp.bfloat16),
            jax.ShapeDtypeStruct(shape, jnp.float32),
            jax.ShapeDtypeStruct(TOKEN, jnp.float32),
        ],
        scratch_shapes=[
            pltpu.VMEM((2 * kinds, depth, share), jnp.bfloat16),
            pltpu.SemaphoreType.DMA((2 * kinds,)),
        ],
        compiler_params=PARAMS,
        cost_estimate=LIGHT,
    )(vis.reshape(1), block, weight, *after)


def on_device(
    image_tokens,
    vision_gain,
    up_weight,
    down_weight,
    project_weight,
    encoder_gain,
    qkv_weight,
    out_weight,
    captions,
    cand_counts,
    caption_lengths,
):
    vis_count = lax.axis_size("vis")
    enc_count = lax.axis_size("enc")
    groups = lax.axis_size("grp")
    vis = lax.axis_index("vis")
    group = lax.axis_index("grp")
    rows, features = image_tokens.shape[1:]
    all_features = features * enc_count
    width = captions.shape[2] * vis_count
    pair = vis_count == 2
    part_rows = rows // vis_count

    cores = 2 if groups % 2 == 0 else 1
    places = groups // cores
    place, core = group // cores, group % cores
    core_swap = [(i, i ^ 1) for i in range(groups)]
    up_weights, down_weights = [up_weight], [down_weight]
    if cores == 2:
        up_weights.append(lax.ppermute(up_weight, "grp", core_swap))
        down_weights.append(lax.ppermute(down_weight, "grp", core_swap))
        if up_weight.shape[1] % 128:
            up_weights = [jnp.concatenate(up_weights, axis=1)]
            down_weights = [jnp.concatenate(down_weights)]

    def to_place(value, step):
        return lax.ppermute(
            value, "grp", [(i, (i + step * cores) % groups) for i in range(groups)]
        )

    def mine_of(value):
        return lax.dynamic_slice_in_dim(value, vis * part_rows, part_rows, axis=0)

    def halves_of(mine, value):
        if pair and value is None:
            return [mine, shifted(mine, "vis", 1)]
        if pair:
            return [mine, lax.dynamic_slice_in_dim(value, (1 - vis) * part_rows, part_rows, axis=0)]
        if value is None:
            value = lax.all_gather(mine, "vis", axis=0, tiled=True)
        return [value[: rows // 2], value[rows // 2 :]]

    token = []

    def gated(value):
        return value + token[0][0, 0].astype(value.dtype) if token else value

    words = wide(captions)
    word_power = summed(jnp.sum(words * words, axis=-1), "vis")
    tokens = wide(image_tokens[0])
    row_total, row_squares = summed(
        jnp.stack([jnp.sum(tokens, axis=-1), jnp.sum(tokens * tokens, axis=-1)]), "enc"
    )
    mean = row_total / all_features
    spread = row_squares / all_features - mean * mean
    normed = slim(
        (tokens - mean[:, None]) * lax.rsqrt(spread + EPSILON)[:, None] * vision_gain
    )
    my_tokens = mine_of(image_tokens[0])
    my_normed = mine_of(normed)

    inner = qkv_weight.shape[2]
    heads = inner // DH
    shares = vis_count if heads % vis_count == 0 else 1
    share = inner // shares
    split_heads = pair and shares == 2
    word_normed = slim(words * lax.rsqrt(word_power / width + EPSILON)[..., None] * encoder_gain)
    all_words = joined(word_normed, "enc", 1)
    cand_local = all_words.shape[0]
    word_rows = cand_local * CAP
    flat_words = all_words.reshape(word_rows, all_words.shape[2])

    def head_weights(which):
        return lax.dynamic_slice_in_dim(qkv_weight, which * share, share, axis=2)

    def heads_of(block, weight):
        return jnp.einsum("rd,kdh->rkh", block, weight, preferred_element_type=jnp.float32)

    def head_sum(values):
        if shares == 1:
            return lax.psum(values, "vis")
        return lax.psum_scatter(values, "vis", scatter_dimension=2, tiled=True)

    arrived, blocks, pres, outs, backs = {}, {}, {}, {}, {}

    def forwarded(step):
        if step < places:
            here = gated(arrived[step])
            if step + 1 < places:
                arrived[step + 1] = to_place(here, 1)
            blocks[step] = halves_of(here, None)

    def up(step, *after):
        if step < places:
            pre, token[:] = (lambda got: (got[0], [got[1]]))(
                up_call(blocks[step], up_weights, [*token, *after])
            )
            if enc_count == 2:
                pres[step] = pre, shifted(pre, "enc", 1)
            else:
                pres[step] = pre, slim(lax.psum(wide(pre), "enc") - wide(pre))

    def down(step, *after):
        if step < places:
            kept, sent, next_token = down_call(*pres[step], down_weights, [*token, *after])
            token[:] = [next_token]
            if pair:
                outs[step] = kept, shifted(sent, "vis", 1)
            else:
                out = jnp.concatenate([kept, wide(sent)])
                kept = lax.psum_scatter(out, "vis", scatter_dimension=0, tiled=True)
                outs[step] = kept, jnp.zeros_like(kept, jnp.bfloat16)

    def back(step):
        if 0 < step < places:
            total = gated(wide(outs[step][0])) + wide(outs[step][1])
            if step > 1:
                total = total + wide(backs[step - 1])
            backs[step] = to_place(slim(total), 1)

    if places > 1:
        arrived[1] = to_place(my_normed, 1)
    if split_heads:
        word_sent, word_kept, word_token = heads_call(flat_words, qkv_weight, 0, vis, [my_normed])
        token[:] = [word_token]
        word_other = shifted(word_sent, "vis", 1)
    else:
        word_kept = head_sum(heads_of(flat_words, qkv_weight)).reshape(word_rows, 3 * share)
        word_other = jnp.zeros_like(word_kept, jnp.bfloat16)
    forwarded(1)
    row_at = jnp.arange(word_rows, dtype=jnp.int32) % CAP
    word_live = row_at < jnp.repeat(caption_lengths, CAP)
    flags = jnp.broadcast_to(word_live[:, None].astype(jnp.bfloat16), (word_rows, 128))
    blocks[0] = halves_of(my_normed, normed)
    up(0)
    forwarded(2)
    up(1, down_weights[-1])
    forwarded(3)
    up(2, pres[0][1], blocks[places - 1][0])
    message = jnp.concatenate([slim(word_kept + wide(word_other)), flags], axis=1)
    messages = [gated(message)]
    for _ in range(1, places):
        messages.append(to_place(messages[-1], 1))
    final_weight = out_weight
    if split_heads:
        final_weight = gated(
            jnp.concatenate(
                [
                    lax.dynamic_slice_in_dim(out_weight, vis * share, share, axis=0),
                    lax.dynamic_slice_in_dim(out_weight, (1 - vis) * share, share, axis=0),
                ]
            )
        )
    down(1)
    down(0, final_weight)
    up(3, messages[min(1, places - 1)])
    down(2, messages[min(2, places - 1)])
    back(1)
    for step in range(4, places):
        forwarded(step)
        up(step)
        down(step - 1)
    down(places - 1, messages[min(3, places - 1)])
    word_block = jnp.concatenate(messages)
    if cores == 2:
        word_blocks = [word_block, lax.ppermute(word_block, "grp", core_swap)]
    else:
        word_blocks = [word_block]
    for step in range(2, places):
        back(step)

    cands = groups * cand_local
    most = min(MOSTC, cands)
    ends = jnp.cumsum(cand_counts)
    start = ends[group] - cand_counts[group]
    near_ids = start * CAP + jnp.arange(most * CAP, dtype=jnp.int32)
    owned = near_ids < ends[group] * CAP

    def ids_of(core_at, sign):
        steps = jnp.arange(places, dtype=jnp.int32)[:, None]
        first = ((place + sign * steps) % places * cores + core_at) * word_rows
        return (first + jnp.arange(word_rows, dtype=jnp.int32)[None]).reshape(-1)

    core_order = [core, 1 - core][:cores]
    near = 0.0
    for core_at, block in zip(core_order, word_blocks):
        pick = near_ids[:, None] == ids_of(core_at, -1)[None, :]
        near = near + dot(pick.astype(jnp.bfloat16), block)
    near = slim(near)
    place_ids = jnp.concatenate(
        [ids_of(core_at, 1).reshape(places, word_rows) for core_at in core_order], axis=1
    ).reshape(-1)
    put = slim((place_ids[:, None] == near_ids[None, :]) & owned[None, :])
    my_out = wide(my_tokens) + (wide(outs[0][0]) + wide(outs[0][1]))
    if places > 1:
        my_out = my_out + wide(backs[places - 1])
    my_vision = slim(my_out)

    def embed(block):
        partial = dot(block, project_weight)
        if enc_count == 2:
            full = partial + wide(shifted(slim(partial), "enc", 1))
        else:
            full = lax.psum(partial, "enc")
        return slim(full * encoder_gain), jnp.sum(full * full, axis=-1)

    if split_heads:
        my_heads, other_heads = head_weights(vis), head_weights(1 - vis)
        other_vision = shifted(my_vision, "vis", 1)
        vision_rows = jnp.where(
            vis == 0,
            jnp.concatenate([my_vision, other_vision]),
            jnp.concatenate([other_vision, my_vision]),
        )
        pieces = []
        for block in (my_vision, other_vision):
            scaled, power = embed(block)
            pieces.append(
                (heads_of(scaled, my_heads[1:]), slim(heads_of(scaled, other_heads[1:])), power)
            )
        image_kv = []
        for here, there in ((0, 1), (1, 0)):
            total = pieces[here][0] + wide(shifted(pieces[there][1], "vis", 1))
            power = pieces[here][2] + shifted(pieces[there][2], "vis", 1)
            image_kv.append(
                slim(total * lax.rsqrt(power / width + EPSILON)[:, None, None])
            )
        image_kv = jnp.concatenate(image_kv)
    else:
        vision_rows = joined(my_vision, "vis", 0)
        scaled, power = embed(vision_rows)
        total = head_sum(heads_of(scaled, qkv_weight[1:]))
        power = lax.psum(power, "vis")
        image_kv = slim(total * lax.rsqrt(power / width + EPSILON)[:, None, None])

    live = near[:, 3 * share] > 0
    near = near[:, : 3 * share].reshape(most * CAP, 3, share // DH, DH)
    row_cand = jnp.arange(most * CAP, dtype=jnp.int32) // CAP
    own_allowed = (row_cand[:, None] == row_cand[None, :]) & live[None, :]
    image_kv = image_kv.reshape(rows, 2, share // DH, DH)
    query = near[:, 0]

    def scores_of(keys):
        return jnp.einsum(
            "qhd,khd->hqk", query, keys, preferred_element_type=jnp.float32
        ) * DH ** (-0.5)

    def mixed(weights, values):
        return jnp.einsum(
            "hqk,khd->hqd", slim(weights), values, preferred_element_type=jnp.float32
        )

    image_scores = scores_of(image_kv[:, 0])
    own_scores = jnp.where(own_allowed[None], scores_of(near[:, 1]), FLOOR)
    top = jnp.maximum(
        jnp.max(image_scores, axis=-1, keepdims=True), jnp.max(own_scores, axis=-1, keepdims=True)
    )
    image_weights = jnp.exp(image_scores - top)
    own_weights = jnp.where(own_allowed[None], jnp.exp(own_scores - top), 0.0)
    total = jnp.sum(image_weights, axis=-1, keepdims=True) + jnp.sum(
        own_weights, axis=-1, keepdims=True
    )
    result = (mixed(image_weights, image_kv[:, 1]) + mixed(own_weights, near[:, 2])) / total
    result = slim(result).transpose(1, 0, 2).reshape(most * CAP, share)
    spread_out = slim(dot(put, result)).reshape(places, cores * word_rows, share)
    landed = spread_out[0]
    for step in range(1, places):
        landed = landed + to_place(spread_out[step], step)
    kept = landed[:word_rows]
    attended = kept
    if cores == 2:
        given = landed[word_rows:]
        attended = kept + lax.ppermute(given, "grp", core_swap)
    if split_heads:
        other = shifted(kept, "vis", 1)
        if cores == 2:
            across = [
                (v * groups + i, (1 - v) * groups + (i ^ 1)) for v in range(2) for i in range(groups)
            ]
            other = other + lax.ppermute(given, ("vis", "grp"), across)
        attended = jnp.concatenate([attended, other], axis=1)
    else:
        if shares > 1:
            attended = lax.all_gather(attended, "vis", axis=1, tiled=True)
    if enc_count == 2:
        enc = lax.axis_index("enc")
        slots = CAP // enc_count
        attended = attended.reshape(cand_local, CAP, inner)

        def branch(which):
            part = lax.dynamic_slice_in_dim(attended, which * slots, slots, axis=1)
            return dot(part.reshape(cand_local * slots, inner), final_weight)

        given = shifted(slim(branch(1 - enc)), "enc", 1)
        words_out = (branch(enc) + wide(given)).reshape(words.shape)
    else:
        partial_words = dot(attended, final_weight).reshape(cand_local, CAP, out_weight.shape[1])
        words_out = lax.psum_scatter(partial_words, "enc", scatter_dimension=1, tiled=True)
    caption_out = slim(words + words_out)
    return (vision_rows[None], caption_out)


def solution(mesh):
    return jax.shard_map(
        on_device,
        mesh=mesh,
        in_specs=(
            P("grp", None, "enc"),
            P("enc"),
            P("enc", ("vis", "grp")),
            P(("vis", "grp"), "enc"),
            P("enc", "vis"),
            P("vis"),
            P(None, "vis", "enc"),
            P("enc", "vis"),
            P("grp", "enc", "vis"),
            P(),
            P("grp"),
        ),
        out_specs=(P("grp", None, "enc"), P("grp", "enc", "vis")),
        check_vma=False,
    )
```

```python
import functools

import jax
import jax.numpy as jnp
from jax import lax
from jax.experimental import pallas as pl
from jax.experimental.pallas import tpu as pltpu
from jax.sharding import PartitionSpec as P

DH = 256
CAP = 16
MOSTC = 12


EPSILON = 1e-06
FLOOR = -1e30


def dot(a, b):
    return jnp.dot(a, b, preferred_element_type=jnp.float32)


def wide(a):
    return a.astype(jnp.float32)


def slim(a):
    return a.astype(jnp.bfloat16)


def shifted(value, axis, step):
    count = lax.axis_size(axis)
    return lax.ppermute(value, axis, [(i, (i + step) % count) for i in range(count)])


def summed(value, axis):
    if lax.axis_size(axis) != 2:
        return lax.psum(value, axis)
    return value + shifted(value, axis, 1)


def joined(value, axis, dim):
    if lax.axis_size(axis) != 2:
        return lax.all_gather(value, axis, axis=dim, tiled=True)
    other = shifted(value, axis, 1)
    first = lax.axis_index(axis) == 0
    return jnp.concatenate(
        [jnp.where(first, value, other), jnp.where(first, other, value)], axis=dim
    )


TOKEN = (8, 128)
HBM = pl.BlockSpec(memory_space=pl.ANY)
VMEM = pl.BlockSpec(memory_space=pltpu.VMEM)
LIGHT = pl.CostEstimate(flops=1024, bytes_accessed=1024, transcendentals=0)
PARAMS = pltpu.CompilerParams(vmem_limit_bytes=20 * 1024 * 1024)


def tile_of(size, most):
    return most if size % most == 0 else size


def pass_kernel(value_ref, token_ref, out_ref):
    pass


def passed(value, token):
    return pl.pallas_call(
        pass_kernel,
        in_specs=[HBM, HBM],
        out_specs=HBM,
        out_shape=jax.ShapeDtypeStruct(value.shape, value.dtype),
        input_output_aliases={0: 0},
        compiler_params=PARAMS,
        cost_estimate=LIGHT,
    )(value, token)


def up_kernel(cores, mine_ref, theirs_ref, *refs):
    weights, (out_ref, token_ref, rows_ref) = refs[:cores], refs[-3:]
    half = mine_ref.shape[0]
    units = weights[0].shape[1]
    tile = tile_of(units, 256)
    rows_ref[:half] = mine_ref[...]
    rows_ref[half:] = theirs_ref[...]
    token_ref[...] = jnp.zeros(TOKEN, jnp.float32)
    for core in range(cores):
        for first in range(0, units, tile):
            out_ref[:, core * units + first : core * units + first + tile] = slim(
                dot(rows_ref[...], weights[core][:, first : first + tile])
            )


def up_call(halves, weights, after):
    cores = len(weights)
    depth, units = weights[0].shape
    rows = 2 * halves[0].shape[0]
    return pl.pallas_call(
        functools.partial(up_kernel, cores),
        in_specs=[VMEM] * (2 + cores) + [HBM] * len(after),
        out_specs=[VMEM, VMEM],
        out_shape=[
            jax.ShapeDtypeStruct((rows, cores * units), jnp.bfloat16),
            jax.ShapeDtypeStruct(TOKEN, jnp.float32),
        ],
        scratch_shapes=[pltpu.VMEM((rows, depth), jnp.bfloat16)],
        compiler_params=PARAMS,
        cost_estimate=LIGHT,
    )(*halves, *weights, *after)


def down_kernel(cores, own_ref, other_ref, *refs):
    weights, (kept_ref, sent_ref, token_ref, total_ref) = refs[:cores], refs[-6:-2]
    hidden = refs[-2:]
    units, columns = weights[0].shape
    tile = tile_of(units, 256)
    half = kept_ref.shape[0]
    part = tile_of(columns, 512)
    token_ref[...] = jnp.zeros(TOKEN, jnp.float32)
    order = [(core, first) for core in range(cores) for first in range(0, units, tile)]

    def fill(at):
        core, first = order[at]
        columns_at = slice(core * units + first, core * units + first + tile)
        total = wide(own_ref[:, columns_at]) + wide(other_ref[:, columns_at])
        hidden[at % 2][...] = slim(0.5 * total * (1.0 + lax.erf(total * 0.5**0.5)))

    fill(0)
    for at, (core, first) in enumerate(order):
        for start in range(0, columns, part):
            term = dot(hidden[at % 2][...], weights[core][first : first + tile, start : start + part])
            if at:
                term = total_ref[:, start : start + part] + term
            if at + 1 < len(order):
                total_ref[:, start : start + part] = term
            else:
                kept_ref[:, start : start + part] = slim(term[:half])
                sent_ref[:, start : start + part] = slim(term[half:])
        if at + 1 < len(order):
            fill(at + 1)


def down_call(own, other, weights, after):
    cores = len(weights)
    units, columns = weights[0].shape
    tile = tile_of(units, 256)
    rows = own.shape[0]
    half = jax.ShapeDtypeStruct((rows // 2, columns), jnp.bfloat16)
    return pl.pallas_call(
        functools.partial(down_kernel, cores),
        in_specs=[VMEM] * (2 + cores) + [HBM] * len(after),
        out_specs=[VMEM, VMEM, VMEM],
        out_shape=[half, half, jax.ShapeDtypeStruct(TOKEN, jnp.float32)],
        scratch_shapes=[pltpu.VMEM((rows, columns), jnp.float32)]
        + [pltpu.VMEM((rows, tile), jnp.bfloat16)] * 2,
        compiler_params=PARAMS,
        cost_estimate=LIGHT,
    )(own, other, *weights, *after)


def project_kernel(rows_ref, weight_ref, out_ref):
    columns = weight_ref.shape[1]
    part = tile_of(columns, 512)
    for first in range(0, columns, part):
        out_ref[:, first : first + part] = slim(
            dot(rows_ref[...], weight_ref[:, first : first + part])
        )


def project_call(rows, weight):
    return pl.pallas_call(
        project_kernel,
        in_specs=[VMEM, VMEM],
        out_specs=VMEM,
        out_shape=jax.ShapeDtypeStruct((rows.shape[0], weight.shape[1]), jnp.bfloat16),
        compiler_params=PARAMS,
        cost_estimate=LIGHT,
    )(rows, weight)


def image_kernel(vis_ref, own_ref, other_ref, gain_ref, weight_ref, kept_ref, sent_ref, power_ref):
    share = weight_ref.shape[2] // 2
    full = wide(own_ref[...]) + wide(other_ref[...])
    power = jnp.sum(full * full, axis=1, keepdims=True)
    scaled = slim(full * gain_ref[...])
    power_ref[...] = jnp.broadcast_to(power, power_ref.shape)
    high = slim(power)
    middle = slim(power - wide(high))
    low = slim(power - wide(high) - wide(middle))
    lane = lax.broadcasted_iota(jnp.int32, (power.shape[0], 128), 1)
    parts = jnp.where(lane == 0, wide(high), jnp.where(lane == 1, wide(middle), wide(low)))
    sent_ref[:, 2 * share :] = slim(jnp.where(lane < 3, parts, 0.0))
    vis = vis_ref[0]
    for kind in range(2):
        columns = slice(kind * share, (kind + 1) * share)
        other = pl.ds(pl.multiple_of((1 - vis) * share, share), share)
        sent_ref[:, columns] = slim(dot(scaled, weight_ref[kind + 1, :, other]))
    for kind in range(2):
        columns = slice(kind * share, (kind + 1) * share)
        mine = pl.ds(pl.multiple_of(vis * share, share), share)
        kept_ref[:, columns] = dot(scaled, weight_ref[kind + 1, :, mine])


def image_call(own, other, gain, weight, vis):
    rows = own.shape[0]
    share = weight.shape[2] // 2
    return pl.pallas_call(
        image_kernel,
        in_specs=[pl.BlockSpec(memory_space=pltpu.SMEM)] + [VMEM] * 4,
        out_specs=[VMEM] * 3,
        out_shape=[
            jax.ShapeDtypeStruct((rows, 2 * share), jnp.float32),
            jax.ShapeDtypeStruct((rows, 2 * share + 128), jnp.bfloat16),
            jax.ShapeDtypeStruct((rows, 128), jnp.float32),
        ],
        compiler_params=PARAMS,
        cost_estimate=LIGHT,
    )(vis.reshape(1), own, other, gain[None], weight)


def heads_kernel(vis_ref, rows_ref, weight_ref, *refs):
    sent_ref, kept_ref, token_ref = refs[-3:]
    kinds, _, inner = weight_ref.shape
    share = inner // 2
    vis = vis_ref[0]
    token_ref[...] = jnp.zeros(TOKEN, jnp.float32)
    for which, out_ref in ((1 - vis, sent_ref), (vis, kept_ref)):
        for kind in range(kinds):
            heads = pl.ds(pl.multiple_of(which * share, share), share)
            term = dot(rows_ref[...], weight_ref[kind, :, heads])
            out_ref[:, kind * share : (kind + 1) * share] = term.astype(out_ref.dtype)


def heads_call(block, weight, vis, after):
    shape = (block.shape[0], weight.shape[0] * weight.shape[2] // 2)
    return pl.pallas_call(
        heads_kernel,
        in_specs=[pl.BlockSpec(memory_space=pltpu.SMEM), VMEM, VMEM] + [HBM] * len(after),
        out_specs=[VMEM, VMEM, VMEM],
        out_shape=[
            jax.ShapeDtypeStruct(shape, jnp.bfloat16),
            jax.ShapeDtypeStruct(shape, jnp.float32),
            jax.ShapeDtypeStruct(TOKEN, jnp.float32),
        ],
        compiler_params=PARAMS,
        cost_estimate=LIGHT,
    )(vis.reshape(1), block, weight, *after)


def on_device(
    image_tokens,
    vision_gain,
    up_weight,
    down_weight,
    project_weight,
    encoder_gain,
    qkv_weight,
    out_weight,
    captions,
    cand_counts,
    caption_lengths,
):
    vis_count = lax.axis_size("vis")
    enc_count = lax.axis_size("enc")
    groups = lax.axis_size("grp")
    vis = lax.axis_index("vis")
    group = lax.axis_index("grp")
    rows, features = image_tokens.shape[1:]
    all_features = features * enc_count
    width = captions.shape[2] * vis_count
    pair = vis_count == 2
    part_rows = rows // vis_count

    cores = 2 if groups % 2 == 0 else 1
    places = groups // cores
    place, core = group // cores, group % cores
    core_swap = [(i, i ^ 1) for i in range(groups)]
    up_weights, down_weights = [up_weight], [down_weight]
    if cores == 2:
        up_weights.append(lax.ppermute(up_weight, "grp", core_swap))
        down_weights.append(lax.ppermute(down_weight, "grp", core_swap))
        if up_weight.shape[1] % 128:
            up_weights = [jnp.concatenate(up_weights, axis=1)]
            down_weights = [jnp.concatenate(down_weights)]

    def to_place(value, step):
        return lax.ppermute(
            value, "grp", [(i, (i + step * cores) % groups) for i in range(groups)]
        )

    def mine_of(value):
        return lax.dynamic_slice_in_dim(value, vis * part_rows, part_rows, axis=0)

    def halves_of(mine, value):
        if pair and value is None:
            return [mine, shifted(mine, "vis", 1)]
        if pair:
            return [mine, lax.dynamic_slice_in_dim(value, (1 - vis) * part_rows, part_rows, axis=0)]
        if value is None:
            value = lax.all_gather(mine, "vis", axis=0, tiled=True)
        return [value[: rows // 2], value[rows // 2 :]]

    token = []

    def gated(value):
        return value + token[0][0, 0].astype(value.dtype) if token else value

    words = wide(captions)
    word_power = summed(jnp.sum(words * words, axis=-1), "vis")
    tokens = wide(image_tokens[0])
    row_total, row_squares = summed(
        jnp.stack([jnp.sum(tokens, axis=-1), jnp.sum(tokens * tokens, axis=-1)]), "enc"
    )
    mean = row_total / all_features
    spread = row_squares / all_features - mean * mean
    normed = slim(
        (tokens - mean[:, None]) * lax.rsqrt(spread + EPSILON)[:, None] * vision_gain
    )
    my_tokens = mine_of(image_tokens[0])
    my_normed = mine_of(normed)

    inner = qkv_weight.shape[2]
    heads = inner // DH
    shares = vis_count if heads % vis_count == 0 else 1
    share = inner // shares
    split_heads = pair and shares == 2
    word_normed = slim(words * lax.rsqrt(word_power / width + EPSILON)[..., None] * encoder_gain)
    all_words = joined(word_normed, "enc", 1)
    cand_local = all_words.shape[0]
    word_rows = cand_local * CAP
    flat_words = all_words.reshape(word_rows, all_words.shape[2])

    def head_weights(which):
        return lax.dynamic_slice_in_dim(qkv_weight, which * share, share, axis=2)

    def heads_of(block, weight):
        return jnp.einsum("rd,kdh->rkh", block, weight, preferred_element_type=jnp.float32)

    def head_sum(values):
        if shares == 1:
            return lax.psum(values, "vis")
        return lax.psum_scatter(values, "vis", scatter_dimension=2, tiled=True)

    arrived, blocks, pres, outs, backs = {}, {}, {}, {}, {}

    def forwarded(step):
        if step < places:
            here = passed(arrived[step], token[0]) if step > 1 else arrived[step]
            if step + 1 < places:
                arrived[step + 1] = to_place(here, 1)
            blocks[step] = halves_of(here, None)

    def up(step, *after):
        if step < places:
            pre, token[:] = (lambda got: (got[0], [got[1]]))(
                up_call(blocks[step], up_weights, [*token, *after])
            )
            if enc_count == 2:
                pres[step] = pre, shifted(pre, "enc", 1)
            else:
                pres[step] = pre, slim(lax.psum(wide(pre), "enc") - wide(pre))

    def down(step, *after):
        if step < places:
            kept, sent, next_token = down_call(*pres[step], down_weights, [*token, *after])
            token[:] = [next_token]
            if pair:
                outs[step] = kept, shifted(sent, "vis", 1)
            else:
                out = jnp.concatenate([kept, wide(sent)])
                kept = lax.psum_scatter(out, "vis", scatter_dimension=0, tiled=True)
                outs[step] = kept, jnp.zeros_like(kept, jnp.bfloat16)

    def back(step):
        if 0 < step < places:
            total = gated(wide(outs[step][0])) + wide(outs[step][1])
            if step > 1:
                total = total + wide(backs[step - 1])
            backs[step] = to_place(slim(total), 1)

    if places > 1:
        arrived[1] = to_place(my_normed, 1)
    if split_heads:
        word_sent, word_kept, word_token = heads_call(flat_words, qkv_weight, vis, [my_normed])
        token[:] = [word_token]
        word_other = shifted(word_sent, "vis", 1)
    else:
        word_kept = head_sum(heads_of(flat_words, qkv_weight)).reshape(word_rows, 3 * share)
        word_other = jnp.zeros_like(word_kept, jnp.bfloat16)
    forwarded(1)
    row_at = jnp.arange(word_rows, dtype=jnp.int32) % CAP
    word_live = row_at < jnp.repeat(caption_lengths, CAP)
    flags = jnp.broadcast_to(word_live[:, None].astype(jnp.bfloat16), (word_rows, 128))
    blocks[0] = halves_of(my_normed, normed)
    up(0)
    forwarded(2)
    up(1, down_weights[-1])
    down(0)
    forwarded(3)
    up(2, blocks[places - 1][0])
    message = jnp.concatenate([slim(word_kept + wide(word_other)), flags], axis=1)
    messages = [gated(message)]
    for _ in range(1, places):
        messages.append(to_place(messages[-1], 1))
    final_weight = out_weight
    if split_heads:
        final_weight = gated(
            jnp.concatenate(
                [
                    lax.dynamic_slice_in_dim(out_weight, vis * share, share, axis=0),
                    lax.dynamic_slice_in_dim(out_weight, (1 - vis) * share, share, axis=0),
                ]
            )
        )
    down(1)
    up(3, final_weight)
    down(2, messages[min(1, places - 1)])
    back(1)
    for step in range(4, places):
        forwarded(step)
        up(step)
        down(step - 1)
    down(places - 1, messages[min(2, places - 1)])
    word_block = jnp.concatenate(messages)
    if cores == 2:
        word_blocks = [word_block, lax.ppermute(word_block, "grp", core_swap)]
    else:
        word_blocks = [word_block]
    for step in range(2, places):
        back(step)

    cands = groups * cand_local
    most = min(MOSTC, cands)
    ends = jnp.cumsum(cand_counts)
    start = ends[group] - cand_counts[group]
    near_ids = start * CAP + jnp.arange(most * CAP, dtype=jnp.int32)
    owned = near_ids < ends[group] * CAP

    def ids_of(core_at, sign):
        steps = jnp.arange(places, dtype=jnp.int32)[:, None]
        first = ((place + sign * steps) % places * cores + core_at) * word_rows
        return (first + jnp.arange(word_rows, dtype=jnp.int32)[None]).reshape(-1)

    core_order = [core, 1 - core][:cores]
    near = 0.0
    for core_at, block in zip(core_order, word_blocks):
        pick = near_ids[:, None] == ids_of(core_at, -1)[None, :]
        near = near + dot(pick.astype(jnp.bfloat16), block)
    near = slim(near)
    place_ids = jnp.concatenate(
        [ids_of(core_at, 1).reshape(places, word_rows) for core_at in core_order], axis=1
    ).reshape(-1)
    put = slim((place_ids[:, None] == near_ids[None, :]) & owned[None, :])
    my_out = wide(my_tokens) + (wide(outs[0][0]) + wide(outs[0][1]))
    if places > 1:
        my_out = my_out + wide(backs[places - 1])
    my_vision = slim(my_out)

    def embed(block):
        partial = dot(block, project_weight)
        if enc_count == 2:
            full = partial + wide(shifted(slim(partial), "enc", 1))
        else:
            full = lax.psum(partial, "enc")
        return slim(full * encoder_gain), jnp.sum(full * full, axis=-1)

    if split_heads:
        other_vision = shifted(my_vision, "vis", 1)
        vision_rows = jnp.where(
            vis == 0,
            jnp.concatenate([my_vision, other_vision]),
            jnp.concatenate([other_vision, my_vision]),
        )
        pieces = []
        for block in (my_vision, other_vision):
            partial = project_call(block, project_weight)
            if enc_count == 2:
                full = shifted(partial, "enc", 1)
            else:
                full = slim(lax.psum(wide(partial), "enc") - wide(partial))
            pieces.append(image_call(partial, full, encoder_gain, qkv_weight, vis))
        image_kv = []
        for here, there in ((0, 1), (1, 0)):
            kept, _, power = pieces[here]
            got = wide(shifted(pieces[there][1], "vis", 1))
            power = power[:, :1] + jnp.sum(got[:, 2 * share : 2 * share + 3], axis=1, keepdims=True)
            total = kept + got[:, : 2 * share]
            image_kv.append(slim(total * lax.rsqrt(power / width + EPSILON)))
        image_kv = jnp.concatenate(image_kv).reshape(rows, 2, share)
    else:
        vision_rows = joined(my_vision, "vis", 0)
        scaled, power = embed(vision_rows)
        total = head_sum(heads_of(scaled, qkv_weight[1:]))
        power = lax.psum(power, "vis")
        image_kv = slim(total * lax.rsqrt(power / width + EPSILON)[:, None, None])

    live = near[:, 3 * share] > 0
    near = near[:, : 3 * share].reshape(most * CAP, 3, share // DH, DH)
    row_cand = jnp.arange(most * CAP, dtype=jnp.int32) // CAP
    own_allowed = (row_cand[:, None] == row_cand[None, :]) & live[None, :]
    image_kv = image_kv.reshape(rows, 2, share // DH, DH)
    query = near[:, 0]

    def scores_of(keys):
        return jnp.einsum(
            "qhd,khd->hqk", query, keys, preferred_element_type=jnp.float32
        ) * DH ** (-0.5)

    def mixed(weights, values):
        return jnp.einsum(
            "hqk,khd->hqd", slim(weights), values, preferred_element_type=jnp.float32
        )

    image_scores = scores_of(image_kv[:, 0])
    own_scores = jnp.where(own_allowed[None], scores_of(near[:, 1]), FLOOR)
    top = jnp.maximum(
        jnp.max(image_scores, axis=-1, keepdims=True), jnp.max(own_scores, axis=-1, keepdims=True)
    )
    image_weights = jnp.exp(image_scores - top)
    own_weights = jnp.where(own_allowed[None], jnp.exp(own_scores - top), 0.0)
    total = jnp.sum(image_weights, axis=-1, keepdims=True) + jnp.sum(
        own_weights, axis=-1, keepdims=True
    )
    result = (mixed(image_weights, image_kv[:, 1]) + mixed(own_weights, near[:, 2])) / total
    result = slim(result).transpose(1, 0, 2).reshape(most * CAP, share)
    spread_out = slim(dot(put, result)).reshape(places, cores * word_rows, share)
    landed = spread_out[0]
    for step in range(1, places):
        landed = landed + to_place(spread_out[step], step)
    kept = landed[:word_rows]
    attended = kept
    if cores == 2:
        given = landed[word_rows:]
        attended = kept + lax.ppermute(given, "grp", core_swap)
    if split_heads:
        other = shifted(kept, "vis", 1)
        if cores == 2:
            across = [
                (v * groups + i, (1 - v) * groups + (i ^ 1)) for v in range(2) for i in range(groups)
            ]
            other = other + lax.ppermute(given, ("vis", "grp"), across)
        attended = jnp.concatenate([attended, other], axis=1)
    else:
        if shares > 1:
            attended = lax.all_gather(attended, "vis", axis=1, tiled=True)
    if enc_count == 2:
        enc = lax.axis_index("enc")
        slots = CAP // enc_count
        attended = attended.reshape(cand_local, CAP, inner)

        def branch(which):
            part = lax.dynamic_slice_in_dim(attended, which * slots, slots, axis=1)
            return dot(part.reshape(cand_local * slots, inner), final_weight)

        given = shifted(slim(branch(1 - enc)), "enc", 1)
        words_out = (branch(enc) + wide(given)).reshape(words.shape)
    else:
        partial_words = dot(attended, final_weight).reshape(cand_local, CAP, out_weight.shape[1])
        words_out = lax.psum_scatter(partial_words, "enc", scatter_dimension=1, tiled=True)
    caption_out = slim(words + words_out)
    return (vision_rows[None], caption_out)


def solution(mesh):
    return jax.shard_map(
        on_device,
        mesh=mesh,
        in_specs=(
            P("grp", None, "enc"),
            P("enc"),
            P("enc", ("vis", "grp")),
            P(("vis", "grp"), "enc"),
            P("enc", "vis"),
            P("vis"),
            P(None, "vis", "enc"),
            P("enc", "vis"),
            P("grp", "enc", "vis"),
            P(),
            P("grp"),
        ),
        out_specs=(P("grp", None, "enc"), P("grp", "enc", "vis")),
        check_vma=False,
    )
```

```python
import functools

import jax
import jax.numpy as jnp
from jax import lax
from jax.experimental import pallas as pl
from jax.experimental.pallas import tpu as pltpu
from jax.sharding import PartitionSpec as P

DH = 256
CAP = 16
MOSTC = 12


EPSILON = 1e-06
FLOOR = -1e30


def dot(a, b):
    return jnp.dot(a, b, preferred_element_type=jnp.float32)


def wide(a):
    return a.astype(jnp.float32)


def slim(a):
    return a.astype(jnp.bfloat16)


def shifted(value, axis, step):
    count = lax.axis_size(axis)
    return lax.ppermute(value, axis, [(i, (i + step) % count) for i in range(count)])


def summed(value, axis):
    if lax.axis_size(axis) != 2:
        return lax.psum(value, axis)
    return value + shifted(value, axis, 1)


def joined(value, axis, dim):
    if lax.axis_size(axis) != 2:
        return lax.all_gather(value, axis, axis=dim, tiled=True)
    other = shifted(value, axis, 1)
    first = lax.axis_index(axis) == 0
    return jnp.concatenate(
        [jnp.where(first, value, other), jnp.where(first, other, value)], axis=dim
    )


TOKEN = (8, 128)
HBM = pl.BlockSpec(memory_space=pl.ANY)
VMEM = pl.BlockSpec(memory_space=pltpu.VMEM)
SMEM = pl.BlockSpec(memory_space=pltpu.SMEM)
LIGHT = pl.CostEstimate(flops=1024, bytes_accessed=1024, transcendentals=0)
PARAMS = pltpu.CompilerParams(vmem_limit_bytes=20 * 1024 * 1024)


def tile_of(size, most):
    return most if size % most == 0 else size


def pass_kernel(value_ref, token_ref, out_ref):
    pass


def passed(value, token):
    return pl.pallas_call(
        pass_kernel,
        in_specs=[HBM, HBM],
        out_specs=HBM,
        out_shape=jax.ShapeDtypeStruct(value.shape, value.dtype),
        input_output_aliases={0: 0},
        compiler_params=PARAMS,
        cost_estimate=LIGHT,
    )(value, token)


def up_kernel(cores, mine_ref, theirs_ref, *refs):
    weights, (out_ref, token_ref, rows_ref) = refs[:cores], refs[-3:]
    half = mine_ref.shape[0]
    units = weights[0].shape[1]
    tile = tile_of(units, 256)
    rows_ref[:half] = mine_ref[...]
    rows_ref[half:] = theirs_ref[...]
    token_ref[...] = jnp.zeros(TOKEN, jnp.float32)
    for core in range(cores):
        for first in range(0, units, tile):
            out_ref[:, core * units + first : core * units + first + tile] = slim(
                dot(rows_ref[...], weights[core][:, first : first + tile])
            )


def up_call(halves, weights, after):
    cores = len(weights)
    depth, units = weights[0].shape
    rows = 2 * halves[0].shape[0]
    return pl.pallas_call(
        functools.partial(up_kernel, cores),
        in_specs=[VMEM] * (2 + cores) + [HBM] * len(after),
        out_specs=[VMEM, VMEM],
        out_shape=[
            jax.ShapeDtypeStruct((rows, cores * units), jnp.bfloat16),
            jax.ShapeDtypeStruct(TOKEN, jnp.float32),
        ],
        scratch_shapes=[pltpu.VMEM((rows, depth), jnp.bfloat16)],
        compiler_params=PARAMS,
        cost_estimate=LIGHT,
    )(*halves, *weights, *after)


def down_kernel(cores, own_ref, other_ref, *refs):
    weights, (kept_ref, sent_ref, token_ref, total_ref) = refs[:cores], refs[-6:-2]
    hidden = refs[-2:]
    units, columns = weights[0].shape
    tile = tile_of(units, 256)
    half = kept_ref.shape[0]
    part = tile_of(columns, 512)
    token_ref[...] = jnp.zeros(TOKEN, jnp.float32)
    order = [(core, first) for core in range(cores) for first in range(0, units, tile)]

    def fill(at):
        core, first = order[at]
        columns_at = slice(core * units + first, core * units + first + tile)
        total = wide(own_ref[:, columns_at]) + wide(other_ref[:, columns_at])
        hidden[at % 2][...] = slim(0.5 * total * (1.0 + lax.erf(total * 0.5**0.5)))

    fill(0)
    for at, (core, first) in enumerate(order):
        for start in range(0, columns, part):
            term = dot(hidden[at % 2][...], weights[core][first : first + tile, start : start + part])
            if at:
                term = total_ref[:, start : start + part] + term
            if at + 1 < len(order):
                total_ref[:, start : start + part] = term
            else:
                kept_ref[:, start : start + part] = slim(term[:half])
                sent_ref[:, start : start + part] = slim(term[half:])
        if at + 1 < len(order):
            fill(at + 1)


def down_call(own, other, weights, after):
    cores = len(weights)
    units, columns = weights[0].shape
    tile = tile_of(units, 256)
    rows = own.shape[0]
    half = jax.ShapeDtypeStruct((rows // 2, columns), jnp.bfloat16)
    return pl.pallas_call(
        functools.partial(down_kernel, cores),
        in_specs=[VMEM] * (2 + cores) + [HBM] * len(after),
        out_specs=[VMEM, VMEM, VMEM],
        out_shape=[half, half, jax.ShapeDtypeStruct(TOKEN, jnp.float32)],
        scratch_shapes=[pltpu.VMEM((rows, columns), jnp.float32)]
        + [pltpu.VMEM((rows, tile), jnp.bfloat16)] * 2,
        compiler_params=PARAMS,
        cost_estimate=LIGHT,
    )(own, other, *weights, *after)


def project_kernel(rows_ref, weight_ref, out_ref):
    columns = weight_ref.shape[1]
    part = tile_of(columns, 512)
    for first in range(0, columns, part):
        out_ref[:, first : first + part] = slim(
            dot(rows_ref[...], weight_ref[:, first : first + part])
        )


def project_call(rows, weight):
    return pl.pallas_call(
        project_kernel,
        in_specs=[VMEM, VMEM],
        out_specs=VMEM,
        out_shape=jax.ShapeDtypeStruct((rows.shape[0], weight.shape[1]), jnp.bfloat16),
        compiler_params=PARAMS,
        cost_estimate=LIGHT,
    )(rows, weight)


def image_kernel(vis_ref, own_ref, other_ref, gain_ref, weight_ref, kept_ref, sent_ref, power_ref):
    share = weight_ref.shape[2] // 2
    full = wide(own_ref[...]) + wide(other_ref[...])
    power = jnp.sum(full * full, axis=1, keepdims=True)
    scaled = slim(full * gain_ref[...])
    power_ref[...] = jnp.broadcast_to(power, power_ref.shape)
    high = slim(power)
    middle = slim(power - wide(high))
    low = slim(power - wide(high) - wide(middle))
    lane = lax.broadcasted_iota(jnp.int32, (power.shape[0], 128), 1)
    parts = jnp.where(lane == 0, wide(high), jnp.where(lane == 1, wide(middle), wide(low)))
    sent_ref[:, 2 * share :] = slim(jnp.where(lane < 3, parts, 0.0))
    vis = vis_ref[0]
    for kind in range(2):
        columns = slice(kind * share, (kind + 1) * share)
        other = pl.ds(pl.multiple_of((1 - vis) * share, share), share)
        sent_ref[:, columns] = slim(dot(scaled, weight_ref[kind + 1, :, other]))
    for kind in range(2):
        columns = slice(kind * share, (kind + 1) * share)
        mine = pl.ds(pl.multiple_of(vis * share, share), share)
        kept_ref[:, columns] = dot(scaled, weight_ref[kind + 1, :, mine])


def image_call(own, other, gain, weight, spots):
    rows = own.shape[0]
    share = weight.shape[2] // 2
    return pl.pallas_call(
        image_kernel,
        in_specs=[pl.BlockSpec(memory_space=pltpu.SMEM)] + [VMEM] * 4,
        out_specs=[VMEM] * 3,
        out_shape=[
            jax.ShapeDtypeStruct((rows, 2 * share), jnp.float32),
            jax.ShapeDtypeStruct((rows, 2 * share + 128), jnp.bfloat16),
            jax.ShapeDtypeStruct((rows, 128), jnp.float32),
        ],
        compiler_params=PARAMS,
        cost_estimate=LIGHT,
    )(spots, own, other, gain[None], weight)


def heads_kernel(vis_ref, rows_ref, weight_ref, *refs):
    sent_ref, kept_ref, token_ref = refs[-3:]
    kinds, _, inner = weight_ref.shape
    share = inner // 2
    vis = vis_ref[0]
    token_ref[...] = jnp.zeros(TOKEN, jnp.float32)
    for which, out_ref in ((1 - vis, sent_ref), (vis, kept_ref)):
        for kind in range(kinds):
            heads = pl.ds(pl.multiple_of(which * share, share), share)
            term = dot(rows_ref[...], weight_ref[kind, :, heads])
            out_ref[:, kind * share : (kind + 1) * share] = term.astype(out_ref.dtype)


def heads_call(block, weight, spots, after):
    shape = (block.shape[0], weight.shape[0] * weight.shape[2] // 2)
    return pl.pallas_call(
        heads_kernel,
        in_specs=[pl.BlockSpec(memory_space=pltpu.SMEM), VMEM, VMEM] + [HBM] * len(after),
        out_specs=[VMEM, VMEM, VMEM],
        out_shape=[
            jax.ShapeDtypeStruct(shape, jnp.bfloat16),
            jax.ShapeDtypeStruct(shape, jnp.float32),
            jax.ShapeDtypeStruct(TOKEN, jnp.float32),
        ],
        compiler_params=PARAMS,
        cost_estimate=LIGHT,
    )(spots, block, weight, *after)


def add_kernel(count, *refs):
    out_ref, token_ref = refs[-2:]
    rows = out_ref.shape[0]
    step = tile_of(rows, 32)

    def body(at, carry):
        part = pl.ds(pl.multiple_of(at * step, step), step)
        total = wide(refs[0][part])
        for ref in refs[1:count]:
            total = total + wide(ref[part])
        out_ref[part] = slim(total)
        return carry

    lax.fori_loop(0, rows // step, body, 0)
    token_ref[...] = jnp.zeros(TOKEN, jnp.float32)


def add_call(values, after):
    return pl.pallas_call(
        functools.partial(add_kernel, len(values)),
        in_specs=[VMEM] * len(values) + [HBM] * len(after),
        out_specs=[VMEM, VMEM],
        out_shape=[
            jax.ShapeDtypeStruct(values[0].shape, jnp.bfloat16),
            jax.ShapeDtypeStruct(TOKEN, jnp.float32),
        ],
        compiler_params=PARAMS,
        cost_estimate=LIGHT,
    )(*values, *after)


def message_kernel(lengths_ref, kept_ref, other_ref, *refs):
    out_ref = refs[-1]
    rows, columns = kept_ref.shape
    out_ref[:, :columns] = slim(kept_ref[...] + wide(other_ref[...]))
    row = lax.broadcasted_iota(jnp.int32, (rows, 128), 0)
    live = jnp.zeros((rows, 128), jnp.float32)
    for cand in range(rows // CAP):
        inside = (row >= cand * CAP) & (row < cand * CAP + lengths_ref[cand])
        live = jnp.where(inside, 1.0, live)
    out_ref[:, columns:] = slim(live)


def message_call(lengths, kept, other, after):
    rows, columns = kept.shape
    return pl.pallas_call(
        message_kernel,
        in_specs=[SMEM, VMEM, VMEM] + [HBM] * len(after),
        out_specs=VMEM,
        out_shape=jax.ShapeDtypeStruct((rows, columns + 128), jnp.bfloat16),
        compiler_params=PARAMS,
        cost_estimate=LIGHT,
    )(lengths, kept, other, *after)


def stack_kernel(count, *refs):
    out_ref = refs[-1]
    rows = refs[0].shape[0]
    for at in range(count):
        out_ref[at * rows : (at + 1) * rows] = refs[at][...]


def stack_call(values):
    rows, columns = values[0].shape
    return pl.pallas_call(
        functools.partial(stack_kernel, len(values)),
        in_specs=[VMEM] * len(values),
        out_specs=VMEM,
        out_shape=jax.ShapeDtypeStruct((rows * len(values), columns), values[0].dtype),
        compiler_params=PARAMS,
        cost_estimate=LIGHT,
    )(*values)


def span_of(counts_ref, group, images):
    first, end = jnp.int32(0), jnp.int32(0)
    for image in range(images):
        first = first + jnp.where(image < group, counts_ref[image], 0)
        end = end + jnp.where(image <= group, counts_ref[image], 0)
    return first, end


def row_ids(index, place, core, places, word_rows, sign):
    step = index // word_rows
    at = lax.rem(place + sign * step + places, places)
    return (at * 2 + core) * word_rows + lax.rem(index, word_rows)


def near_kernel(places, spots_ref, counts_ref, own_ref, other_ref, *refs):
    out_ref, token_ref = refs[-2:]
    near_rows = out_ref.shape[0]
    rows = own_ref.shape[0]
    place, core, group = spots_ref[1], spots_ref[2], spots_ref[4]
    first, _ = span_of(counts_ref, group, counts_ref.shape[0])
    near_id = first * CAP + lax.broadcasted_iota(jnp.int32, (near_rows, rows), 0)
    column = lax.broadcasted_iota(jnp.int32, (near_rows, rows), 1)
    total = 0.0
    for core_at, ref in ((core, own_ref), (1 - core, other_ref)):
        pick = near_id == row_ids(column, place, core_at, places, rows // places, -1)
        total = total + dot(slim(jnp.where(pick, 1.0, 0.0)), ref[...])
    out_ref[...] = slim(total)
    token_ref[...] = jnp.zeros(TOKEN, jnp.float32)


def near_call(spots, counts, own, other, places, near_rows, after):
    return pl.pallas_call(
        functools.partial(near_kernel, places),
        in_specs=[SMEM, SMEM, VMEM, VMEM] + [HBM] * len(after),
        out_specs=[VMEM, VMEM],
        out_shape=[
            jax.ShapeDtypeStruct((near_rows, own.shape[1]), jnp.bfloat16),
            jax.ShapeDtypeStruct(TOKEN, jnp.float32),
        ],
        compiler_params=PARAMS,
        cost_estimate=LIGHT,
    )(spots, counts, own, other, *after)


def across(a, b):
    return lax.dot_general(a, b, (((1,), (1,)), ((), ())), preferred_element_type=jnp.float32)


def attend_kernel(places, word_rows, width, spots_ref, counts_ref, near_ref, *refs):
    parts, outs, result_ref = refs[:6], refs[6 : 6 + places], refs[-1]
    near_rows = near_ref.shape[0]
    share = result_ref.shape[1]
    place, core, group = spots_ref[1], spots_ref[2], spots_ref[4]
    first, end = span_of(counts_ref, group, counts_ref.shape[0])
    sources = []
    for kept_ref, got_ref, power_ref in (parts[:3], parts[3:]):
        power = power_ref[:, :1] + jnp.sum(
            wide(got_ref[:, 2 * share : 2 * share + 128]), axis=1, keepdims=True
        )
        scale = lax.rsqrt(power / width + EPSILON)
        total = slim((kept_ref[...] + wide(got_ref[:, : 2 * share])) * scale)
        sources.append((total[:, :share], total[:, share:], None))
    lane = lax.broadcasted_iota(jnp.int32, (16, 128), 1)
    pick = slim(jnp.where(lane == 0, 1.0, 0.0))
    live = across(pick, near_ref[:, 3 * share :])[:1]
    shape = (near_rows, near_rows)
    own = lax.broadcasted_iota(jnp.int32, shape, 0) // CAP == lax.broadcasted_iota(jnp.int32, shape, 1) // CAP
    allowed = own & (live > 0.5)
    sources.append((near_ref[:, share : 2 * share], near_ref[:, 2 * share : 3 * share], allowed))
    for head in range(share // DH):
        columns = slice(head * DH, (head + 1) * DH)
        query = near_ref[:, columns]
        scores = []
        for keys, _, mask in sources:
            score = across(query, keys[:, columns]) * DH ** (-0.5)
            scores.append(score if mask is None else jnp.where(mask, score, FLOOR))
        top = functools.reduce(
            jnp.maximum, [jnp.max(score, axis=1, keepdims=True) for score in scores]
        )
        total, mixed = 0.0, 0.0
        for score, (_, values, mask) in zip(scores, sources):
            weights = jnp.exp(score - top)
            if mask is not None:
                weights = jnp.where(mask, weights, 0.0)
            total = total + jnp.sum(weights, axis=1, keepdims=True)
            mixed = mixed + dot(slim(weights), values[:, columns])
        result_ref[:, columns] = slim(mixed / total)
    block = 2 * word_rows
    row = lax.broadcasted_iota(jnp.int32, (block, near_rows), 0)
    near_id = first * CAP + lax.broadcasted_iota(jnp.int32, (block, near_rows), 1)
    core_at = jnp.where(row < word_rows, core, 1 - core)
    for step, out_ref in enumerate(outs):
        home = lax.rem(place + step, places)
        ids = (home * 2 + core_at) * word_rows + lax.rem(row, word_rows)
        put = (ids == near_id) & (near_id < end * CAP)
        out_ref[...] = slim(dot(slim(jnp.where(put, 1.0, 0.0)), result_ref[...]))


def attend_call(spots, counts, near, pieces, places, word_rows, width):
    share = pieces[0].shape[1] // 2
    return pl.pallas_call(
        functools.partial(attend_kernel, places, word_rows, width),
        in_specs=[SMEM, SMEM] + [VMEM] * (1 + len(pieces)),
        out_specs=[VMEM] * places,
        out_shape=[jax.ShapeDtypeStruct((2 * word_rows, share), jnp.bfloat16)] * places,
        scratch_shapes=[pltpu.VMEM((near.shape[0], share), jnp.bfloat16)],
        compiler_params=PARAMS,
        cost_estimate=LIGHT,
    )(spots, counts, near, *pieces)


def land_kernel(*refs):
    kept_ref, given_ref = refs[-2:]
    rows = kept_ref.shape[0]
    total = wide(refs[0][...])
    for ref in refs[1:-2]:
        total = total + wide(ref[...])
    kept_ref[...] = slim(total[:rows])
    given_ref[...] = slim(total[rows:])


def land_call(values):
    rows, columns = values[0].shape
    return pl.pallas_call(
        land_kernel,
        in_specs=[VMEM] * len(values),
        out_specs=[VMEM, VMEM],
        out_shape=[jax.ShapeDtypeStruct((rows // 2, columns), jnp.bfloat16)] * 2,
        compiler_params=PARAMS,
        cost_estimate=LIGHT,
    )(*values)


def output_kernel(spots_ref, kept_ref, core_ref, vis_ref, both_ref, weight_ref, mine_ref, sent_ref):
    vis, enc = spots_ref[0], spots_ref[3]
    share = kept_ref.shape[1]
    own = slim(wide(kept_ref[...]) + wide(core_ref[...]))
    other = slim(wide(vis_ref[...]) + wide(both_ref[...]))
    slots = CAP // 2
    columns = weight_ref.shape[1]
    part = tile_of(columns, 512)
    for start in range(0, columns, part):
        span = slice(start, start + part)
        total = dot(own, weight_ref[pl.ds(pl.multiple_of(vis * share, share), share), span])
        total = total + dot(other, weight_ref[pl.ds(pl.multiple_of((1 - vis) * share, share), share), span])
        firsts = range(0, total.shape[0], CAP)
        low = jnp.concatenate([total[at : at + slots] for at in firsts])
        high = jnp.concatenate([total[at + slots : at + CAP] for at in firsts])
        mine_ref[:, span] = jnp.where(enc == 0, low, high)
        sent_ref[:, span] = slim(jnp.where(enc == 0, high, low))


def output_call(spots, pieces, weight):
    shape = (pieces[0].shape[0] // 2, weight.shape[1])
    return pl.pallas_call(
        output_kernel,
        in_specs=[SMEM] + [VMEM] * 5,
        out_specs=[VMEM, VMEM],
        out_shape=[
            jax.ShapeDtypeStruct(shape, jnp.float32),
            jax.ShapeDtypeStruct(shape, jnp.bfloat16),
        ],
        compiler_params=PARAMS,
        cost_estimate=LIGHT,
    )(spots, *pieces, weight)


def on_device(
    image_tokens,
    vision_gain,
    up_weight,
    down_weight,
    project_weight,
    encoder_gain,
    qkv_weight,
    out_weight,
    captions,
    cand_counts,
    caption_lengths,
):
    vis_count = lax.axis_size("vis")
    enc_count = lax.axis_size("enc")
    groups = lax.axis_size("grp")
    vis = lax.axis_index("vis")
    group = lax.axis_index("grp")
    rows, features = image_tokens.shape[1:]
    all_features = features * enc_count
    width = captions.shape[2] * vis_count
    pair = vis_count == 2
    part_rows = rows // vis_count

    cores = 2 if groups % 2 == 0 else 1
    places = groups // cores
    place, core = group // cores, group % cores
    core_swap = [(i, i ^ 1) for i in range(groups)]
    up_weights, down_weights = [up_weight], [down_weight]
    if cores == 2:
        up_weights.append(lax.ppermute(up_weight, "grp", core_swap))
        down_weights.append(lax.ppermute(down_weight, "grp", core_swap))
        if up_weight.shape[1] % 128:
            up_weights = [jnp.concatenate(up_weights, axis=1)]
            down_weights = [jnp.concatenate(down_weights)]

    def to_place(value, step):
        return lax.ppermute(
            value, "grp", [(i, (i + step * cores) % groups) for i in range(groups)]
        )

    def mine_of(value):
        return lax.dynamic_slice_in_dim(value, vis * part_rows, part_rows, axis=0)

    def halves_of(mine, value):
        if pair and value is None:
            return [mine, shifted(mine, "vis", 1)]
        if pair:
            return [mine, lax.dynamic_slice_in_dim(value, (1 - vis) * part_rows, part_rows, axis=0)]
        if value is None:
            value = lax.all_gather(mine, "vis", axis=0, tiled=True)
        return [value[: rows // 2], value[rows // 2 :]]

    token = []

    def gated(value):
        return value + token[0][0, 0].astype(value.dtype) if token else value

    words = wide(captions)
    word_power = summed(jnp.sum(words * words, axis=-1), "vis")
    tokens = wide(image_tokens[0])
    row_total, row_squares = summed(
        jnp.stack([jnp.sum(tokens, axis=-1), jnp.sum(tokens * tokens, axis=-1)]), "enc"
    )
    mean = row_total / all_features
    spread = row_squares / all_features - mean * mean
    normed = slim(
        (tokens - mean[:, None]) * lax.rsqrt(spread + EPSILON)[:, None] * vision_gain
    )
    my_tokens = mine_of(image_tokens[0])
    my_normed = mine_of(normed)

    inner = qkv_weight.shape[2]
    heads = inner // DH
    shares = vis_count if heads % vis_count == 0 else 1
    share = inner // shares
    fast = pair and shares == 2 and cores == 2 and enc_count == 2
    spots = jnp.stack([vis, place, core, lax.axis_index("enc"), group])
    word_normed = slim(words * lax.rsqrt(word_power / width + EPSILON)[..., None] * encoder_gain)
    all_words = joined(word_normed, "enc", 1)
    cand_local = all_words.shape[0]
    word_rows = cand_local * CAP
    flat_words = all_words.reshape(word_rows, all_words.shape[2])

    def head_weights(which):
        return lax.dynamic_slice_in_dim(qkv_weight, which * share, share, axis=2)

    def heads_of(block, weight):
        return jnp.einsum("rd,kdh->rkh", block, weight, preferred_element_type=jnp.float32)

    def head_sum(values):
        if shares == 1:
            return lax.psum(values, "vis")
        return lax.psum_scatter(values, "vis", scatter_dimension=2, tiled=True)

    arrived, blocks, pres, outs, backs = {}, {}, {}, {}, {}

    def forwarded(step):
        if step < places:
            here = passed(arrived[step], token[0]) if step > 1 else arrived[step]
            if step + 1 < places:
                arrived[step + 1] = to_place(here, 1)
            blocks[step] = halves_of(here, None)

    def up(step, *after):
        if step < places:
            pre, token[:] = (lambda got: (got[0], [got[1]]))(
                up_call(blocks[step], up_weights, [*token, *after])
            )
            if enc_count == 2:
                pres[step] = pre, shifted(pre, "enc", 1)
            else:
                pres[step] = pre, slim(lax.psum(wide(pre), "enc") - wide(pre))

    def down(step, *after):
        if step < places:
            kept, sent, next_token = down_call(*pres[step], down_weights, [*token, *after])
            token[:] = [next_token]
            if pair:
                outs[step] = kept, shifted(sent, "vis", 1)
            else:
                out = jnp.concatenate([kept, wide(sent)])
                kept = lax.psum_scatter(out, "vis", scatter_dimension=0, tiled=True)
                outs[step] = kept, jnp.zeros_like(kept, jnp.bfloat16)

    def back(step):
        if 0 < step < places:
            parts = [*outs[step], *([backs[step - 1]] if step > 1 else [])]
            total, next_token = add_call(parts, token)
            token[:] = [next_token]
            backs[step] = to_place(total, 1)

    if places > 1:
        arrived[1] = to_place(my_normed, 1)
    if fast:
        word_sent, word_kept, word_token = heads_call(
            flat_words, qkv_weight, spots, [my_normed, my_tokens]
        )
        token[:] = [word_token]
        word_other = shifted(word_sent, "vis", 1)
    else:
        word_kept = head_sum(heads_of(flat_words, qkv_weight)).reshape(word_rows, 3 * share)
        word_other = jnp.zeros_like(word_kept, jnp.bfloat16)
    forwarded(1)
    messages = []

    def hop():
        if len(messages) < places:
            messages.append(to_place(messages[-1], 1))
        return messages[-1]

    blocks[0] = halves_of(my_normed, normed)
    up(0)
    forwarded(2)
    messages.append(message_call(caption_lengths, word_kept, word_other, token))
    up(1, down_weights[-1], messages[0])
    down(0)
    forwarded(3)
    up(2, blocks[places - 1][0], hop())
    down(1)
    up(3, hop())
    down(2, hop())
    word_block = stack_call(messages)
    if cores == 2:
        word_blocks = [word_block, lax.ppermute(word_block, "grp", core_swap)]
    else:
        word_blocks = [word_block]
    back(1)
    for step in range(4, places):
        forwarded(step)
        up(step)
        down(step - 1)
    down(places - 1)
    for step in range(2, places):
        back(step)

    home = [my_tokens, *outs[0], *([backs[places - 1]] if places > 1 else [])]
    cands = groups * cand_local
    most = min(MOSTC, cands)
    if fast:
        near, near_token = near_call(
            spots, cand_counts, *word_blocks, places, most * CAP, token
        )
        my_vision, _ = add_call(home, [near_token])
        other_vision = shifted(my_vision, "vis", 1)
        pieces = []
        for block in (my_vision, other_vision):
            partial = project_call(block, project_weight)
            full = shifted(partial, "enc", 1)
            pieces.append(image_call(partial, full, encoder_gain, qkv_weight, spots))
        got = [shifted(sent, "vis", 1) for _, sent, _ in pieces]
        parts = []
        for here, there in ((0, 1), (1, 0)):
            parts += [pieces[here][0], got[there], pieces[here][2]]
        placed = attend_call(spots, cand_counts, near, parts, places, word_rows, width)
        landed = [to_place(part, step) if step else part for step, part in enumerate(placed)]
        kept, given = land_call(landed)
        across_both = [
            (v * groups + i, (1 - v) * groups + (i ^ 1)) for v in range(2) for i in range(groups)
        ]
        from_core = lax.ppermute(given, "grp", core_swap)
        from_both = lax.ppermute(given, ("vis", "grp"), across_both)
        from_vis = shifted(kept, "vis", 1)
        mine, sent = output_call(spots, [kept, from_core, from_vis, from_both], out_weight)
        words_out = (mine + wide(shifted(sent, "enc", 1))).reshape(words.shape)
        vision_rows = jnp.where(
            vis == 0,
            jnp.concatenate([my_vision, other_vision]),
            jnp.concatenate([other_vision, my_vision]),
        )
        return (vision_rows[None], slim(words + words_out))
    my_vision = slim(sum([wide(part) for part in home]))

    ends = jnp.cumsum(cand_counts)
    start = ends[group] - cand_counts[group]
    near_ids = start * CAP + jnp.arange(most * CAP, dtype=jnp.int32)
    owned = near_ids < ends[group] * CAP

    def ids_of(core_at, sign):
        steps = jnp.arange(places, dtype=jnp.int32)[:, None]
        first = ((place + sign * steps) % places * cores + core_at) * word_rows
        return (first + jnp.arange(word_rows, dtype=jnp.int32)[None]).reshape(-1)

    core_order = [core, 1 - core][:cores]
    near = 0.0
    for core_at, block in zip(core_order, word_blocks):
        pick = near_ids[:, None] == ids_of(core_at, -1)[None, :]
        near = near + dot(pick.astype(jnp.bfloat16), block)
    near = slim(near)
    place_ids = jnp.concatenate(
        [ids_of(core_at, 1).reshape(places, word_rows) for core_at in core_order], axis=1
    ).reshape(-1)
    put = slim((place_ids[:, None] == near_ids[None, :]) & owned[None, :])
    def embed(block):
        partial = dot(block, project_weight)
        if enc_count == 2:
            full = partial + wide(shifted(slim(partial), "enc", 1))
        else:
            full = lax.psum(partial, "enc")
        return slim(full * encoder_gain), jnp.sum(full * full, axis=-1)

    vision_rows = joined(my_vision, "vis", 0)
    scaled, power = embed(vision_rows)
    total = head_sum(heads_of(scaled, qkv_weight[1:]))
    power = lax.psum(power, "vis")
    image_kv = slim(total * lax.rsqrt(power / width + EPSILON)[:, None, None])

    live = near[:, 3 * share] > 0
    near = near[:, : 3 * share].reshape(most * CAP, 3, share // DH, DH)
    row_cand = jnp.arange(most * CAP, dtype=jnp.int32) // CAP
    own_allowed = (row_cand[:, None] == row_cand[None, :]) & live[None, :]
    image_kv = image_kv.reshape(rows, 2, share // DH, DH)
    query = near[:, 0]

    def scores_of(keys):
        return jnp.einsum(
            "qhd,khd->hqk", query, keys, preferred_element_type=jnp.float32
        ) * DH ** (-0.5)

    def mixed(weights, values):
        return jnp.einsum(
            "hqk,khd->hqd", slim(weights), values, preferred_element_type=jnp.float32
        )

    image_scores = scores_of(image_kv[:, 0])
    own_scores = jnp.where(own_allowed[None], scores_of(near[:, 1]), FLOOR)
    top = jnp.maximum(
        jnp.max(image_scores, axis=-1, keepdims=True), jnp.max(own_scores, axis=-1, keepdims=True)
    )
    image_weights = jnp.exp(image_scores - top)
    own_weights = jnp.where(own_allowed[None], jnp.exp(own_scores - top), 0.0)
    total = jnp.sum(image_weights, axis=-1, keepdims=True) + jnp.sum(
        own_weights, axis=-1, keepdims=True
    )
    result = (mixed(image_weights, image_kv[:, 1]) + mixed(own_weights, near[:, 2])) / total
    result = slim(result).transpose(1, 0, 2).reshape(most * CAP, share)
    spread_out = slim(dot(put, result)).reshape(places, cores * word_rows, share)
    landed = spread_out[0]
    for step in range(1, places):
        landed = landed + to_place(spread_out[step], step)
    kept = landed[:word_rows]
    attended = kept
    if cores == 2:
        given = landed[word_rows:]
        attended = kept + lax.ppermute(given, "grp", core_swap)
    if shares > 1:
        attended = lax.all_gather(attended, "vis", axis=1, tiled=True)
    partial_words = dot(attended, out_weight).reshape(cand_local, CAP, out_weight.shape[1])
    words_out = lax.psum_scatter(partial_words, "enc", scatter_dimension=1, tiled=True)
    caption_out = slim(words + words_out)
    return (vision_rows[None], caption_out)


def solution(mesh):
    return jax.shard_map(
        on_device,
        mesh=mesh,
        in_specs=(
            P("grp", None, "enc"),
            P("enc"),
            P("enc", ("vis", "grp")),
            P(("vis", "grp"), "enc"),
            P("enc", "vis"),
            P("vis"),
            P(None, "vis", "enc"),
            P("enc", "vis"),
            P("grp", "enc", "vis"),
            P(),
            P("grp"),
        ),
        out_specs=(P("grp", None, "enc"), P("grp", "enc", "vis")),
        check_vma=False,
    )
```

```python
import functools

import jax
import jax.numpy as jnp
from jax import lax
from jax.experimental import pallas as pl
from jax.experimental.pallas import tpu as pltpu
from jax.sharding import PartitionSpec as P

DH = 256
CAP = 16
MOSTC = 12


EPSILON = 1e-06
FLOOR = -1e30


def dot(a, b):
    return jnp.dot(a, b, preferred_element_type=jnp.float32)


def wide(a):
    return a.astype(jnp.float32)


def slim(a):
    return a.astype(jnp.bfloat16)


def shifted(value, axis, step):
    count = lax.axis_size(axis)
    return lax.ppermute(value, axis, [(i, (i + step) % count) for i in range(count)])


def summed(value, axis):
    if lax.axis_size(axis) != 2:
        return lax.psum(value, axis)
    return value + shifted(value, axis, 1)


def joined(value, axis, dim):
    if lax.axis_size(axis) != 2:
        return lax.all_gather(value, axis, axis=dim, tiled=True)
    other = shifted(value, axis, 1)
    first = lax.axis_index(axis) == 0
    return jnp.concatenate(
        [jnp.where(first, value, other), jnp.where(first, other, value)], axis=dim
    )


TOKEN = (8, 128)
HBM = pl.BlockSpec(memory_space=pl.ANY)
VMEM = pl.BlockSpec(memory_space=pltpu.VMEM)
SMEM = pl.BlockSpec(memory_space=pltpu.SMEM)
LIGHT = pl.CostEstimate(flops=1024, bytes_accessed=1024, transcendentals=0)
PARAMS = pltpu.CompilerParams(vmem_limit_bytes=12 * 1024 * 1024)


def tile_of(size, most):
    return most if size % most == 0 else size


def pass_kernel(value_ref, token_ref, out_ref):
    pass


def passed(value, token):
    return pl.pallas_call(
        pass_kernel,
        in_specs=[HBM, HBM],
        out_specs=HBM,
        out_shape=jax.ShapeDtypeStruct(value.shape, value.dtype),
        input_output_aliases={0: 0},
        compiler_params=PARAMS,
        cost_estimate=LIGHT,
    )(value, token)


def up_kernel(cores, mine_ref, theirs_ref, *refs):
    weights, (out_ref, token_ref, rows_ref) = refs[:cores], refs[-3:]
    half = mine_ref.shape[0]
    units = weights[0].shape[1]
    tile = tile_of(units, 768)
    rows_ref[:half] = mine_ref[...]
    rows_ref[half:] = theirs_ref[...]
    token_ref[...] = jnp.zeros(TOKEN, jnp.float32)
    for core in range(cores):
        for first in range(0, units, tile):
            out_ref[:, core * units + first : core * units + first + tile] = slim(
                dot(rows_ref[...], weights[core][:, first : first + tile])
            )


def up_call(halves, weights, after):
    cores = len(weights)
    depth, units = weights[0].shape
    rows = 2 * halves[0].shape[0]
    return pl.pallas_call(
        functools.partial(up_kernel, cores),
        in_specs=[VMEM] * (2 + cores) + [HBM] * len(after),
        out_specs=[VMEM, VMEM],
        out_shape=[
            jax.ShapeDtypeStruct((rows, cores * units), jnp.bfloat16),
            jax.ShapeDtypeStruct(TOKEN, jnp.float32),
        ],
        scratch_shapes=[pltpu.VMEM((rows, depth), jnp.bfloat16)],
        compiler_params=PARAMS,
        cost_estimate=LIGHT,
    )(*halves, *weights, *after)


def down_kernel(cores, own_ref, other_ref, *refs):
    weights, (kept_ref, sent_ref, token_ref, total_ref) = refs[:cores], refs[-6:-2]
    hidden = refs[-2:]
    units, columns = weights[0].shape
    tile = tile_of(units, 256)
    half = kept_ref.shape[0]
    part = tile_of(columns, 1536)
    token_ref[...] = jnp.zeros(TOKEN, jnp.float32)
    order = [(core, first) for core in range(cores) for first in range(0, units, tile)]

    def fill(at):
        core, first = order[at]
        columns_at = slice(core * units + first, core * units + first + tile)
        total = wide(own_ref[:, columns_at]) + wide(other_ref[:, columns_at])
        hidden[at % 2][...] = slim(0.5 * total * (1.0 + lax.erf(total * 0.5**0.5)))

    fill(0)
    for at, (core, first) in enumerate(order):
        for start in range(0, columns, part):
            term = dot(hidden[at % 2][...], weights[core][first : first + tile, start : start + part])
            if at:
                term = total_ref[:, start : start + part] + term
            if at + 1 < len(order):
                total_ref[:, start : start + part] = term
            else:
                kept_ref[:, start : start + part] = slim(term[:half])
                sent_ref[:, start : start + part] = slim(term[half:])
        if at + 1 < len(order):
            fill(at + 1)


def down_call(own, other, weights, after):
    cores = len(weights)
    units, columns = weights[0].shape
    tile = tile_of(units, 256)
    rows = own.shape[0]
    half = jax.ShapeDtypeStruct((rows // 2, columns), jnp.bfloat16)
    return pl.pallas_call(
        functools.partial(down_kernel, cores),
        in_specs=[VMEM] * (2 + cores) + [HBM] * len(after),
        out_specs=[VMEM, VMEM, VMEM],
        out_shape=[half, half, jax.ShapeDtypeStruct(TOKEN, jnp.float32)],
        scratch_shapes=[pltpu.VMEM((rows, columns), jnp.float32)]
        + [pltpu.VMEM((rows, tile), jnp.bfloat16)] * 2,
        compiler_params=PARAMS,
        cost_estimate=LIGHT,
    )(own, other, *weights, *after)


def project_kernel(rows_ref, weight_ref, *refs):
    out_ref = refs[-1]
    columns = weight_ref.shape[1]
    part = tile_of(columns, 512)
    for first in range(0, columns, part):
        out_ref[:, first : first + part] = slim(
            dot(rows_ref[...], weight_ref[:, first : first + part])
        )


def project_call(rows, weight, after):
    return pl.pallas_call(
        project_kernel,
        in_specs=[VMEM, VMEM] + [VMEM] * len(after),
        out_specs=VMEM,
        out_shape=jax.ShapeDtypeStruct((rows.shape[0], weight.shape[1]), jnp.bfloat16),
        compiler_params=PARAMS,
        cost_estimate=LIGHT,
    )(rows, weight, *after)


def image_kernel(vis_ref, own_ref, other_ref, gain_ref, weight_ref, kept_ref, sent_ref, power_ref):
    share = weight_ref.shape[2] // 2
    full = wide(own_ref[...]) + wide(other_ref[...])
    power = jnp.sum(full * full, axis=1, keepdims=True)
    scaled = slim(full * gain_ref[...])
    power_ref[...] = jnp.broadcast_to(power, power_ref.shape)
    high = slim(power)
    middle = slim(power - wide(high))
    low = slim(power - wide(high) - wide(middle))
    lane = lax.broadcasted_iota(jnp.int32, (power.shape[0], 128), 1)
    parts = jnp.where(lane == 0, wide(high), jnp.where(lane == 1, wide(middle), wide(low)))
    sent_ref[:, 2 * share :] = slim(jnp.where(lane < 3, parts, 0.0))
    vis = vis_ref[0]
    for kind in range(2):
        columns = slice(kind * share, (kind + 1) * share)
        other = pl.ds(pl.multiple_of((1 - vis) * share, share), share)
        sent_ref[:, columns] = slim(dot(scaled, weight_ref[kind + 1, :, other]))
    for kind in range(2):
        columns = slice(kind * share, (kind + 1) * share)
        mine = pl.ds(pl.multiple_of(vis * share, share), share)
        kept_ref[:, columns] = dot(scaled, weight_ref[kind + 1, :, mine])


def image_call(own, other, gain, weight, spots):
    rows = own.shape[0]
    share = weight.shape[2] // 2
    return pl.pallas_call(
        image_kernel,
        in_specs=[pl.BlockSpec(memory_space=pltpu.SMEM)] + [VMEM] * 4,
        out_specs=[VMEM] * 3,
        out_shape=[
            jax.ShapeDtypeStruct((rows, 2 * share), jnp.float32),
            jax.ShapeDtypeStruct((rows, 2 * share + 128), jnp.bfloat16),
            jax.ShapeDtypeStruct((rows, 128), jnp.float32),
        ],
        compiler_params=PARAMS,
        cost_estimate=LIGHT,
    )(spots, own, other, gain[None], weight)


def heads_kernel(vis_ref, rows_ref, weight_ref, *refs):
    sent_ref, kept_ref, token_ref = refs[-3:]
    kinds, _, inner = weight_ref.shape
    share = inner // 2
    vis = vis_ref[0]
    token_ref[...] = jnp.zeros(TOKEN, jnp.float32)
    for which, out_ref in ((1 - vis, sent_ref), (vis, kept_ref)):
        for kind in range(kinds):
            heads = pl.ds(pl.multiple_of(which * share, share), share)
            term = dot(rows_ref[...], weight_ref[kind, :, heads])
            out_ref[:, kind * share : (kind + 1) * share] = term.astype(out_ref.dtype)


def heads_call(block, weight, spots, after):
    shape = (block.shape[0], weight.shape[0] * weight.shape[2] // 2)
    return pl.pallas_call(
        heads_kernel,
        in_specs=[pl.BlockSpec(memory_space=pltpu.SMEM), VMEM, VMEM] + [HBM] * len(after),
        out_specs=[VMEM, VMEM, VMEM],
        out_shape=[
            jax.ShapeDtypeStruct(shape, jnp.bfloat16),
            jax.ShapeDtypeStruct(shape, jnp.float32),
            jax.ShapeDtypeStruct(TOKEN, jnp.float32),
        ],
        compiler_params=PARAMS,
        cost_estimate=LIGHT,
    )(spots, block, weight, *after)


def add_kernel(count, *refs):
    out_ref, token_ref = refs[-2:]
    rows = out_ref.shape[0]
    step = tile_of(rows, 32)

    def body(at, carry):
        part = pl.ds(pl.multiple_of(at * step, step), step)
        total = wide(refs[0][part])
        for ref in refs[1:count]:
            total = total + wide(ref[part])
        out_ref[part] = slim(total)
        return carry

    lax.fori_loop(0, rows // step, body, 0)
    token_ref[...] = jnp.zeros(TOKEN, jnp.float32)


def add_call(values, after):
    return pl.pallas_call(
        functools.partial(add_kernel, len(values)),
        in_specs=[VMEM] * len(values) + [HBM] * len(after),
        out_specs=[VMEM, VMEM],
        out_shape=[
            jax.ShapeDtypeStruct(values[0].shape, jnp.bfloat16),
            jax.ShapeDtypeStruct(TOKEN, jnp.float32),
        ],
        compiler_params=PARAMS,
        cost_estimate=LIGHT,
    )(*values, *after)


def message_kernel(lengths_ref, kept_ref, other_ref, *refs):
    out_ref = refs[-1]
    rows, columns = kept_ref.shape
    out_ref[:, :columns] = slim(kept_ref[...] + wide(other_ref[...]))
    row = lax.broadcasted_iota(jnp.int32, (rows, 128), 0)
    live = jnp.zeros((rows, 128), jnp.float32)
    for cand in range(rows // CAP):
        inside = (row >= cand * CAP) & (row < cand * CAP + lengths_ref[cand])
        live = jnp.where(inside, 1.0, live)
    out_ref[:, columns:] = slim(live)


def message_call(lengths, kept, other, after):
    rows, columns = kept.shape
    return pl.pallas_call(
        message_kernel,
        in_specs=[SMEM, VMEM, VMEM] + [HBM] * len(after),
        out_specs=VMEM,
        out_shape=jax.ShapeDtypeStruct((rows, columns + 128), jnp.bfloat16),
        compiler_params=PARAMS,
        cost_estimate=LIGHT,
    )(lengths, kept, other, *after)


def stack_kernel(count, *refs):
    out_ref = refs[-1]
    rows = refs[0].shape[0]
    for at in range(count):
        out_ref[at * rows : (at + 1) * rows] = refs[at][...]


def stack_call(values):
    rows, columns = values[0].shape
    return pl.pallas_call(
        functools.partial(stack_kernel, len(values)),
        in_specs=[VMEM] * len(values),
        out_specs=VMEM,
        out_shape=jax.ShapeDtypeStruct((rows * len(values), columns), values[0].dtype),
        compiler_params=PARAMS,
        cost_estimate=LIGHT,
    )(*values)


def span_of(counts_ref, group, images):
    first, end = jnp.int32(0), jnp.int32(0)
    for image in range(images):
        first = first + jnp.where(image < group, counts_ref[image], 0)
        end = end + jnp.where(image <= group, counts_ref[image], 0)
    return first, end


def row_ids(index, place, core, places, word_rows, sign):
    step = index // word_rows
    at = lax.rem(place + sign * step + places, places)
    return (at * 2 + core) * word_rows + lax.rem(index, word_rows)


def near_kernel(places, spots_ref, counts_ref, own_ref, other_ref, *refs):
    out_ref, token_ref = refs[-2:]
    near_rows = out_ref.shape[0]
    rows = own_ref.shape[0]
    place, core, group = spots_ref[1], spots_ref[2], spots_ref[4]
    first, _ = span_of(counts_ref, group, counts_ref.shape[0])
    near_id = first * CAP + lax.broadcasted_iota(jnp.int32, (near_rows, rows), 0)
    column = lax.broadcasted_iota(jnp.int32, (near_rows, rows), 1)
    total = 0.0
    for core_at, ref in ((core, own_ref), (1 - core, other_ref)):
        pick = near_id == row_ids(column, place, core_at, places, rows // places, -1)
        total = total + dot(slim(jnp.where(pick, 1.0, 0.0)), ref[...])
    out_ref[...] = slim(total)
    token_ref[...] = jnp.zeros(TOKEN, jnp.float32)


def near_call(spots, counts, own, other, places, near_rows, after):
    return pl.pallas_call(
        functools.partial(near_kernel, places),
        in_specs=[SMEM, SMEM, VMEM, VMEM] + [HBM] * len(after),
        out_specs=[VMEM, VMEM],
        out_shape=[
            jax.ShapeDtypeStruct((near_rows, own.shape[1]), jnp.bfloat16),
            jax.ShapeDtypeStruct(TOKEN, jnp.float32),
        ],
        compiler_params=PARAMS,
        cost_estimate=LIGHT,
    )(spots, counts, own, other, *after)


def across(a, b):
    return lax.dot_general(a, b, (((1,), (1,)), ((), ())), preferred_element_type=jnp.float32)


def attend_kernel(places, word_rows, width, spots_ref, counts_ref, near_ref, *refs):
    parts, outs, result_ref = refs[:6], refs[6 : 6 + places], refs[-1]
    near_rows = near_ref.shape[0]
    share = result_ref.shape[1]
    place, core, group = spots_ref[1], spots_ref[2], spots_ref[4]
    first, end = span_of(counts_ref, group, counts_ref.shape[0])
    sources = []
    for kept_ref, got_ref, power_ref in (parts[:3], parts[3:]):
        power = power_ref[:, :1] + jnp.sum(
            wide(got_ref[:, 2 * share : 2 * share + 128]), axis=1, keepdims=True
        )
        scale = lax.rsqrt(power / width + EPSILON)
        total = slim((kept_ref[...] + wide(got_ref[:, : 2 * share])) * scale)
        sources.append((total[:, :share], total[:, share:], None))
    lane = lax.broadcasted_iota(jnp.int32, (16, 128), 1)
    pick = slim(jnp.where(lane == 0, 1.0, 0.0))
    live = across(pick, near_ref[:, 3 * share :])[:1]
    shape = (near_rows, near_rows)
    own = lax.broadcasted_iota(jnp.int32, shape, 0) // CAP == lax.broadcasted_iota(jnp.int32, shape, 1) // CAP
    allowed = own & (live > 0.5)
    sources.append((near_ref[:, share : 2 * share], near_ref[:, 2 * share : 3 * share], allowed))
    for head in range(share // DH):
        columns = slice(head * DH, (head + 1) * DH)
        query = near_ref[:, columns]
        scores = []
        for keys, _, mask in sources:
            score = across(query, keys[:, columns]) * DH ** (-0.5)
            scores.append(score if mask is None else jnp.where(mask, score, FLOOR))
        top = functools.reduce(
            jnp.maximum, [jnp.max(score, axis=1, keepdims=True) for score in scores]
        )
        total, mixed = 0.0, 0.0
        for score, (_, values, mask) in zip(scores, sources):
            weights = jnp.exp(score - top)
            if mask is not None:
                weights = jnp.where(mask, weights, 0.0)
            total = total + jnp.sum(weights, axis=1, keepdims=True)
            mixed = mixed + dot(slim(weights), values[:, columns])
        result_ref[:, columns] = slim(mixed / total)
    block = 2 * word_rows
    row = lax.broadcasted_iota(jnp.int32, (block, near_rows), 0)
    near_id = first * CAP + lax.broadcasted_iota(jnp.int32, (block, near_rows), 1)
    core_at = jnp.where(row < word_rows, core, 1 - core)
    for step, out_ref in enumerate(outs):
        home = lax.rem(place + step, places)
        ids = (home * 2 + core_at) * word_rows + lax.rem(row, word_rows)
        put = (ids == near_id) & (near_id < end * CAP)
        out_ref[...] = slim(dot(slim(jnp.where(put, 1.0, 0.0)), result_ref[...]))


def attend_call(spots, counts, near, pieces, places, word_rows, width):
    share = pieces[0].shape[1] // 2
    return pl.pallas_call(
        functools.partial(attend_kernel, places, word_rows, width),
        in_specs=[SMEM, SMEM] + [VMEM] * (1 + len(pieces)),
        out_specs=[VMEM] * places,
        out_shape=[jax.ShapeDtypeStruct((2 * word_rows, share), jnp.bfloat16)] * places,
        scratch_shapes=[pltpu.VMEM((near.shape[0], share), jnp.bfloat16)],
        compiler_params=PARAMS,
        cost_estimate=LIGHT,
    )(spots, counts, near, *pieces)


def land_kernel(*refs):
    kept_ref, given_ref = refs[-2:]
    rows = kept_ref.shape[0]
    total = wide(refs[0][...])
    for ref in refs[1:-2]:
        total = total + wide(ref[...])
    kept_ref[...] = slim(total[:rows])
    given_ref[...] = slim(total[rows:])


def land_call(values):
    rows, columns = values[0].shape
    return pl.pallas_call(
        land_kernel,
        in_specs=[VMEM] * len(values),
        out_specs=[VMEM, VMEM],
        out_shape=[jax.ShapeDtypeStruct((rows // 2, columns), jnp.bfloat16)] * 2,
        compiler_params=PARAMS,
        cost_estimate=LIGHT,
    )(*values)


def output_kernel(spots_ref, kept_ref, core_ref, vis_ref, both_ref, weight_ref, mine_ref, sent_ref):
    vis, enc = spots_ref[0], spots_ref[3]
    share = kept_ref.shape[1]
    own = slim(wide(kept_ref[...]) + wide(core_ref[...]))
    other = slim(wide(vis_ref[...]) + wide(both_ref[...]))
    slots = CAP // 2
    columns = weight_ref.shape[1]
    part = tile_of(columns, 512)
    for start in range(0, columns, part):
        span = slice(start, start + part)
        total = dot(own, weight_ref[pl.ds(pl.multiple_of(vis * share, share), share), span])
        total = total + dot(other, weight_ref[pl.ds(pl.multiple_of((1 - vis) * share, share), share), span])
        firsts = range(0, total.shape[0], CAP)
        low = jnp.concatenate([total[at : at + slots] for at in firsts])
        high = jnp.concatenate([total[at + slots : at + CAP] for at in firsts])
        mine_ref[:, span] = jnp.where(enc == 0, low, high)
        sent_ref[:, span] = slim(jnp.where(enc == 0, high, low))


def output_call(spots, pieces, weight):
    shape = (pieces[0].shape[0] // 2, weight.shape[1])
    return pl.pallas_call(
        output_kernel,
        in_specs=[SMEM] + [VMEM] * 5,
        out_specs=[VMEM, VMEM],
        out_shape=[
            jax.ShapeDtypeStruct(shape, jnp.float32),
            jax.ShapeDtypeStruct(shape, jnp.bfloat16),
        ],
        compiler_params=PARAMS,
        cost_estimate=LIGHT,
    )(spots, *pieces, weight)


def on_device(
    image_tokens,
    vision_gain,
    up_weight,
    down_weight,
    project_weight,
    encoder_gain,
    qkv_weight,
    out_weight,
    captions,
    cand_counts,
    caption_lengths,
):
    vis_count = lax.axis_size("vis")
    enc_count = lax.axis_size("enc")
    groups = lax.axis_size("grp")
    vis = lax.axis_index("vis")
    group = lax.axis_index("grp")
    rows, features = image_tokens.shape[1:]
    all_features = features * enc_count
    width = captions.shape[2] * vis_count
    pair = vis_count == 2
    part_rows = rows // vis_count

    cores = 2 if groups % 2 == 0 else 1
    places = groups // cores
    place, core = group // cores, group % cores
    core_swap = [(i, i ^ 1) for i in range(groups)]
    up_weights, down_weights = [up_weight], [down_weight]
    if cores == 2:
        up_weights.append(lax.ppermute(up_weight, "grp", core_swap))
        down_weights.append(lax.ppermute(down_weight, "grp", core_swap))
        if up_weight.shape[1] % 128:
            up_weights = [jnp.concatenate(up_weights, axis=1)]
            down_weights = [jnp.concatenate(down_weights)]

    def to_place(value, step):
        return lax.ppermute(
            value, "grp", [(i, (i + step * cores) % groups) for i in range(groups)]
        )

    def mine_of(value):
        return lax.dynamic_slice_in_dim(value, vis * part_rows, part_rows, axis=0)

    def halves_of(mine, value):
        if pair and value is None:
            return [mine, shifted(mine, "vis", 1)]
        if pair:
            return [mine, lax.dynamic_slice_in_dim(value, (1 - vis) * part_rows, part_rows, axis=0)]
        if value is None:
            value = lax.all_gather(mine, "vis", axis=0, tiled=True)
        return [value[: rows // 2], value[rows // 2 :]]

    token = []

    def gated(value):
        return value + token[0][0, 0].astype(value.dtype) if token else value

    words = wide(captions)
    word_power = summed(jnp.sum(words * words, axis=-1), "vis")
    tokens = wide(image_tokens[0])
    row_total, row_squares = summed(
        jnp.stack([jnp.sum(tokens, axis=-1), jnp.sum(tokens * tokens, axis=-1)]), "enc"
    )
    mean = row_total / all_features
    spread = row_squares / all_features - mean * mean
    normed = slim(
        (tokens - mean[:, None]) * lax.rsqrt(spread + EPSILON)[:, None] * vision_gain
    )
    my_tokens = mine_of(image_tokens[0])
    my_normed = mine_of(normed)

    inner = qkv_weight.shape[2]
    heads = inner // DH
    shares = vis_count if heads % vis_count == 0 else 1
    share = inner // shares
    fast = pair and shares == 2 and cores == 2 and enc_count == 2
    spots = jnp.stack([vis, place, core, lax.axis_index("enc"), group])
    word_normed = slim(words * lax.rsqrt(word_power / width + EPSILON)[..., None] * encoder_gain)
    all_words = joined(word_normed, "enc", 1)
    cand_local = all_words.shape[0]
    word_rows = cand_local * CAP
    flat_words = all_words.reshape(word_rows, all_words.shape[2])

    def head_weights(which):
        return lax.dynamic_slice_in_dim(qkv_weight, which * share, share, axis=2)

    def heads_of(block, weight):
        return jnp.einsum("rd,kdh->rkh", block, weight, preferred_element_type=jnp.float32)

    def head_sum(values):
        if shares == 1:
            return lax.psum(values, "vis")
        return lax.psum_scatter(values, "vis", scatter_dimension=2, tiled=True)

    arrived, blocks, pres, outs, backs = {}, {}, {}, {}, {}

    def forwarded(step):
        if step < places:
            here = passed(arrived[step], token[0]) if step > 1 and token else arrived[step]
            if step + 1 < places:
                arrived[step + 1] = to_place(here, 1)
            blocks[step] = halves_of(here, None)

    def up(step, *after):
        if step < places:
            pre, token[:] = (lambda got: (got[0], [got[1]]))(
                up_call(blocks[step], up_weights, [*token, *after])
            )
            if enc_count == 2:
                pres[step] = pre, shifted(pre, "enc", 1)
            else:
                pres[step] = pre, slim(lax.psum(wide(pre), "enc") - wide(pre))

    def down(step, *after):
        if step < places:
            kept, sent, next_token = down_call(*pres[step], down_weights, [*token, *after])
            token[:] = [next_token]
            if pair:
                outs[step] = kept, shifted(sent, "vis", 1)
            else:
                out = jnp.concatenate([kept, wide(sent)])
                kept = lax.psum_scatter(out, "vis", scatter_dimension=0, tiled=True)
                outs[step] = kept, jnp.zeros_like(kept, jnp.bfloat16)

    def back(step):
        if 0 < step < places:
            parts = [*outs[step], *([backs[step - 1]] if step > 1 else [])]
            total, next_token = add_call(parts, token)
            token[:] = [next_token]
            backs[step] = to_place(total, 1)

    if places > 1:
        arrived[1] = to_place(my_normed, 1)
    if fast:
        word_sent, word_kept, word_token = heads_call(
            flat_words, qkv_weight, spots, [my_normed, my_tokens]
        )
        token[:] = [word_token]
        word_other = shifted(word_sent, "vis", 1)
    else:
        word_kept = head_sum(heads_of(flat_words, qkv_weight)).reshape(word_rows, 3 * share)
        word_other = jnp.zeros_like(word_kept, jnp.bfloat16)
    forwarded(1)
    messages = []

    def hop():
        if len(messages) < places:
            messages.append(to_place(messages[-1], 1))
        return messages[-1]

    blocks[0] = halves_of(my_normed, normed)
    up(0)
    forwarded(2)
    messages.append(message_call(caption_lengths, word_kept, word_other, token))
    up(1, down_weights[-1], messages[0])
    forwarded(3)
    up(2, blocks[places - 1][0], hop())
    down(1, hop())
    down(0)
    up(3)
    down(2, hop())
    back(1)
    word_block = stack_call(messages)
    if cores == 2:
        word_blocks = [word_block, lax.ppermute(word_block, "grp", core_swap)]
    else:
        word_blocks = [word_block]
    for step in range(4, places):
        forwarded(step)
        up(step)
        down(step - 1)
    down(places - 1)
    for step in range(2, places):
        back(step)

    home = [my_tokens, *outs[0], *([backs[places - 1]] if places > 1 else [])]
    cands = groups * cand_local
    most = min(MOSTC, cands)
    if fast:
        near, near_token = near_call(
            spots, cand_counts, *word_blocks, places, most * CAP, token
        )
        my_vision, _ = add_call(home, [near_token])
        other_vision = shifted(my_vision, "vis", 1)
        pieces = []
        for block in (my_vision, other_vision):
            partial = project_call(block, project_weight, [out_weight])
            full = shifted(partial, "enc", 1)
            pieces.append(image_call(partial, full, encoder_gain, qkv_weight, spots))
        got = [shifted(sent, "vis", 1) for _, sent, _ in pieces]
        parts = []
        for here, there in ((0, 1), (1, 0)):
            parts += [pieces[here][0], got[there], pieces[here][2]]
        placed = attend_call(spots, cand_counts, near, parts, places, word_rows, width)
        landed = [to_place(part, step) if step else part for step, part in enumerate(placed)]
        kept, given = land_call(landed)
        across_both = [
            (v * groups + i, (1 - v) * groups + (i ^ 1)) for v in range(2) for i in range(groups)
        ]
        from_core = lax.ppermute(given, "grp", core_swap)
        from_both = lax.ppermute(given, ("vis", "grp"), across_both)
        from_vis = shifted(kept, "vis", 1)
        mine, sent = output_call(spots, [kept, from_core, from_vis, from_both], out_weight)
        words_out = (mine + wide(shifted(sent, "enc", 1))).reshape(words.shape)
        vision_rows = jnp.where(
            vis == 0,
            jnp.concatenate([my_vision, other_vision]),
            jnp.concatenate([other_vision, my_vision]),
        )
        return (vision_rows[None], slim(words + words_out))
    my_vision = slim(sum([wide(part) for part in home]))

    ends = jnp.cumsum(cand_counts)
    start = ends[group] - cand_counts[group]
    near_ids = start * CAP + jnp.arange(most * CAP, dtype=jnp.int32)
    owned = near_ids < ends[group] * CAP

    def ids_of(core_at, sign):
        steps = jnp.arange(places, dtype=jnp.int32)[:, None]
        first = ((place + sign * steps) % places * cores + core_at) * word_rows
        return (first + jnp.arange(word_rows, dtype=jnp.int32)[None]).reshape(-1)

    core_order = [core, 1 - core][:cores]
    near = 0.0
    for core_at, block in zip(core_order, word_blocks):
        pick = near_ids[:, None] == ids_of(core_at, -1)[None, :]
        near = near + dot(pick.astype(jnp.bfloat16), block)
    near = slim(near)
    place_ids = jnp.concatenate(
        [ids_of(core_at, 1).reshape(places, word_rows) for core_at in core_order], axis=1
    ).reshape(-1)
    put = slim((place_ids[:, None] == near_ids[None, :]) & owned[None, :])
    def embed(block):
        partial = dot(block, project_weight)
        if enc_count == 2:
            full = partial + wide(shifted(slim(partial), "enc", 1))
        else:
            full = lax.psum(partial, "enc")
        return slim(full * encoder_gain), jnp.sum(full * full, axis=-1)

    vision_rows = joined(my_vision, "vis", 0)
    scaled, power = embed(vision_rows)
    total = head_sum(heads_of(scaled, qkv_weight[1:]))
    power = lax.psum(power, "vis")
    image_kv = slim(total * lax.rsqrt(power / width + EPSILON)[:, None, None])

    live = near[:, 3 * share] > 0
    near = near[:, : 3 * share].reshape(most * CAP, 3, share // DH, DH)
    row_cand = jnp.arange(most * CAP, dtype=jnp.int32) // CAP
    own_allowed = (row_cand[:, None] == row_cand[None, :]) & live[None, :]
    image_kv = image_kv.reshape(rows, 2, share // DH, DH)
    query = near[:, 0]

    def scores_of(keys):
        return jnp.einsum(
            "qhd,khd->hqk", query, keys, preferred_element_type=jnp.float32
        ) * DH ** (-0.5)

    def mixed(weights, values):
        return jnp.einsum(
            "hqk,khd->hqd", slim(weights), values, preferred_element_type=jnp.float32
        )

    image_scores = scores_of(image_kv[:, 0])
    own_scores = jnp.where(own_allowed[None], scores_of(near[:, 1]), FLOOR)
    top = jnp.maximum(
        jnp.max(image_scores, axis=-1, keepdims=True), jnp.max(own_scores, axis=-1, keepdims=True)
    )
    image_weights = jnp.exp(image_scores - top)
    own_weights = jnp.where(own_allowed[None], jnp.exp(own_scores - top), 0.0)
    total = jnp.sum(image_weights, axis=-1, keepdims=True) + jnp.sum(
        own_weights, axis=-1, keepdims=True
    )
    result = (mixed(image_weights, image_kv[:, 1]) + mixed(own_weights, near[:, 2])) / total
    result = slim(result).transpose(1, 0, 2).reshape(most * CAP, share)
    spread_out = slim(dot(put, result)).reshape(places, cores * word_rows, share)
    landed = spread_out[0]
    for step in range(1, places):
        landed = landed + to_place(spread_out[step], step)
    kept = landed[:word_rows]
    attended = kept
    if cores == 2:
        given = landed[word_rows:]
        attended = kept + lax.ppermute(given, "grp", core_swap)
    if shares > 1:
        attended = lax.all_gather(attended, "vis", axis=1, tiled=True)
    partial_words = dot(attended, out_weight).reshape(cand_local, CAP, out_weight.shape[1])
    words_out = lax.psum_scatter(partial_words, "enc", scatter_dimension=1, tiled=True)
    caption_out = slim(words + words_out)
    return (vision_rows[None], caption_out)


def solution(mesh):
    return jax.shard_map(
        on_device,
        mesh=mesh,
        in_specs=(
            P("grp", None, "enc"),
            P("enc"),
            P("enc", ("vis", "grp")),
            P(("vis", "grp"), "enc"),
            P("enc", "vis"),
            P("vis"),
            P(None, "vis", "enc"),
            P("enc", "vis"),
            P("grp", "enc", "vis"),
            P(),
            P("grp"),
        ),
        out_specs=(P("grp", None, "enc"), P("grp", "enc", "vis")),
        check_vma=False,
    )
```

```python
import functools

import jax
import jax.numpy as jnp
from jax import lax
from jax.experimental import pallas as pl
from jax.experimental.pallas import tpu as pltpu
from jax.sharding import PartitionSpec as P

DH = 256
CAP = 16
MOSTC = 12


EPSILON = 1e-06
FLOOR = -1e30


def dot(a, b):
    return jnp.dot(a, b, preferred_element_type=jnp.float32)


def wide(a):
    return a.astype(jnp.float32)


def slim(a):
    return a.astype(jnp.bfloat16)


def shifted(value, axis, step):
    count = lax.axis_size(axis)
    return lax.ppermute(value, axis, [(i, (i + step) % count) for i in range(count)])


def summed(value, axis):
    if lax.axis_size(axis) != 2:
        return lax.psum(value, axis)
    return value + shifted(value, axis, 1)


def joined(value, axis, dim):
    if lax.axis_size(axis) != 2:
        return lax.all_gather(value, axis, axis=dim, tiled=True)
    other = shifted(value, axis, 1)
    first = lax.axis_index(axis) == 0
    return jnp.concatenate(
        [jnp.where(first, value, other), jnp.where(first, other, value)], axis=dim
    )


TOKEN = (8, 128)
HBM = pl.BlockSpec(memory_space=pl.ANY)
VMEM = pl.BlockSpec(memory_space=pltpu.VMEM)
SMEM = pl.BlockSpec(memory_space=pltpu.SMEM)
LIGHT = pl.CostEstimate(flops=1024, bytes_accessed=1024, transcendentals=0)
PARAMS = pltpu.CompilerParams(vmem_limit_bytes=12 * 1024 * 1024)


def tile_of(size, most):
    return most if size % most == 0 else size


def pass_kernel(value_ref, token_ref, out_ref):
    pass


def passed(value, token):
    return pl.pallas_call(
        pass_kernel,
        in_specs=[HBM, HBM],
        out_specs=HBM,
        out_shape=jax.ShapeDtypeStruct(value.shape, value.dtype),
        input_output_aliases={0: 0},
        compiler_params=PARAMS,
        cost_estimate=LIGHT,
    )(value, token)


def hold_kernel(value_ref, *refs):
    out_ref, sem = refs[-2:]
    copy = pltpu.make_async_copy(value_ref, out_ref, sem)
    copy.start()
    copy.wait()


def held_call(value, after):
    return pl.pallas_call(
        hold_kernel,
        in_specs=[HBM] * (1 + len(after)),
        out_specs=VMEM,
        out_shape=jax.ShapeDtypeStruct(value.shape, value.dtype),
        scratch_shapes=[pltpu.SemaphoreType.DMA],
        compiler_params=PARAMS,
        cost_estimate=LIGHT,
    )(value, *after)


def up_kernel(cores, mine_ref, theirs_ref, *refs):
    weights, (out_ref, token_ref, rows_ref) = refs[:cores], refs[-3:]
    half = mine_ref.shape[0]
    units = weights[0].shape[1]
    tile = tile_of(units, 256)
    rows_ref[:half] = mine_ref[...]
    rows_ref[half:] = theirs_ref[...]
    token_ref[...] = jnp.zeros(TOKEN, jnp.float32)
    for core in range(cores):
        for first in range(0, units, tile):
            out_ref[:, core * units + first : core * units + first + tile] = slim(
                dot(rows_ref[...], weights[core][:, first : first + tile])
            )


def up_call(halves, weights, after):
    cores = len(weights)
    depth, units = weights[0].shape
    rows = 2 * halves[0].shape[0]
    return pl.pallas_call(
        functools.partial(up_kernel, cores),
        in_specs=[VMEM] * (2 + cores) + [HBM] * len(after),
        out_specs=[VMEM, VMEM],
        out_shape=[
            jax.ShapeDtypeStruct((rows, cores * units), jnp.bfloat16),
            jax.ShapeDtypeStruct(TOKEN, jnp.float32),
        ],
        scratch_shapes=[pltpu.VMEM((rows, depth), jnp.bfloat16)],
        compiler_params=PARAMS,
        cost_estimate=LIGHT,
    )(*halves, *weights, *after)


def down_kernel(cores, own_ref, other_ref, *refs):
    weights, (kept_ref, sent_ref, token_ref, total_ref) = refs[:cores], refs[-6:-2]
    hidden = refs[-2:]
    units, columns = weights[0].shape
    tile = tile_of(units, 256)
    half = kept_ref.shape[0]
    part = tile_of(columns, 1536)
    token_ref[...] = jnp.zeros(TOKEN, jnp.float32)
    order = [(core, first) for core in range(cores) for first in range(0, units, tile)]

    def fill(at):
        core, first = order[at]
        columns_at = slice(core * units + first, core * units + first + tile)
        total = wide(own_ref[:, columns_at]) + wide(other_ref[:, columns_at])
        hidden[at % 2][...] = slim(0.5 * total * (1.0 + lax.erf(total * 0.5**0.5)))

    fill(0)
    for at, (core, first) in enumerate(order):
        for start in range(0, columns, part):
            term = dot(hidden[at % 2][...], weights[core][first : first + tile, start : start + part])
            if at:
                term = total_ref[:, start : start + part] + term
            if at + 1 < len(order):
                total_ref[:, start : start + part] = term
            else:
                kept_ref[:, start : start + part] = slim(term[:half])
                sent_ref[:, start : start + part] = slim(term[half:])
        if at + 1 < len(order):
            fill(at + 1)


def down_call(own, other, weights, after):
    cores = len(weights)
    units, columns = weights[0].shape
    tile = tile_of(units, 256)
    rows = own.shape[0]
    half = jax.ShapeDtypeStruct((rows // 2, columns), jnp.bfloat16)
    return pl.pallas_call(
        functools.partial(down_kernel, cores),
        in_specs=[VMEM] * (2 + cores) + [HBM] * len(after),
        out_specs=[VMEM, VMEM, VMEM],
        out_shape=[half, half, jax.ShapeDtypeStruct(TOKEN, jnp.float32)],
        scratch_shapes=[pltpu.VMEM((rows, columns), jnp.float32)]
        + [pltpu.VMEM((rows, tile), jnp.bfloat16)] * 2,
        compiler_params=PARAMS,
        cost_estimate=LIGHT,
    )(own, other, *weights, *after)


def project_kernel(rows_ref, weight_ref, *refs):
    out_ref = refs[-1]
    columns = weight_ref.shape[1]
    part = tile_of(columns, 512)
    for first in range(0, columns, part):
        out_ref[:, first : first + part] = slim(
            dot(rows_ref[...], weight_ref[:, first : first + part])
        )


def project_call(rows, weight, after):
    return pl.pallas_call(
        project_kernel,
        in_specs=[VMEM, VMEM] + [HBM] * len(after),
        out_specs=VMEM,
        out_shape=jax.ShapeDtypeStruct((rows.shape[0], weight.shape[1]), jnp.bfloat16),
        compiler_params=PARAMS,
        cost_estimate=LIGHT,
    )(rows, weight, *after)


def image_kernel(vis_ref, own_ref, other_ref, gain_ref, weight_ref, kept_ref, sent_ref, power_ref):
    share = weight_ref.shape[2] // 2
    full = wide(own_ref[...]) + wide(other_ref[...])
    power = jnp.sum(full * full, axis=1, keepdims=True)
    scaled = slim(full * gain_ref[...])
    power_ref[...] = jnp.broadcast_to(power, power_ref.shape)
    high = slim(power)
    middle = slim(power - wide(high))
    low = slim(power - wide(high) - wide(middle))
    lane = lax.broadcasted_iota(jnp.int32, (power.shape[0], 128), 1)
    parts = jnp.where(lane == 0, wide(high), jnp.where(lane == 1, wide(middle), wide(low)))
    sent_ref[:, 2 * share :] = slim(jnp.where(lane < 3, parts, 0.0))
    vis = vis_ref[0]
    for kind in range(2):
        columns = slice(kind * share, (kind + 1) * share)
        other = pl.ds(pl.multiple_of((1 - vis) * share, share), share)
        sent_ref[:, columns] = slim(dot(scaled, weight_ref[kind + 1, :, other]))
    for kind in range(2):
        columns = slice(kind * share, (kind + 1) * share)
        mine = pl.ds(pl.multiple_of(vis * share, share), share)
        kept_ref[:, columns] = dot(scaled, weight_ref[kind + 1, :, mine])


def image_call(own, other, gain, weight, spots):
    rows = own.shape[0]
    share = weight.shape[2] // 2
    return pl.pallas_call(
        image_kernel,
        in_specs=[pl.BlockSpec(memory_space=pltpu.SMEM)] + [VMEM] * 4,
        out_specs=[VMEM] * 3,
        out_shape=[
            jax.ShapeDtypeStruct((rows, 2 * share), jnp.float32),
            jax.ShapeDtypeStruct((rows, 2 * share + 128), jnp.bfloat16),
            jax.ShapeDtypeStruct((rows, 128), jnp.float32),
        ],
        compiler_params=PARAMS,
        cost_estimate=LIGHT,
    )(spots, own, other, gain[None], weight)


def heads_kernel(vis_ref, rows_ref, weight_ref, *refs):
    sent_ref, kept_ref, token_ref = refs[-3:]
    kinds, _, inner = weight_ref.shape
    share = inner // 2
    vis = vis_ref[0]
    token_ref[...] = jnp.zeros(TOKEN, jnp.float32)
    for which, out_ref in ((1 - vis, sent_ref), (vis, kept_ref)):
        for kind in range(kinds):
            heads = pl.ds(pl.multiple_of(which * share, share), share)
            term = dot(rows_ref[...], weight_ref[kind, :, heads])
            out_ref[:, kind * share : (kind + 1) * share] = term.astype(out_ref.dtype)


def heads_call(block, weight, spots, after):
    shape = (block.shape[0], weight.shape[0] * weight.shape[2] // 2)
    return pl.pallas_call(
        heads_kernel,
        in_specs=[pl.BlockSpec(memory_space=pltpu.SMEM), VMEM, VMEM] + [HBM] * len(after),
        out_specs=[VMEM, VMEM, VMEM],
        out_shape=[
            jax.ShapeDtypeStruct(shape, jnp.bfloat16),
            jax.ShapeDtypeStruct(shape, jnp.float32),
            jax.ShapeDtypeStruct(TOKEN, jnp.float32),
        ],
        compiler_params=PARAMS,
        cost_estimate=LIGHT,
    )(spots, block, weight, *after)


def add_kernel(count, *refs):
    out_ref, token_ref = refs[-2:]
    rows = out_ref.shape[0]
    step = tile_of(rows, 32)

    def body(at, carry):
        part = pl.ds(pl.multiple_of(at * step, step), step)
        total = wide(refs[0][part])
        for ref in refs[1:count]:
            total = total + wide(ref[part])
        out_ref[part] = slim(total)
        return carry

    lax.fori_loop(0, rows // step, body, 0)
    token_ref[...] = jnp.zeros(TOKEN, jnp.float32)


def add_call(values, after):
    return pl.pallas_call(
        functools.partial(add_kernel, len(values)),
        in_specs=[VMEM] * len(values) + [HBM] * len(after),
        out_specs=[VMEM, VMEM],
        out_shape=[
            jax.ShapeDtypeStruct(values[0].shape, jnp.bfloat16),
            jax.ShapeDtypeStruct(TOKEN, jnp.float32),
        ],
        compiler_params=PARAMS,
        cost_estimate=LIGHT,
    )(*values, *after)


def message_kernel(lengths_ref, kept_ref, other_ref, *refs):
    out_ref = refs[-1]
    rows, columns = kept_ref.shape
    out_ref[:, :columns] = slim(kept_ref[...] + wide(other_ref[...]))
    row = lax.broadcasted_iota(jnp.int32, (rows, 128), 0)
    live = jnp.zeros((rows, 128), jnp.float32)
    for cand in range(rows // CAP):
        inside = (row >= cand * CAP) & (row < cand * CAP + lengths_ref[cand])
        live = jnp.where(inside, 1.0, live)
    out_ref[:, columns:] = slim(live)


def message_call(lengths, kept, other, after):
    rows, columns = kept.shape
    return pl.pallas_call(
        message_kernel,
        in_specs=[SMEM, VMEM, VMEM] + [HBM] * len(after),
        out_specs=VMEM,
        out_shape=jax.ShapeDtypeStruct((rows, columns + 128), jnp.bfloat16),
        compiler_params=PARAMS,
        cost_estimate=LIGHT,
    )(lengths, kept, other, *after)


def stack_kernel(count, *refs):
    out_ref = refs[-1]
    rows = refs[0].shape[0]
    for at in range(count):
        out_ref[at * rows : (at + 1) * rows] = refs[at][...]


def stack_call(values):
    rows, columns = values[0].shape
    return pl.pallas_call(
        functools.partial(stack_kernel, len(values)),
        in_specs=[VMEM] * len(values),
        out_specs=VMEM,
        out_shape=jax.ShapeDtypeStruct((rows * len(values), columns), values[0].dtype),
        compiler_params=PARAMS,
        cost_estimate=LIGHT,
    )(*values)


def span_of(counts_ref, group, images):
    first, end = jnp.int32(0), jnp.int32(0)
    for image in range(images):
        first = first + jnp.where(image < group, counts_ref[image], 0)
        end = end + jnp.where(image <= group, counts_ref[image], 0)
    return first, end


def row_ids(index, place, core, places, word_rows, sign):
    step = index // word_rows
    at = lax.rem(place + sign * step + places, places)
    return (at * 2 + core) * word_rows + lax.rem(index, word_rows)


def near_kernel(places, spots_ref, counts_ref, own_ref, other_ref, *refs):
    out_ref, token_ref = refs[-2:]
    near_rows = out_ref.shape[0]
    rows = own_ref.shape[0]
    place, core, group = spots_ref[1], spots_ref[2], spots_ref[4]
    first, _ = span_of(counts_ref, group, counts_ref.shape[0])
    near_id = first * CAP + lax.broadcasted_iota(jnp.int32, (near_rows, rows), 0)
    column = lax.broadcasted_iota(jnp.int32, (near_rows, rows), 1)
    total = 0.0
    for core_at, ref in ((core, own_ref), (1 - core, other_ref)):
        pick = near_id == row_ids(column, place, core_at, places, rows // places, -1)
        total = total + dot(slim(jnp.where(pick, 1.0, 0.0)), ref[...])
    out_ref[...] = slim(total)
    token_ref[...] = jnp.zeros(TOKEN, jnp.float32)


def near_call(spots, counts, own, other, places, near_rows, after):
    return pl.pallas_call(
        functools.partial(near_kernel, places),
        in_specs=[SMEM, SMEM, VMEM, VMEM] + [HBM] * len(after),
        out_specs=[VMEM, VMEM],
        out_shape=[
            jax.ShapeDtypeStruct((near_rows, own.shape[1]), jnp.bfloat16),
            jax.ShapeDtypeStruct(TOKEN, jnp.float32),
        ],
        compiler_params=PARAMS,
        cost_estimate=LIGHT,
    )(spots, counts, own, other, *after)


def across(a, b):
    return lax.dot_general(a, b, (((1,), (1,)), ((), ())), preferred_element_type=jnp.float32)


def attend_kernel(places, word_rows, width, spots_ref, counts_ref, near_ref, *refs):
    parts, outs, result_ref = refs[:6], refs[6 : 6 + places], refs[-1]
    near_rows = near_ref.shape[0]
    share = result_ref.shape[1]
    place, core, group = spots_ref[1], spots_ref[2], spots_ref[4]
    first, end = span_of(counts_ref, group, counts_ref.shape[0])
    sources = []
    for kept_ref, got_ref, power_ref in (parts[:3], parts[3:]):
        power = power_ref[:, :1] + jnp.sum(
            wide(got_ref[:, 2 * share : 2 * share + 128]), axis=1, keepdims=True
        )
        scale = lax.rsqrt(power / width + EPSILON)
        total = slim((kept_ref[...] + wide(got_ref[:, : 2 * share])) * scale)
        sources.append((total[:, :share], total[:, share:], None))
    lane = lax.broadcasted_iota(jnp.int32, (16, 128), 1)
    pick = slim(jnp.where(lane == 0, 1.0, 0.0))
    live = across(pick, near_ref[:, 3 * share :])[:1]
    shape = (near_rows, near_rows)
    own = lax.broadcasted_iota(jnp.int32, shape, 0) // CAP == lax.broadcasted_iota(jnp.int32, shape, 1) // CAP
    allowed = own & (live > 0.5)
    sources.append((near_ref[:, share : 2 * share], near_ref[:, 2 * share : 3 * share], allowed))
    for head in range(share // DH):
        columns = slice(head * DH, (head + 1) * DH)
        query = near_ref[:, columns]
        scores = []
        for keys, _, mask in sources:
            score = across(query, keys[:, columns]) * DH ** (-0.5)
            scores.append(score if mask is None else jnp.where(mask, score, FLOOR))
        top = functools.reduce(
            jnp.maximum, [jnp.max(score, axis=1, keepdims=True) for score in scores]
        )
        total, mixed = 0.0, 0.0
        for score, (_, values, mask) in zip(scores, sources):
            weights = jnp.exp(score - top)
            if mask is not None:
                weights = jnp.where(mask, weights, 0.0)
            total = total + jnp.sum(weights, axis=1, keepdims=True)
            mixed = mixed + dot(slim(weights), values[:, columns])
        result_ref[:, columns] = slim(mixed / total)
    block = 2 * word_rows
    row = lax.broadcasted_iota(jnp.int32, (block, near_rows), 0)
    near_id = first * CAP + lax.broadcasted_iota(jnp.int32, (block, near_rows), 1)
    core_at = jnp.where(row < word_rows, core, 1 - core)
    for step, out_ref in enumerate(outs):
        home = lax.rem(place + step, places)
        ids = (home * 2 + core_at) * word_rows + lax.rem(row, word_rows)
        put = (ids == near_id) & (near_id < end * CAP)
        out_ref[...] = slim(dot(slim(jnp.where(put, 1.0, 0.0)), result_ref[...]))


def attend_call(spots, counts, near, pieces, places, word_rows, width):
    share = pieces[0].shape[1] // 2
    return pl.pallas_call(
        functools.partial(attend_kernel, places, word_rows, width),
        in_specs=[SMEM, SMEM] + [VMEM] * (1 + len(pieces)),
        out_specs=[VMEM] * places,
        out_shape=[jax.ShapeDtypeStruct((2 * word_rows, share), jnp.bfloat16)] * places,
        scratch_shapes=[pltpu.VMEM((near.shape[0], share), jnp.bfloat16)],
        compiler_params=PARAMS,
        cost_estimate=LIGHT,
    )(spots, counts, near, *pieces)


def land_kernel(*refs):
    kept_ref, given_ref = refs[-2:]
    rows = kept_ref.shape[0]
    total = wide(refs[0][...])
    for ref in refs[1:-2]:
        total = total + wide(ref[...])
    kept_ref[...] = slim(total[:rows])
    given_ref[...] = slim(total[rows:])


def land_call(values):
    rows, columns = values[0].shape
    return pl.pallas_call(
        land_kernel,
        in_specs=[VMEM] * len(values),
        out_specs=[VMEM, VMEM],
        out_shape=[jax.ShapeDtypeStruct((rows // 2, columns), jnp.bfloat16)] * 2,
        compiler_params=PARAMS,
        cost_estimate=LIGHT,
    )(*values)


def output_kernel(spots_ref, kept_ref, core_ref, vis_ref, both_ref, weight_ref, mine_ref, sent_ref):
    vis, enc = spots_ref[0], spots_ref[3]
    share = kept_ref.shape[1]
    own = slim(wide(kept_ref[...]) + wide(core_ref[...]))
    other = slim(wide(vis_ref[...]) + wide(both_ref[...]))
    slots = CAP // 2
    columns = weight_ref.shape[1]
    part = tile_of(columns, 512)
    for start in range(0, columns, part):
        span = slice(start, start + part)
        total = dot(own, weight_ref[pl.ds(pl.multiple_of(vis * share, share), share), span])
        total = total + dot(other, weight_ref[pl.ds(pl.multiple_of((1 - vis) * share, share), share), span])
        firsts = range(0, total.shape[0], CAP)
        low = jnp.concatenate([total[at : at + slots] for at in firsts])
        high = jnp.concatenate([total[at + slots : at + CAP] for at in firsts])
        mine_ref[:, span] = jnp.where(enc == 0, low, high)
        sent_ref[:, span] = slim(jnp.where(enc == 0, high, low))


def output_call(spots, pieces, weight):
    shape = (pieces[0].shape[0] // 2, weight.shape[1])
    return pl.pallas_call(
        output_kernel,
        in_specs=[SMEM] + [VMEM] * 5,
        out_specs=[VMEM, VMEM],
        out_shape=[
            jax.ShapeDtypeStruct(shape, jnp.float32),
            jax.ShapeDtypeStruct(shape, jnp.bfloat16),
        ],
        compiler_params=PARAMS,
        cost_estimate=LIGHT,
    )(spots, *pieces, weight)


def on_device(
    image_tokens,
    vision_gain,
    up_weight,
    down_weight,
    project_weight,
    encoder_gain,
    qkv_weight,
    out_weight,
    captions,
    cand_counts,
    caption_lengths,
):
    vis_count = lax.axis_size("vis")
    enc_count = lax.axis_size("enc")
    groups = lax.axis_size("grp")
    vis = lax.axis_index("vis")
    group = lax.axis_index("grp")
    rows, features = image_tokens.shape[1:]
    all_features = features * enc_count
    width = captions.shape[2] * vis_count
    pair = vis_count == 2
    part_rows = rows // vis_count

    cores = 2 if groups % 2 == 0 else 1
    places = groups // cores
    place, core = group // cores, group % cores
    core_swap = [(i, i ^ 1) for i in range(groups)]
    up_weights, down_weights = [up_weight], [down_weight]
    if cores == 2:
        up_weights.append(lax.ppermute(up_weight, "grp", core_swap))
        down_weights.append(lax.ppermute(down_weight, "grp", core_swap))
        if up_weight.shape[1] % 128:
            up_weights = [jnp.concatenate(up_weights, axis=1)]
            down_weights = [jnp.concatenate(down_weights)]

    def to_place(value, step):
        return lax.ppermute(
            value, "grp", [(i, (i + step * cores) % groups) for i in range(groups)]
        )

    def mine_of(value):
        return lax.dynamic_slice_in_dim(value, vis * part_rows, part_rows, axis=0)

    def halves_of(mine, value):
        if pair and value is None:
            return [mine, shifted(mine, "vis", 1)]
        if pair:
            return [mine, lax.dynamic_slice_in_dim(value, (1 - vis) * part_rows, part_rows, axis=0)]
        if value is None:
            value = lax.all_gather(mine, "vis", axis=0, tiled=True)
        return [value[: rows // 2], value[rows // 2 :]]

    token = []

    def gated(value):
        return value + token[0][0, 0].astype(value.dtype) if token else value

    words = wide(captions)
    word_power = summed(jnp.sum(words * words, axis=-1), "vis")
    tokens = wide(image_tokens[0])
    row_total, row_squares = summed(
        jnp.stack([jnp.sum(tokens, axis=-1), jnp.sum(tokens * tokens, axis=-1)]), "enc"
    )
    mean = row_total / all_features
    spread = row_squares / all_features - mean * mean
    normed = slim(
        (tokens - mean[:, None]) * lax.rsqrt(spread + EPSILON)[:, None] * vision_gain
    )
    my_tokens = mine_of(image_tokens[0])
    my_normed = mine_of(normed)

    inner = qkv_weight.shape[2]
    heads = inner // DH
    shares = vis_count if heads % vis_count == 0 else 1
    share = inner // shares
    fast = pair and shares == 2 and cores == 2 and enc_count == 2
    spots = jnp.stack([vis, place, core, lax.axis_index("enc"), group])
    word_normed = slim(words * lax.rsqrt(word_power / width + EPSILON)[..., None] * encoder_gain)
    all_words = joined(word_normed, "enc", 1)
    cand_local = all_words.shape[0]
    word_rows = cand_local * CAP
    flat_words = all_words.reshape(word_rows, all_words.shape[2])

    def head_weights(which):
        return lax.dynamic_slice_in_dim(qkv_weight, which * share, share, axis=2)

    def heads_of(block, weight):
        return jnp.einsum("rd,kdh->rkh", block, weight, preferred_element_type=jnp.float32)

    def head_sum(values):
        if shares == 1:
            return lax.psum(values, "vis")
        return lax.psum_scatter(values, "vis", scatter_dimension=2, tiled=True)

    arrived, blocks, pres, outs, backs = {}, {}, {}, {}, {}

    def forwarded(step):
        if step < places:
            here = passed(arrived[step], token[0]) if step > 1 and token else arrived[step]
            if step + 1 < places:
                arrived[step + 1] = to_place(here, 1)
            blocks[step] = halves_of(here, None)

    def up(step, *after):
        if step < places:
            pre, token[:] = (lambda got: (got[0], [got[1]]))(
                up_call(blocks[step], up_weights, [*token, *after])
            )
            if enc_count == 2:
                pres[step] = pre, shifted(pre, "enc", 1)
            else:
                pres[step] = pre, slim(lax.psum(wide(pre), "enc") - wide(pre))

    def down(step, *after):
        if step < places:
            kept, sent, next_token = down_call(*pres[step], down_weights, [*token, *after])
            token[:] = [next_token]
            if pair:
                outs[step] = kept, shifted(sent, "vis", 1)
            else:
                out = jnp.concatenate([kept, wide(sent)])
                kept = lax.psum_scatter(out, "vis", scatter_dimension=0, tiled=True)
                outs[step] = kept, jnp.zeros_like(kept, jnp.bfloat16)

    def back(step):
        if 0 < step < places:
            parts = [*outs[step], *([backs[step - 1]] if step > 1 else [])]
            total, next_token = add_call(parts, token)
            token[:] = [next_token]
            backs[step] = to_place(total, 1)

    if places > 1:
        arrived[1] = to_place(my_normed, 1)
    if fast:
        word_sent, word_kept, word_token = heads_call(
            flat_words, qkv_weight, spots, [my_normed, my_tokens]
        )
        token[:] = [word_token]
        word_other = shifted(word_sent, "vis", 1)
    else:
        word_kept = head_sum(heads_of(flat_words, qkv_weight)).reshape(word_rows, 3 * share)
        word_other = jnp.zeros_like(word_kept, jnp.bfloat16)
    forwarded(1)
    messages = []

    def hops():
        for step in range(1, places):
            back_one = step > 1 and step == places - 1
            messages.append(
                to_place(messages[0], -1) if back_one else to_place(messages[-1], 1)
            )

    blocks[0] = halves_of(my_normed, normed)
    if fast:
        up_weights[-1] = held_call(up_weights[-1], token)
    up(0)
    forwarded(2)
    messages.append(message_call(caption_lengths, word_kept, word_other, token))
    up(1, messages[0])
    hops()
    if fast:
        down_weights[-1] = held_call(down_weights[-1], token)
    down(0)
    forwarded(3)
    up(2, blocks[places - 1][0], *messages[1:2])
    down(1)
    up(3)
    down(2, *messages[2:])
    back(1)
    for step in range(4, places):
        forwarded(step)
        up(step)
        down(step - 1)
    down(places - 1)
    word_block = stack_call(messages)
    if cores == 2:
        word_blocks = [word_block, lax.ppermute(word_block, "grp", core_swap)]
    else:
        word_blocks = [word_block]
    for step in range(2, places):
        back(step)

    home = [my_tokens, *outs[0], *([backs[places - 1]] if places > 1 else [])]
    cands = groups * cand_local
    most = min(MOSTC, cands)
    if fast:
        near, near_token = near_call(
            spots, cand_counts, *word_blocks, places, most * CAP, token
        )
        final_weight = held_call(out_weight, [near_token])
        my_vision, _ = add_call(home, [near_token, final_weight])
        other_vision = shifted(my_vision, "vis", 1)
        pieces = []
        for block in (my_vision, other_vision):
            partial = project_call(block, project_weight, [])
            full = shifted(partial, "enc", 1)
            pieces.append(image_call(partial, full, encoder_gain, qkv_weight, spots))
        got = [shifted(sent, "vis", 1) for _, sent, _ in pieces]
        parts = []
        for here, there in ((0, 1), (1, 0)):
            parts += [pieces[here][0], got[there], pieces[here][2]]
        placed = attend_call(spots, cand_counts, near, parts, places, word_rows, width)
        landed = [to_place(part, step) if step else part for step, part in enumerate(placed)]
        kept, given = land_call(landed)
        across_both = [
            (v * groups + i, (1 - v) * groups + (i ^ 1)) for v in range(2) for i in range(groups)
        ]
        from_core = lax.ppermute(given, "grp", core_swap)
        from_both = lax.ppermute(given, ("vis", "grp"), across_both)
        from_vis = shifted(kept, "vis", 1)
        mine, sent = output_call(spots, [kept, from_core, from_vis, from_both], final_weight)
        words_out = (mine + wide(shifted(sent, "enc", 1))).reshape(words.shape)
        vision_rows = jnp.where(
            vis == 0,
            jnp.concatenate([my_vision, other_vision]),
            jnp.concatenate([other_vision, my_vision]),
        )
        return (vision_rows[None], slim(words + words_out))
    my_vision = slim(sum([wide(part) for part in home]))

    ends = jnp.cumsum(cand_counts)
    start = ends[group] - cand_counts[group]
    near_ids = start * CAP + jnp.arange(most * CAP, dtype=jnp.int32)
    owned = near_ids < ends[group] * CAP

    def ids_of(core_at, sign):
        steps = jnp.arange(places, dtype=jnp.int32)[:, None]
        first = ((place + sign * steps) % places * cores + core_at) * word_rows
        return (first + jnp.arange(word_rows, dtype=jnp.int32)[None]).reshape(-1)

    core_order = [core, 1 - core][:cores]
    near = 0.0
    for core_at, block in zip(core_order, word_blocks):
        pick = near_ids[:, None] == ids_of(core_at, -1)[None, :]
        near = near + dot(pick.astype(jnp.bfloat16), block)
    near = slim(near)
    place_ids = jnp.concatenate(
        [ids_of(core_at, 1).reshape(places, word_rows) for core_at in core_order], axis=1
    ).reshape(-1)
    put = slim((place_ids[:, None] == near_ids[None, :]) & owned[None, :])
    def embed(block):
        partial = dot(block, project_weight)
        if enc_count == 2:
            full = partial + wide(shifted(slim(partial), "enc", 1))
        else:
            full = lax.psum(partial, "enc")
        return slim(full * encoder_gain), jnp.sum(full * full, axis=-1)

    vision_rows = joined(my_vision, "vis", 0)
    scaled, power = embed(vision_rows)
    total = head_sum(heads_of(scaled, qkv_weight[1:]))
    power = lax.psum(power, "vis")
    image_kv = slim(total * lax.rsqrt(power / width + EPSILON)[:, None, None])

    live = near[:, 3 * share] > 0
    near = near[:, : 3 * share].reshape(most * CAP, 3, share // DH, DH)
    row_cand = jnp.arange(most * CAP, dtype=jnp.int32) // CAP
    own_allowed = (row_cand[:, None] == row_cand[None, :]) & live[None, :]
    image_kv = image_kv.reshape(rows, 2, share // DH, DH)
    query = near[:, 0]

    def scores_of(keys):
        return jnp.einsum(
            "qhd,khd->hqk", query, keys, preferred_element_type=jnp.float32
        ) * DH ** (-0.5)

    def mixed(weights, values):
        return jnp.einsum(
            "hqk,khd->hqd", slim(weights), values, preferred_element_type=jnp.float32
        )

    image_scores = scores_of(image_kv[:, 0])
    own_scores = jnp.where(own_allowed[None], scores_of(near[:, 1]), FLOOR)
    top = jnp.maximum(
        jnp.max(image_scores, axis=-1, keepdims=True), jnp.max(own_scores, axis=-1, keepdims=True)
    )
    image_weights = jnp.exp(image_scores - top)
    own_weights = jnp.where(own_allowed[None], jnp.exp(own_scores - top), 0.0)
    total = jnp.sum(image_weights, axis=-1, keepdims=True) + jnp.sum(
        own_weights, axis=-1, keepdims=True
    )
    result = (mixed(image_weights, image_kv[:, 1]) + mixed(own_weights, near[:, 2])) / total
    result = slim(result).transpose(1, 0, 2).reshape(most * CAP, share)
    spread_out = slim(dot(put, result)).reshape(places, cores * word_rows, share)
    landed = spread_out[0]
    for step in range(1, places):
        landed = landed + to_place(spread_out[step], step)
    kept = landed[:word_rows]
    attended = kept
    if cores == 2:
        given = landed[word_rows:]
        attended = kept + lax.ppermute(given, "grp", core_swap)
    if shares > 1:
        attended = lax.all_gather(attended, "vis", axis=1, tiled=True)
    partial_words = dot(attended, out_weight).reshape(cand_local, CAP, out_weight.shape[1])
    words_out = lax.psum_scatter(partial_words, "enc", scatter_dimension=1, tiled=True)
    caption_out = slim(words + words_out)
    return (vision_rows[None], caption_out)


def solution(mesh):
    return jax.shard_map(
        on_device,
        mesh=mesh,
        in_specs=(
            P("grp", None, "enc"),
            P("enc"),
            P("enc", ("vis", "grp")),
            P(("vis", "grp"), "enc"),
            P("enc", "vis"),
            P("vis"),
            P(None, "vis", "enc"),
            P("enc", "vis"),
            P("grp", "enc", "vis"),
            P(),
            P("grp"),
        ),
        out_specs=(P("grp", None, "enc"), P("grp", "enc", "vis")),
        check_vma=False,
    )
```

```python
import functools

import jax
import jax.numpy as jnp
from jax import lax
from jax.experimental import pallas as pl
from jax.experimental.pallas import tpu as pltpu
from jax.sharding import PartitionSpec as P

DH = 256
CAP = 16
MOSTC = 12


EPSILON = 1e-06
FLOOR = -1e30


def dot(a, b):
    return jnp.dot(a, b, preferred_element_type=jnp.float32)


def wide(a):
    return a.astype(jnp.float32)


def slim(a):
    return a.astype(jnp.bfloat16)


def shifted(value, axis, step):
    count = lax.axis_size(axis)
    return lax.ppermute(value, axis, [(i, (i + step) % count) for i in range(count)])


def summed(value, axis):
    if lax.axis_size(axis) != 2:
        return lax.psum(value, axis)
    return value + shifted(value, axis, 1)


def joined(value, axis, dim):
    if lax.axis_size(axis) != 2:
        return lax.all_gather(value, axis, axis=dim, tiled=True)
    other = shifted(value, axis, 1)
    first = lax.axis_index(axis) == 0
    return jnp.concatenate(
        [jnp.where(first, value, other), jnp.where(first, other, value)], axis=dim
    )


TOKEN = (8, 128)
HBM = pl.BlockSpec(memory_space=pl.ANY)
VMEM = pl.BlockSpec(memory_space=pltpu.VMEM)
SMEM = pl.BlockSpec(memory_space=pltpu.SMEM)
LIGHT = pl.CostEstimate(flops=1024, bytes_accessed=1024, transcendentals=0)
PARAMS = pltpu.CompilerParams(vmem_limit_bytes=12 * 1024 * 1024)


def tile_of(size, most):
    return most if size % most == 0 else size


def pass_kernel(value_ref, token_ref, out_ref):
    pass


def passed(value, token):
    return pl.pallas_call(
        pass_kernel,
        in_specs=[HBM, HBM],
        out_specs=HBM,
        out_shape=jax.ShapeDtypeStruct(value.shape, value.dtype),
        input_output_aliases={0: 0},
        compiler_params=PARAMS,
        cost_estimate=LIGHT,
    )(value, token)


def hold_kernel(value_ref, *refs):
    out_ref, sem = refs[-2:]
    copy = pltpu.make_async_copy(value_ref, out_ref, sem)
    copy.start()
    copy.wait()


def held_call(value, after):
    return pl.pallas_call(
        hold_kernel,
        in_specs=[HBM] * (1 + len(after)),
        out_specs=VMEM,
        out_shape=jax.ShapeDtypeStruct(value.shape, value.dtype),
        scratch_shapes=[pltpu.SemaphoreType.DMA],
        compiler_params=PARAMS,
        cost_estimate=LIGHT,
    )(value, *after)


def up_kernel(cores, mine_ref, theirs_ref, *refs):
    weights, (out_ref, token_ref, rows_ref) = refs[:cores], refs[-3:]
    half = mine_ref.shape[0]
    units = weights[0].shape[1]
    tile = tile_of(units, 256)
    rows_ref[:half] = mine_ref[...]
    rows_ref[half:] = theirs_ref[...]
    token_ref[...] = jnp.zeros(TOKEN, jnp.float32)
    for core in range(cores):
        for first in range(0, units, tile):
            out_ref[:, core * units + first : core * units + first + tile] = slim(
                dot(rows_ref[...], weights[core][:, first : first + tile])
            )


def up_call(halves, weights, after):
    cores = len(weights)
    depth, units = weights[0].shape
    rows = 2 * halves[0].shape[0]
    return pl.pallas_call(
        functools.partial(up_kernel, cores),
        in_specs=[VMEM] * (2 + cores) + [HBM] * len(after),
        out_specs=[VMEM, VMEM],
        out_shape=[
            jax.ShapeDtypeStruct((rows, cores * units), jnp.bfloat16),
            jax.ShapeDtypeStruct(TOKEN, jnp.float32),
        ],
        scratch_shapes=[pltpu.VMEM((rows, depth), jnp.bfloat16)],
        compiler_params=PARAMS,
        cost_estimate=LIGHT,
    )(*halves, *weights, *after)


def down_kernel(cores, own_ref, other_ref, *refs):
    weights, (kept_ref, sent_ref, token_ref, total_ref) = refs[:cores], refs[-6:-2]
    hidden = refs[-2:]
    units, columns = weights[0].shape
    tile = tile_of(units, 256)
    half = kept_ref.shape[0]
    part = tile_of(columns, 1536)
    token_ref[...] = jnp.zeros(TOKEN, jnp.float32)
    order = [(core, first) for core in range(cores) for first in range(0, units, tile)]

    def fill(at):
        core, first = order[at]
        columns_at = slice(core * units + first, core * units + first + tile)
        total = wide(own_ref[:, columns_at]) + wide(other_ref[:, columns_at])
        hidden[at % 2][...] = slim(0.5 * total * (1.0 + lax.erf(total * 0.5**0.5)))

    fill(0)
    for at, (core, first) in enumerate(order):
        for start in range(0, columns, part):
            term = dot(hidden[at % 2][...], weights[core][first : first + tile, start : start + part])
            if at:
                term = total_ref[:, start : start + part] + term
            if at + 1 < len(order):
                total_ref[:, start : start + part] = term
            else:
                kept_ref[:, start : start + part] = slim(term[:half])
                sent_ref[:, start : start + part] = slim(term[half:])
        if at + 1 < len(order):
            fill(at + 1)


def down_call(own, other, weights, after):
    cores = len(weights)
    units, columns = weights[0].shape
    tile = tile_of(units, 256)
    rows = own.shape[0]
    half = jax.ShapeDtypeStruct((rows // 2, columns), jnp.bfloat16)
    return pl.pallas_call(
        functools.partial(down_kernel, cores),
        in_specs=[VMEM] * (2 + cores) + [HBM] * len(after),
        out_specs=[VMEM, VMEM, VMEM],
        out_shape=[half, half, jax.ShapeDtypeStruct(TOKEN, jnp.float32)],
        scratch_shapes=[pltpu.VMEM((rows, columns), jnp.float32)]
        + [pltpu.VMEM((rows, tile), jnp.bfloat16)] * 2,
        compiler_params=PARAMS,
        cost_estimate=LIGHT,
    )(own, other, *weights, *after)


def project_kernel(rows_ref, weight_ref, *refs):
    out_ref = refs[-1]
    columns = weight_ref.shape[1]
    part = tile_of(columns, 512)
    for first in range(0, columns, part):
        out_ref[:, first : first + part] = slim(
            dot(rows_ref[...], weight_ref[:, first : first + part])
        )


def project_call(rows, weight, after):
    return pl.pallas_call(
        project_kernel,
        in_specs=[VMEM, VMEM] + [HBM] * len(after),
        out_specs=VMEM,
        out_shape=jax.ShapeDtypeStruct((rows.shape[0], weight.shape[1]), jnp.bfloat16),
        compiler_params=PARAMS,
        cost_estimate=LIGHT,
    )(rows, weight, *after)


def image_kernel(vis_ref, own_ref, other_ref, gain_ref, weight_ref, kept_ref, sent_ref, power_ref):
    share = weight_ref.shape[2] // 2
    full = wide(own_ref[...]) + wide(other_ref[...])
    power = jnp.sum(full * full, axis=1, keepdims=True)
    scaled = slim(full * gain_ref[...])
    power_ref[...] = jnp.broadcast_to(power, power_ref.shape)
    high = slim(power)
    middle = slim(power - wide(high))
    low = slim(power - wide(high) - wide(middle))
    lane = lax.broadcasted_iota(jnp.int32, (power.shape[0], 128), 1)
    parts = jnp.where(lane == 0, wide(high), jnp.where(lane == 1, wide(middle), wide(low)))
    sent_ref[:, 2 * share :] = slim(jnp.where(lane < 3, parts, 0.0))
    vis = vis_ref[0]
    for kind in range(2):
        columns = slice(kind * share, (kind + 1) * share)
        other = pl.ds(pl.multiple_of((1 - vis) * share, share), share)
        sent_ref[:, columns] = slim(dot(scaled, weight_ref[kind + 1, :, other]))
    for kind in range(2):
        columns = slice(kind * share, (kind + 1) * share)
        mine = pl.ds(pl.multiple_of(vis * share, share), share)
        kept_ref[:, columns] = dot(scaled, weight_ref[kind + 1, :, mine])


def image_call(own, other, gain, weight, spots):
    rows = own.shape[0]
    share = weight.shape[2] // 2
    return pl.pallas_call(
        image_kernel,
        in_specs=[pl.BlockSpec(memory_space=pltpu.SMEM)] + [VMEM] * 4,
        out_specs=[VMEM] * 3,
        out_shape=[
            jax.ShapeDtypeStruct((rows, 2 * share), jnp.float32),
            jax.ShapeDtypeStruct((rows, 2 * share + 128), jnp.bfloat16),
            jax.ShapeDtypeStruct((rows, 128), jnp.float32),
        ],
        compiler_params=PARAMS,
        cost_estimate=LIGHT,
    )(spots, own, other, gain[None], weight)


def heads_kernel(vis_ref, rows_ref, weight_ref, *refs):
    sent_ref, kept_ref, token_ref = refs[-3:]
    kinds, _, inner = weight_ref.shape
    share = inner // 2
    vis = vis_ref[0]
    token_ref[...] = jnp.zeros(TOKEN, jnp.float32)
    for which, out_ref in ((1 - vis, sent_ref), (vis, kept_ref)):
        for kind in range(kinds):
            heads = pl.ds(pl.multiple_of(which * share, share), share)
            term = dot(rows_ref[...], weight_ref[kind, :, heads])
            out_ref[:, kind * share : (kind + 1) * share] = term.astype(out_ref.dtype)


def heads_call(block, weight, spots, after):
    shape = (block.shape[0], weight.shape[0] * weight.shape[2] // 2)
    return pl.pallas_call(
        heads_kernel,
        in_specs=[pl.BlockSpec(memory_space=pltpu.SMEM), VMEM, VMEM] + [HBM] * len(after),
        out_specs=[VMEM, VMEM, VMEM],
        out_shape=[
            jax.ShapeDtypeStruct(shape, jnp.bfloat16),
            jax.ShapeDtypeStruct(shape, jnp.float32),
            jax.ShapeDtypeStruct(TOKEN, jnp.float32),
        ],
        compiler_params=PARAMS,
        cost_estimate=LIGHT,
    )(spots, block, weight, *after)


def add_kernel(count, *refs):
    out_ref, token_ref = refs[-2:]
    rows = out_ref.shape[0]
    step = tile_of(rows, 32)

    def body(at, carry):
        part = pl.ds(pl.multiple_of(at * step, step), step)
        total = wide(refs[0][part])
        for ref in refs[1:count]:
            total = total + wide(ref[part])
        out_ref[part] = slim(total)
        return carry

    lax.fori_loop(0, rows // step, body, 0)
    token_ref[...] = jnp.zeros(TOKEN, jnp.float32)


def add_call(values, after):
    return pl.pallas_call(
        functools.partial(add_kernel, len(values)),
        in_specs=[VMEM] * len(values) + [HBM] * len(after),
        out_specs=[VMEM, VMEM],
        out_shape=[
            jax.ShapeDtypeStruct(values[0].shape, jnp.bfloat16),
            jax.ShapeDtypeStruct(TOKEN, jnp.float32),
        ],
        compiler_params=PARAMS,
        cost_estimate=LIGHT,
    )(*values, *after)


def message_kernel(lengths_ref, kept_ref, other_ref, *refs):
    out_ref = refs[-1]
    rows, columns = kept_ref.shape
    out_ref[:, :columns] = slim(kept_ref[...] + wide(other_ref[...]))
    row = lax.broadcasted_iota(jnp.int32, (rows, 128), 0)
    live = jnp.zeros((rows, 128), jnp.float32)
    for cand in range(rows // CAP):
        inside = (row >= cand * CAP) & (row < cand * CAP + lengths_ref[cand])
        live = jnp.where(inside, 1.0, live)
    out_ref[:, columns:] = slim(live)


def message_call(lengths, kept, other, after):
    rows, columns = kept.shape
    return pl.pallas_call(
        message_kernel,
        in_specs=[SMEM, VMEM, VMEM] + [HBM] * len(after),
        out_specs=VMEM,
        out_shape=jax.ShapeDtypeStruct((rows, columns + 128), jnp.bfloat16),
        compiler_params=PARAMS,
        cost_estimate=LIGHT,
    )(lengths, kept, other, *after)


def stack_kernel(count, *refs):
    out_ref = refs[-1]
    rows = refs[0].shape[0]
    for at in range(count):
        out_ref[at * rows : (at + 1) * rows] = refs[at][...]


def stack_call(values):
    rows, columns = values[0].shape
    return pl.pallas_call(
        functools.partial(stack_kernel, len(values)),
        in_specs=[VMEM] * len(values),
        out_specs=VMEM,
        out_shape=jax.ShapeDtypeStruct((rows * len(values), columns), values[0].dtype),
        compiler_params=PARAMS,
        cost_estimate=LIGHT,
    )(*values)


def span_of(counts_ref, group, images):
    first, end = jnp.int32(0), jnp.int32(0)
    for image in range(images):
        first = first + jnp.where(image < group, counts_ref[image], 0)
        end = end + jnp.where(image <= group, counts_ref[image], 0)
    return first, end


def row_ids(index, place, core, places, word_rows, sign):
    step = index // word_rows
    at = lax.rem(place + sign * step + places, places)
    return (at * 2 + core) * word_rows + lax.rem(index, word_rows)


def near_kernel(places, spots_ref, counts_ref, own_ref, other_ref, *refs):
    out_ref, token_ref = refs[-2:]
    near_rows = out_ref.shape[0]
    rows = own_ref.shape[0]
    place, core, group = spots_ref[1], spots_ref[2], spots_ref[4]
    first, _ = span_of(counts_ref, group, counts_ref.shape[0])
    near_id = first * CAP + lax.broadcasted_iota(jnp.int32, (near_rows, rows), 0)
    column = lax.broadcasted_iota(jnp.int32, (near_rows, rows), 1)
    total = 0.0
    for core_at, ref in ((core, own_ref), (1 - core, other_ref)):
        pick = near_id == row_ids(column, place, core_at, places, rows // places, -1)
        total = total + dot(slim(jnp.where(pick, 1.0, 0.0)), ref[...])
    out_ref[...] = slim(total)
    token_ref[...] = jnp.zeros(TOKEN, jnp.float32)


def near_call(spots, counts, own, other, places, near_rows, after):
    return pl.pallas_call(
        functools.partial(near_kernel, places),
        in_specs=[SMEM, SMEM, VMEM, VMEM] + [HBM] * len(after),
        out_specs=[VMEM, VMEM],
        out_shape=[
            jax.ShapeDtypeStruct((near_rows, own.shape[1]), jnp.bfloat16),
            jax.ShapeDtypeStruct(TOKEN, jnp.float32),
        ],
        compiler_params=PARAMS,
        cost_estimate=LIGHT,
    )(spots, counts, own, other, *after)


def across(a, b):
    return lax.dot_general(a, b, (((1,), (1,)), ((), ())), preferred_element_type=jnp.float32)


def attend_kernel(places, word_rows, width, spots_ref, counts_ref, near_ref, *refs):
    parts, outs, result_ref = refs[:6], refs[6 : 6 + places], refs[-1]
    near_rows = near_ref.shape[0]
    share = result_ref.shape[1]
    place, core, group = spots_ref[1], spots_ref[2], spots_ref[4]
    first, end = span_of(counts_ref, group, counts_ref.shape[0])
    sources = []
    for kept_ref, got_ref, power_ref in (parts[:3], parts[3:]):
        power = power_ref[:, :1] + jnp.sum(
            wide(got_ref[:, 2 * share : 2 * share + 128]), axis=1, keepdims=True
        )
        scale = lax.rsqrt(power / width + EPSILON)
        total = slim((kept_ref[...] + wide(got_ref[:, : 2 * share])) * scale)
        sources.append((total[:, :share], total[:, share:], None))
    lane = lax.broadcasted_iota(jnp.int32, (16, 128), 1)
    pick = slim(jnp.where(lane == 0, 1.0, 0.0))
    live = across(pick, near_ref[:, 3 * share :])[:1]
    shape = (near_rows, near_rows)
    own = lax.broadcasted_iota(jnp.int32, shape, 0) // CAP == lax.broadcasted_iota(jnp.int32, shape, 1) // CAP
    allowed = own & (live > 0.5)
    sources.append((near_ref[:, share : 2 * share], near_ref[:, 2 * share : 3 * share], allowed))
    for head in range(share // DH):
        columns = slice(head * DH, (head + 1) * DH)
        query = near_ref[:, columns]
        scores = []
        for keys, _, mask in sources:
            score = across(query, keys[:, columns]) * DH ** (-0.5)
            scores.append(score if mask is None else jnp.where(mask, score, FLOOR))
        top = functools.reduce(
            jnp.maximum, [jnp.max(score, axis=1, keepdims=True) for score in scores]
        )
        total, mixed = 0.0, 0.0
        for score, (_, values, mask) in zip(scores, sources):
            weights = jnp.exp(score - top)
            if mask is not None:
                weights = jnp.where(mask, weights, 0.0)
            total = total + jnp.sum(weights, axis=1, keepdims=True)
            mixed = mixed + dot(slim(weights), values[:, columns])
        result_ref[:, columns] = slim(mixed / total)
    block = 2 * word_rows
    row = lax.broadcasted_iota(jnp.int32, (block, near_rows), 0)
    near_id = first * CAP + lax.broadcasted_iota(jnp.int32, (block, near_rows), 1)
    core_at = jnp.where(row < word_rows, core, 1 - core)
    for step, out_ref in enumerate(outs):
        home = lax.rem(place + step, places)
        ids = (home * 2 + core_at) * word_rows + lax.rem(row, word_rows)
        put = (ids == near_id) & (near_id < end * CAP)
        out_ref[...] = slim(dot(slim(jnp.where(put, 1.0, 0.0)), result_ref[...]))


def attend_call(spots, counts, near, pieces, places, word_rows, width):
    share = pieces[0].shape[1] // 2
    return pl.pallas_call(
        functools.partial(attend_kernel, places, word_rows, width),
        in_specs=[SMEM, SMEM] + [VMEM] * (1 + len(pieces)),
        out_specs=[VMEM] * places,
        out_shape=[jax.ShapeDtypeStruct((2 * word_rows, share), jnp.bfloat16)] * places,
        scratch_shapes=[pltpu.VMEM((near.shape[0], share), jnp.bfloat16)],
        compiler_params=PARAMS,
        cost_estimate=LIGHT,
    )(spots, counts, near, *pieces)


def land_kernel(*refs):
    kept_ref, given_ref = refs[-2:]
    rows = kept_ref.shape[0]
    total = wide(refs[0][...])
    for ref in refs[1:-2]:
        total = total + wide(ref[...])
    kept_ref[...] = slim(total[:rows])
    given_ref[...] = slim(total[rows:])


def land_call(values):
    rows, columns = values[0].shape
    return pl.pallas_call(
        land_kernel,
        in_specs=[VMEM] * len(values),
        out_specs=[VMEM, VMEM],
        out_shape=[jax.ShapeDtypeStruct((rows // 2, columns), jnp.bfloat16)] * 2,
        compiler_params=PARAMS,
        cost_estimate=LIGHT,
    )(*values)


def output_kernel(spots_ref, kept_ref, core_ref, vis_ref, both_ref, weight_ref, mine_ref, sent_ref):
    vis, enc = spots_ref[0], spots_ref[3]
    share = kept_ref.shape[1]
    own = slim(wide(kept_ref[...]) + wide(core_ref[...]))
    other = slim(wide(vis_ref[...]) + wide(both_ref[...]))
    slots = CAP // 2
    columns = weight_ref.shape[1]
    part = tile_of(columns, 512)
    for start in range(0, columns, part):
        span = slice(start, start + part)
        total = dot(own, weight_ref[pl.ds(pl.multiple_of(vis * share, share), share), span])
        total = total + dot(other, weight_ref[pl.ds(pl.multiple_of((1 - vis) * share, share), share), span])
        firsts = range(0, total.shape[0], CAP)
        low = jnp.concatenate([total[at : at + slots] for at in firsts])
        high = jnp.concatenate([total[at + slots : at + CAP] for at in firsts])
        mine_ref[:, span] = jnp.where(enc == 0, low, high)
        sent_ref[:, span] = slim(jnp.where(enc == 0, high, low))


def output_call(spots, pieces, weight):
    shape = (pieces[0].shape[0] // 2, weight.shape[1])
    return pl.pallas_call(
        output_kernel,
        in_specs=[SMEM] + [VMEM] * 5,
        out_specs=[VMEM, VMEM],
        out_shape=[
            jax.ShapeDtypeStruct(shape, jnp.float32),
            jax.ShapeDtypeStruct(shape, jnp.bfloat16),
        ],
        compiler_params=PARAMS,
        cost_estimate=LIGHT,
    )(spots, *pieces, weight)


def on_device(
    image_tokens,
    vision_gain,
    up_weight,
    down_weight,
    project_weight,
    encoder_gain,
    qkv_weight,
    out_weight,
    captions,
    cand_counts,
    caption_lengths,
):
    vis_count = lax.axis_size("vis")
    enc_count = lax.axis_size("enc")
    groups = lax.axis_size("grp")
    vis = lax.axis_index("vis")
    group = lax.axis_index("grp")
    rows, features = image_tokens.shape[1:]
    all_features = features * enc_count
    width = captions.shape[2] * vis_count
    pair = vis_count == 2
    part_rows = rows // vis_count

    cores = 2 if groups % 2 == 0 else 1
    places = groups // cores
    place, core = group // cores, group % cores
    core_swap = [(i, i ^ 1) for i in range(groups)]
    up_weights, down_weights = [up_weight], [down_weight]
    if cores == 2:
        up_weights.append(lax.ppermute(up_weight, "grp", core_swap))
        down_weights.append(lax.ppermute(down_weight, "grp", core_swap))
        if up_weight.shape[1] % 128:
            up_weights = [jnp.concatenate(up_weights, axis=1)]
            down_weights = [jnp.concatenate(down_weights)]

    def to_place(value, step):
        return lax.ppermute(
            value, "grp", [(i, (i + step * cores) % groups) for i in range(groups)]
        )

    def mine_of(value):
        return lax.dynamic_slice_in_dim(value, vis * part_rows, part_rows, axis=0)

    def halves_of(mine, value):
        if pair and value is None:
            return [mine, shifted(mine, "vis", 1)]
        if pair:
            return [mine, lax.dynamic_slice_in_dim(value, (1 - vis) * part_rows, part_rows, axis=0)]
        if value is None:
            value = lax.all_gather(mine, "vis", axis=0, tiled=True)
        return [value[: rows // 2], value[rows // 2 :]]

    token = []

    def gated(value):
        return value + token[0][0, 0].astype(value.dtype) if token else value

    tokens = wide(image_tokens[0])
    row_total, row_squares = summed(
        jnp.stack([jnp.sum(tokens, axis=-1), jnp.sum(tokens * tokens, axis=-1)]), "enc"
    )
    mean = row_total / all_features
    spread = row_squares / all_features - mean * mean
    normed = slim(
        (tokens - mean[:, None]) * lax.rsqrt(spread + EPSILON)[:, None] * vision_gain
    )
    my_tokens = mine_of(image_tokens[0])
    my_normed = mine_of(normed)
    words = wide(captions) + wide(my_normed[0, 0]) * 0.0
    word_power = summed(jnp.sum(words * words, axis=-1), "vis")

    inner = qkv_weight.shape[2]
    heads = inner // DH
    shares = vis_count if heads % vis_count == 0 else 1
    share = inner // shares
    fast = pair and shares == 2 and cores == 2 and enc_count == 2
    spots = jnp.stack([vis, place, core, lax.axis_index("enc"), group])
    word_normed = slim(words * lax.rsqrt(word_power / width + EPSILON)[..., None] * encoder_gain)
    all_words = joined(word_normed, "enc", 1)
    cand_local = all_words.shape[0]
    word_rows = cand_local * CAP
    flat_words = all_words.reshape(word_rows, all_words.shape[2])

    def head_weights(which):
        return lax.dynamic_slice_in_dim(qkv_weight, which * share, share, axis=2)

    def heads_of(block, weight):
        return jnp.einsum("rd,kdh->rkh", block, weight, preferred_element_type=jnp.float32)

    def head_sum(values):
        if shares == 1:
            return lax.psum(values, "vis")
        return lax.psum_scatter(values, "vis", scatter_dimension=2, tiled=True)

    arrived, blocks, pres, outs, backs = {}, {}, {}, {}, {}

    def forwarded(step):
        if step < places:
            here = passed(arrived[step], token[0]) if step > 1 and token else arrived[step]
            if step + 1 < places:
                arrived[step + 1] = to_place(here, 1)
            blocks[step] = halves_of(here, None)

    def up(step, *after):
        if step < places:
            pre, token[:] = (lambda got: (got[0], [got[1]]))(
                up_call(blocks[step], up_weights, [*token, *after])
            )
            if enc_count == 2:
                pres[step] = pre, shifted(pre, "enc", 1)
            else:
                pres[step] = pre, slim(lax.psum(wide(pre), "enc") - wide(pre))

    def down(step, *after):
        if step < places:
            kept, sent, next_token = down_call(*pres[step], down_weights, [*token, *after])
            token[:] = [next_token]
            if pair:
                outs[step] = kept, shifted(sent, "vis", 1)
            else:
                out = jnp.concatenate([kept, wide(sent)])
                kept = lax.psum_scatter(out, "vis", scatter_dimension=0, tiled=True)
                outs[step] = kept, jnp.zeros_like(kept, jnp.bfloat16)

    def back(step):
        if 0 < step < places:
            parts = [*outs[step], *([backs[step - 1]] if step > 1 else [])]
            total, next_token = add_call(parts, token)
            token[:] = [next_token]
            backs[step] = to_place(total, 1)

    if places > 1:
        arrived[1] = to_place(my_normed, 1)
    if fast:
        word_sent, word_kept, word_token = heads_call(
            flat_words, qkv_weight, spots, [my_normed, my_tokens]
        )
        token[:] = [word_token]
        word_other = shifted(word_sent, "vis", 1)
    else:
        word_kept = head_sum(heads_of(flat_words, qkv_weight)).reshape(word_rows, 3 * share)
        word_other = jnp.zeros_like(word_kept, jnp.bfloat16)
    forwarded(1)
    messages = []

    def hops():
        for step in range(1, places):
            back_one = step > 1 and step == places - 1
            messages.append(
                to_place(messages[0], -1) if back_one else to_place(messages[-1], 1)
            )

    blocks[0] = halves_of(my_normed, normed)
    if fast:
        up_weights[-1] = held_call(up_weights[-1], token)
    messages.append(
        message_call(caption_lengths, word_kept, word_other, [*token, up_weights[-1]])
    )
    up(1, messages[0])
    hops()
    forwarded(2)
    if fast:
        down_weights[-1] = held_call(down_weights[-1], token)
    down(1)
    forwarded(3)
    up(2, blocks[places - 1][0], *messages[1:2])
    back(1)
    up(3)
    down(2, *messages[2:])
    up(0, *[backs[step] for step in backs])
    for step in range(4, places):
        forwarded(step)
        up(step)
        down(step - 1)
    down(places - 1)
    for step in range(2, places - 1):
        back(step)
    down(0)
    word_block = stack_call(messages)
    if cores == 2:
        word_blocks = [word_block, lax.ppermute(word_block, "grp", core_swap)]
    else:
        word_blocks = [word_block]
    if places > 2:
        back(places - 1)

    home = [my_tokens, *outs[0], *([backs[places - 1]] if places > 1 else [])]
    cands = groups * cand_local
    most = min(MOSTC, cands)
    if fast:
        near, near_token = near_call(
            spots, cand_counts, *word_blocks, places, most * CAP, token
        )
        final_weight = held_call(out_weight, [near_token])
        my_vision, _ = add_call(home, [near_token, final_weight])
        other_vision = shifted(my_vision, "vis", 1)
        pieces = []
        for block in (my_vision, other_vision):
            partial = project_call(block, project_weight, [])
            full = shifted(partial, "enc", 1)
            pieces.append(image_call(partial, full, encoder_gain, qkv_weight, spots))
        got = [shifted(sent, "vis", 1) for _, sent, _ in pieces]
        parts = []
        for here, there in ((0, 1), (1, 0)):
            parts += [pieces[here][0], got[there], pieces[here][2]]
        placed = attend_call(spots, cand_counts, near, parts, places, word_rows, width)
        landed = [to_place(part, step) if step else part for step, part in enumerate(placed)]
        kept, given = land_call(landed)
        across_both = [
            (v * groups + i, (1 - v) * groups + (i ^ 1)) for v in range(2) for i in range(groups)
        ]
        from_core = lax.ppermute(given, "grp", core_swap)
        from_both = lax.ppermute(given, ("vis", "grp"), across_both)
        from_vis = shifted(kept, "vis", 1)
        mine, sent = output_call(spots, [kept, from_core, from_vis, from_both], final_weight)
        words_out = (mine + wide(shifted(sent, "enc", 1))).reshape(words.shape)
        vision_rows = jnp.where(
            vis == 0,
            jnp.concatenate([my_vision, other_vision]),
            jnp.concatenate([other_vision, my_vision]),
        )
        return (vision_rows[None], slim(words + words_out))
    my_vision = slim(sum([wide(part) for part in home]))

    ends = jnp.cumsum(cand_counts)
    start = ends[group] - cand_counts[group]
    near_ids = start * CAP + jnp.arange(most * CAP, dtype=jnp.int32)
    owned = near_ids < ends[group] * CAP

    def ids_of(core_at, sign):
        steps = jnp.arange(places, dtype=jnp.int32)[:, None]
        first = ((place + sign * steps) % places * cores + core_at) * word_rows
        return (first + jnp.arange(word_rows, dtype=jnp.int32)[None]).reshape(-1)

    core_order = [core, 1 - core][:cores]
    near = 0.0
    for core_at, block in zip(core_order, word_blocks):
        pick = near_ids[:, None] == ids_of(core_at, -1)[None, :]
        near = near + dot(pick.astype(jnp.bfloat16), block)
    near = slim(near)
    place_ids = jnp.concatenate(
        [ids_of(core_at, 1).reshape(places, word_rows) for core_at in core_order], axis=1
    ).reshape(-1)
    put = slim((place_ids[:, None] == near_ids[None, :]) & owned[None, :])
    def embed(block):
        partial = dot(block, project_weight)
        if enc_count == 2:
            full = partial + wide(shifted(slim(partial), "enc", 1))
        else:
            full = lax.psum(partial, "enc")
        return slim(full * encoder_gain), jnp.sum(full * full, axis=-1)

    vision_rows = joined(my_vision, "vis", 0)
    scaled, power = embed(vision_rows)
    total = head_sum(heads_of(scaled, qkv_weight[1:]))
    power = lax.psum(power, "vis")
    image_kv = slim(total * lax.rsqrt(power / width + EPSILON)[:, None, None])

    live = near[:, 3 * share] > 0
    near = near[:, : 3 * share].reshape(most * CAP, 3, share // DH, DH)
    row_cand = jnp.arange(most * CAP, dtype=jnp.int32) // CAP
    own_allowed = (row_cand[:, None] == row_cand[None, :]) & live[None, :]
    image_kv = image_kv.reshape(rows, 2, share // DH, DH)
    query = near[:, 0]

    def scores_of(keys):
        return jnp.einsum(
            "qhd,khd->hqk", query, keys, preferred_element_type=jnp.float32
        ) * DH ** (-0.5)

    def mixed(weights, values):
        return jnp.einsum(
            "hqk,khd->hqd", slim(weights), values, preferred_element_type=jnp.float32
        )

    image_scores = scores_of(image_kv[:, 0])
    own_scores = jnp.where(own_allowed[None], scores_of(near[:, 1]), FLOOR)
    top = jnp.maximum(
        jnp.max(image_scores, axis=-1, keepdims=True), jnp.max(own_scores, axis=-1, keepdims=True)
    )
    image_weights = jnp.exp(image_scores - top)
    own_weights = jnp.where(own_allowed[None], jnp.exp(own_scores - top), 0.0)
    total = jnp.sum(image_weights, axis=-1, keepdims=True) + jnp.sum(
        own_weights, axis=-1, keepdims=True
    )
    result = (mixed(image_weights, image_kv[:, 1]) + mixed(own_weights, near[:, 2])) / total
    result = slim(result).transpose(1, 0, 2).reshape(most * CAP, share)
    spread_out = slim(dot(put, result)).reshape(places, cores * word_rows, share)
    landed = spread_out[0]
    for step in range(1, places):
        landed = landed + to_place(spread_out[step], step)
    kept = landed[:word_rows]
    attended = kept
    if cores == 2:
        given = landed[word_rows:]
        attended = kept + lax.ppermute(given, "grp", core_swap)
    if shares > 1:
        attended = lax.all_gather(attended, "vis", axis=1, tiled=True)
    partial_words = dot(attended, out_weight).reshape(cand_local, CAP, out_weight.shape[1])
    words_out = lax.psum_scatter(partial_words, "enc", scatter_dimension=1, tiled=True)
    caption_out = slim(words + words_out)
    return (vision_rows[None], caption_out)


def solution(mesh):
    return jax.shard_map(
        on_device,
        mesh=mesh,
        in_specs=(
            P("grp", None, "enc"),
            P("enc"),
            P("enc", ("vis", "grp")),
            P(("vis", "grp"), "enc"),
            P("enc", "vis"),
            P("vis"),
            P(None, "vis", "enc"),
            P("enc", "vis"),
            P("grp", "enc", "vis"),
            P(),
            P("grp"),
        ),
        out_specs=(P("grp", None, "enc"), P("grp", "enc", "vis")),
        check_vma=False,
    )
```

```python
import functools

import jax
import jax.numpy as jnp
from jax import lax
from jax.experimental import pallas as pl
from jax.experimental.pallas import tpu as pltpu
from jax.sharding import PartitionSpec as P

DH = 256
CAP = 16
MOSTC = 12


EPSILON = 1e-06
FLOOR = -1e30


def dot(a, b):
    return jnp.dot(a, b, preferred_element_type=jnp.float32)


def wide(a):
    return a.astype(jnp.float32)


def slim(a):
    return a.astype(jnp.bfloat16)


def shifted(value, axis, step):
    count = lax.axis_size(axis)
    return lax.ppermute(value, axis, [(i, (i + step) % count) for i in range(count)])


def summed(value, axis):
    if lax.axis_size(axis) != 2:
        return lax.psum(value, axis)
    return value + shifted(value, axis, 1)


def joined(value, axis, dim):
    if lax.axis_size(axis) != 2:
        return lax.all_gather(value, axis, axis=dim, tiled=True)
    other = shifted(value, axis, 1)
    first = lax.axis_index(axis) == 0
    return jnp.concatenate(
        [jnp.where(first, value, other), jnp.where(first, other, value)], axis=dim
    )


TOKEN = (8, 128)
HBM = pl.BlockSpec(memory_space=pl.ANY)
VMEM = pl.BlockSpec(memory_space=pltpu.VMEM)
SMEM = pl.BlockSpec(memory_space=pltpu.SMEM)
LIGHT = pl.CostEstimate(flops=1024, bytes_accessed=1024, transcendentals=0)
PARAMS = pltpu.CompilerParams(vmem_limit_bytes=12 * 1024 * 1024)


def tile_of(size, most):
    return most if size % most == 0 else size


def pass_kernel(value_ref, token_ref, out_ref):
    pass


def passed(value, token):
    return pl.pallas_call(
        pass_kernel,
        in_specs=[HBM, HBM],
        out_specs=HBM,
        out_shape=jax.ShapeDtypeStruct(value.shape, value.dtype),
        input_output_aliases={0: 0},
        compiler_params=PARAMS,
        cost_estimate=LIGHT,
    )(value, token)


def hold_kernel(value_ref, *refs):
    out_ref, sem = refs[-2:]
    copy = pltpu.make_async_copy(value_ref, out_ref, sem)
    copy.start()
    copy.wait()


def held_call(value, after):
    return pl.pallas_call(
        hold_kernel,
        in_specs=[HBM] * (1 + len(after)),
        out_specs=VMEM,
        out_shape=jax.ShapeDtypeStruct(value.shape, value.dtype),
        scratch_shapes=[pltpu.SemaphoreType.DMA],
        compiler_params=PARAMS,
        cost_estimate=LIGHT,
    )(value, *after)


def up_kernel(cores, mine_ref, theirs_ref, *refs):
    weights, (out_ref, token_ref, rows_ref) = refs[:cores], refs[-3:]
    half = mine_ref.shape[0]
    units = weights[0].shape[1]
    tile = tile_of(units, 256)
    rows_ref[:half] = mine_ref[...]
    rows_ref[half:] = theirs_ref[...]
    token_ref[...] = jnp.zeros(TOKEN, jnp.float32)
    for core in range(cores):
        for first in range(0, units, tile):
            out_ref[:, core * units + first : core * units + first + tile] = slim(
                dot(rows_ref[...], weights[core][:, first : first + tile])
            )


def up_call(halves, weights, after):
    cores = len(weights)
    depth, units = weights[0].shape
    rows = 2 * halves[0].shape[0]
    return pl.pallas_call(
        functools.partial(up_kernel, cores),
        in_specs=[VMEM] * (2 + cores) + [HBM] * len(after),
        out_specs=[VMEM, VMEM],
        out_shape=[
            jax.ShapeDtypeStruct((rows, cores * units), jnp.bfloat16),
            jax.ShapeDtypeStruct(TOKEN, jnp.float32),
        ],
        scratch_shapes=[pltpu.VMEM((rows, depth), jnp.bfloat16)],
        compiler_params=PARAMS,
        cost_estimate=LIGHT,
    )(*halves, *weights, *after)


def down_kernel(cores, own_ref, other_ref, *refs):
    weights, (kept_ref, sent_ref, token_ref, total_ref) = refs[:cores], refs[-6:-2]
    hidden = refs[-2:]
    units, columns = weights[0].shape
    tile = tile_of(units, 256)
    half = kept_ref.shape[0]
    part = tile_of(columns, 1536)
    token_ref[...] = jnp.zeros(TOKEN, jnp.float32)
    order = [(core, first) for core in range(cores) for first in range(0, units, tile)]

    def fill(at):
        core, first = order[at]
        columns_at = slice(core * units + first, core * units + first + tile)
        total = wide(own_ref[:, columns_at]) + wide(other_ref[:, columns_at])
        hidden[at % 2][...] = slim(0.5 * total * (1.0 + lax.erf(total * 0.5**0.5)))

    fill(0)
    for at, (core, first) in enumerate(order):
        for start in range(0, columns, part):
            term = dot(hidden[at % 2][...], weights[core][first : first + tile, start : start + part])
            if at:
                term = total_ref[:, start : start + part] + term
            if at + 1 < len(order):
                total_ref[:, start : start + part] = term
            else:
                kept_ref[:, start : start + part] = slim(term[:half])
                sent_ref[:, start : start + part] = slim(term[half:])
        if at + 1 < len(order):
            fill(at + 1)


def down_call(own, other, weights, after):
    cores = len(weights)
    units, columns = weights[0].shape
    tile = tile_of(units, 256)
    rows = own.shape[0]
    half = jax.ShapeDtypeStruct((rows // 2, columns), jnp.bfloat16)
    return pl.pallas_call(
        functools.partial(down_kernel, cores),
        in_specs=[VMEM] * (2 + cores) + [HBM] * len(after),
        out_specs=[VMEM, VMEM, VMEM],
        out_shape=[half, half, jax.ShapeDtypeStruct(TOKEN, jnp.float32)],
        scratch_shapes=[pltpu.VMEM((rows, columns), jnp.float32)]
        + [pltpu.VMEM((rows, tile), jnp.bfloat16)] * 2,
        compiler_params=PARAMS,
        cost_estimate=LIGHT,
    )(own, other, *weights, *after)


def project_kernel(rows_ref, weight_ref, *refs):
    out_ref = refs[-1]
    columns = weight_ref.shape[1]
    part = tile_of(columns, 512)
    for first in range(0, columns, part):
        out_ref[:, first : first + part] = slim(
            dot(rows_ref[...], weight_ref[:, first : first + part])
        )


def project_call(rows, weight, after):
    return pl.pallas_call(
        project_kernel,
        in_specs=[VMEM, VMEM] + [HBM] * len(after),
        out_specs=VMEM,
        out_shape=jax.ShapeDtypeStruct((rows.shape[0], weight.shape[1]), jnp.bfloat16),
        compiler_params=PARAMS,
        cost_estimate=LIGHT,
    )(rows, weight, *after)


def image_kernel(vis_ref, own_ref, other_ref, gain_ref, weight_ref, kept_ref, sent_ref, power_ref):
    share = weight_ref.shape[2] // 2
    full = wide(own_ref[...]) + wide(other_ref[...])
    power = jnp.sum(full * full, axis=1, keepdims=True)
    scaled = slim(full * gain_ref[...])
    power_ref[...] = jnp.broadcast_to(power, power_ref.shape)
    high = slim(power)
    middle = slim(power - wide(high))
    low = slim(power - wide(high) - wide(middle))
    lane = lax.broadcasted_iota(jnp.int32, (power.shape[0], 128), 1)
    parts = jnp.where(lane == 0, wide(high), jnp.where(lane == 1, wide(middle), wide(low)))
    sent_ref[:, 2 * share :] = slim(jnp.where(lane < 3, parts, 0.0))
    vis = vis_ref[0]
    for kind in range(2):
        columns = slice(kind * share, (kind + 1) * share)
        other = pl.ds(pl.multiple_of((1 - vis) * share, share), share)
        sent_ref[:, columns] = slim(dot(scaled, weight_ref[kind + 1, :, other]))
    for kind in range(2):
        columns = slice(kind * share, (kind + 1) * share)
        mine = pl.ds(pl.multiple_of(vis * share, share), share)
        kept_ref[:, columns] = dot(scaled, weight_ref[kind + 1, :, mine])


def image_call(own, other, gain, weight, spots):
    rows = own.shape[0]
    share = weight.shape[2] // 2
    return pl.pallas_call(
        image_kernel,
        in_specs=[pl.BlockSpec(memory_space=pltpu.SMEM)] + [VMEM] * 4,
        out_specs=[VMEM] * 3,
        out_shape=[
            jax.ShapeDtypeStruct((rows, 2 * share), jnp.float32),
            jax.ShapeDtypeStruct((rows, 2 * share + 128), jnp.bfloat16),
            jax.ShapeDtypeStruct((rows, 128), jnp.float32),
        ],
        compiler_params=PARAMS,
        cost_estimate=LIGHT,
    )(spots, own, other, gain[None], weight)


def heads_kernel(vis_ref, rows_ref, weight_ref, *refs):
    sent_ref, kept_ref, token_ref = refs[-3:]
    kinds, _, inner = weight_ref.shape
    share = inner // 2
    vis = vis_ref[0]
    token_ref[...] = jnp.zeros(TOKEN, jnp.float32)
    for which, out_ref in ((1 - vis, sent_ref), (vis, kept_ref)):
        for kind in range(kinds):
            heads = pl.ds(pl.multiple_of(which * share, share), share)
            term = dot(rows_ref[...], weight_ref[kind, :, heads])
            out_ref[:, kind * share : (kind + 1) * share] = term.astype(out_ref.dtype)


def heads_call(block, weight, spots, after):
    shape = (block.shape[0], weight.shape[0] * weight.shape[2] // 2)
    return pl.pallas_call(
        heads_kernel,
        in_specs=[pl.BlockSpec(memory_space=pltpu.SMEM), VMEM, VMEM] + [HBM] * len(after),
        out_specs=[VMEM, VMEM, VMEM],
        out_shape=[
            jax.ShapeDtypeStruct(shape, jnp.bfloat16),
            jax.ShapeDtypeStruct(shape, jnp.float32),
            jax.ShapeDtypeStruct(TOKEN, jnp.float32),
        ],
        compiler_params=PARAMS,
        cost_estimate=LIGHT,
    )(spots, block, weight, *after)


def add_kernel(count, *refs):
    out_ref, token_ref = refs[-2:]
    rows = out_ref.shape[0]
    step = tile_of(rows, 32)

    def body(at, carry):
        part = pl.ds(pl.multiple_of(at * step, step), step)
        total = wide(refs[0][part])
        for ref in refs[1:count]:
            total = total + wide(ref[part])
        out_ref[part] = slim(total)
        return carry

    lax.fori_loop(0, rows // step, body, 0)
    token_ref[...] = jnp.zeros(TOKEN, jnp.float32)


def add_call(values, after):
    return pl.pallas_call(
        functools.partial(add_kernel, len(values)),
        in_specs=[VMEM] * len(values) + [HBM] * len(after),
        out_specs=[VMEM, VMEM],
        out_shape=[
            jax.ShapeDtypeStruct(values[0].shape, jnp.bfloat16),
            jax.ShapeDtypeStruct(TOKEN, jnp.float32),
        ],
        compiler_params=PARAMS,
        cost_estimate=LIGHT,
    )(*values, *after)


def message_kernel(lengths_ref, kept_ref, other_ref, *refs):
    out_ref = refs[-1]
    rows, columns = kept_ref.shape
    out_ref[:, :columns] = slim(kept_ref[...] + wide(other_ref[...]))
    row = lax.broadcasted_iota(jnp.int32, (rows, 128), 0)
    live = jnp.zeros((rows, 128), jnp.float32)
    for cand in range(rows // CAP):
        inside = (row >= cand * CAP) & (row < cand * CAP + lengths_ref[cand])
        live = jnp.where(inside, 1.0, live)
    out_ref[:, columns:] = slim(live)


def message_call(lengths, kept, other, after):
    rows, columns = kept.shape
    return pl.pallas_call(
        message_kernel,
        in_specs=[SMEM, VMEM, VMEM] + [HBM] * len(after),
        out_specs=VMEM,
        out_shape=jax.ShapeDtypeStruct((rows, columns + 128), jnp.bfloat16),
        compiler_params=PARAMS,
        cost_estimate=LIGHT,
    )(lengths, kept, other, *after)


def stack_kernel(count, *refs):
    out_ref = refs[-1]
    rows = refs[0].shape[0]
    for at in range(count):
        out_ref[at * rows : (at + 1) * rows] = refs[at][...]


def stack_call(values):
    rows, columns = values[0].shape
    return pl.pallas_call(
        functools.partial(stack_kernel, len(values)),
        in_specs=[VMEM] * len(values),
        out_specs=VMEM,
        out_shape=jax.ShapeDtypeStruct((rows * len(values), columns), values[0].dtype),
        compiler_params=PARAMS,
        cost_estimate=LIGHT,
    )(*values)


def span_of(counts_ref, group, images):
    first, end = jnp.int32(0), jnp.int32(0)
    for image in range(images):
        first = first + jnp.where(image < group, counts_ref[image], 0)
        end = end + jnp.where(image <= group, counts_ref[image], 0)
    return first, end


def row_ids(index, place, core, places, word_rows, sign):
    step = index // word_rows
    at = lax.rem(place + sign * step + places, places)
    return (at * 2 + core) * word_rows + lax.rem(index, word_rows)


def near_kernel(places, spots_ref, counts_ref, own_ref, other_ref, *refs):
    out_ref, token_ref = refs[-2:]
    near_rows = out_ref.shape[0]
    rows = own_ref.shape[0]
    place, core, group = spots_ref[1], spots_ref[2], spots_ref[4]
    first, _ = span_of(counts_ref, group, counts_ref.shape[0])
    near_id = first * CAP + lax.broadcasted_iota(jnp.int32, (near_rows, rows), 0)
    column = lax.broadcasted_iota(jnp.int32, (near_rows, rows), 1)
    total = 0.0
    for core_at, ref in ((core, own_ref), (1 - core, other_ref)):
        pick = near_id == row_ids(column, place, core_at, places, rows // places, -1)
        total = total + dot(slim(jnp.where(pick, 1.0, 0.0)), ref[...])
    out_ref[...] = slim(total)
    token_ref[...] = jnp.zeros(TOKEN, jnp.float32)


def near_call(spots, counts, own, other, places, near_rows, after):
    return pl.pallas_call(
        functools.partial(near_kernel, places),
        in_specs=[SMEM, SMEM, VMEM, VMEM] + [HBM] * len(after),
        out_specs=[VMEM, VMEM],
        out_shape=[
            jax.ShapeDtypeStruct((near_rows, own.shape[1]), jnp.bfloat16),
            jax.ShapeDtypeStruct(TOKEN, jnp.float32),
        ],
        compiler_params=PARAMS,
        cost_estimate=LIGHT,
    )(spots, counts, own, other, *after)


def across(a, b):
    return lax.dot_general(a, b, (((1,), (1,)), ((), ())), preferred_element_type=jnp.float32)


def attend_kernel(places, word_rows, width, spots_ref, counts_ref, near_ref, *refs):
    parts, outs, result_ref = refs[:6], refs[6 : 6 + places], refs[-1]
    near_rows = near_ref.shape[0]
    share = result_ref.shape[1]
    place, core, group = spots_ref[1], spots_ref[2], spots_ref[4]
    first, end = span_of(counts_ref, group, counts_ref.shape[0])
    sources = []
    for kept_ref, got_ref, power_ref in (parts[:3], parts[3:]):
        power = power_ref[:, :1] + jnp.sum(
            wide(got_ref[:, 2 * share : 2 * share + 128]), axis=1, keepdims=True
        )
        scale = lax.rsqrt(power / width + EPSILON)
        total = slim((kept_ref[...] + wide(got_ref[:, : 2 * share])) * scale)
        sources.append((total[:, :share], total[:, share:], None))
    lane = lax.broadcasted_iota(jnp.int32, (16, 128), 1)
    pick = slim(jnp.where(lane == 0, 1.0, 0.0))
    live = across(pick, near_ref[:, 3 * share :])[:1]
    shape = (near_rows, near_rows)
    own = lax.broadcasted_iota(jnp.int32, shape, 0) // CAP == lax.broadcasted_iota(jnp.int32, shape, 1) // CAP
    allowed = own & (live > 0.5)
    sources.append((near_ref[:, share : 2 * share], near_ref[:, 2 * share : 3 * share], allowed))
    for head in range(share // DH):
        columns = slice(head * DH, (head + 1) * DH)
        query = near_ref[:, columns]
        scores = []
        for keys, _, mask in sources:
            score = across(query, keys[:, columns]) * DH ** (-0.5)
            scores.append(score if mask is None else jnp.where(mask, score, FLOOR))
        top = functools.reduce(
            jnp.maximum, [jnp.max(score, axis=1, keepdims=True) for score in scores]
        )
        total, mixed = 0.0, 0.0
        for score, (_, values, mask) in zip(scores, sources):
            weights = jnp.exp(score - top)
            if mask is not None:
                weights = jnp.where(mask, weights, 0.0)
            total = total + jnp.sum(weights, axis=1, keepdims=True)
            mixed = mixed + dot(slim(weights), values[:, columns])
        result_ref[:, columns] = slim(mixed / total)
    block = 2 * word_rows
    row = lax.broadcasted_iota(jnp.int32, (block, near_rows), 0)
    near_id = first * CAP + lax.broadcasted_iota(jnp.int32, (block, near_rows), 1)
    core_at = jnp.where(row < word_rows, core, 1 - core)
    for step, out_ref in enumerate(outs):
        home = lax.rem(place + step, places)
        ids = (home * 2 + core_at) * word_rows + lax.rem(row, word_rows)
        put = (ids == near_id) & (near_id < end * CAP)
        out_ref[...] = slim(dot(slim(jnp.where(put, 1.0, 0.0)), result_ref[...]))


def attend_call(spots, counts, near, pieces, places, word_rows, width):
    share = pieces[0].shape[1] // 2
    return pl.pallas_call(
        functools.partial(attend_kernel, places, word_rows, width),
        in_specs=[SMEM, SMEM] + [VMEM] * (1 + len(pieces)),
        out_specs=[VMEM] * places,
        out_shape=[jax.ShapeDtypeStruct((2 * word_rows, share), jnp.bfloat16)] * places,
        scratch_shapes=[pltpu.VMEM((near.shape[0], share), jnp.bfloat16)],
        compiler_params=PARAMS,
        cost_estimate=LIGHT,
    )(spots, counts, near, *pieces)


def land_kernel(*refs):
    kept_ref, given_ref = refs[-2:]
    rows = kept_ref.shape[0]
    total = wide(refs[0][...])
    for ref in refs[1:-2]:
        total = total + wide(ref[...])
    kept_ref[...] = slim(total[:rows])
    given_ref[...] = slim(total[rows:])


def land_call(values):
    rows, columns = values[0].shape
    return pl.pallas_call(
        land_kernel,
        in_specs=[VMEM] * len(values),
        out_specs=[VMEM, VMEM],
        out_shape=[jax.ShapeDtypeStruct((rows // 2, columns), jnp.bfloat16)] * 2,
        compiler_params=PARAMS,
        cost_estimate=LIGHT,
    )(*values)


def output_kernel(spots_ref, kept_ref, core_ref, vis_ref, both_ref, weight_ref, mine_ref, sent_ref):
    vis, enc = spots_ref[0], spots_ref[3]
    share = kept_ref.shape[1]
    own = slim(wide(kept_ref[...]) + wide(core_ref[...]))
    other = slim(wide(vis_ref[...]) + wide(both_ref[...]))
    slots = CAP // 2
    columns = weight_ref.shape[1]
    part = tile_of(columns, 512)
    for start in range(0, columns, part):
        span = slice(start, start + part)
        total = dot(own, weight_ref[pl.ds(pl.multiple_of(vis * share, share), share), span])
        total = total + dot(other, weight_ref[pl.ds(pl.multiple_of((1 - vis) * share, share), share), span])
        firsts = range(0, total.shape[0], CAP)
        low = jnp.concatenate([total[at : at + slots] for at in firsts])
        high = jnp.concatenate([total[at + slots : at + CAP] for at in firsts])
        mine_ref[:, span] = jnp.where(enc == 0, low, high)
        sent_ref[:, span] = slim(jnp.where(enc == 0, high, low))


def output_call(spots, pieces, weight):
    shape = (pieces[0].shape[0] // 2, weight.shape[1])
    return pl.pallas_call(
        output_kernel,
        in_specs=[SMEM] + [VMEM] * 5,
        out_specs=[VMEM, VMEM],
        out_shape=[
            jax.ShapeDtypeStruct(shape, jnp.float32),
            jax.ShapeDtypeStruct(shape, jnp.bfloat16),
        ],
        compiler_params=PARAMS,
        cost_estimate=LIGHT,
    )(spots, *pieces, weight)


def on_device(
    image_tokens,
    vision_gain,
    up_weight,
    down_weight,
    project_weight,
    encoder_gain,
    qkv_weight,
    out_weight,
    captions,
    cand_counts,
    caption_lengths,
):
    vis_count = lax.axis_size("vis")
    enc_count = lax.axis_size("enc")
    groups = lax.axis_size("grp")
    vis = lax.axis_index("vis")
    group = lax.axis_index("grp")
    rows, features = image_tokens.shape[1:]
    all_features = features * enc_count
    width = captions.shape[2] * vis_count
    pair = vis_count == 2
    part_rows = rows // vis_count

    cores = 2 if groups % 2 == 0 else 1
    places = groups // cores
    place, core = group // cores, group % cores
    core_swap = [(i, i ^ 1) for i in range(groups)]
    up_weights, down_weights = [up_weight], [down_weight]
    if cores == 2:
        up_weights.append(lax.ppermute(up_weight, "grp", core_swap))
        down_weights.append(lax.ppermute(down_weight, "grp", core_swap))
        if up_weight.shape[1] % 128:
            up_weights = [jnp.concatenate(up_weights, axis=1)]
            down_weights = [jnp.concatenate(down_weights)]

    def to_place(value, step):
        return lax.ppermute(
            value, "grp", [(i, (i + step * cores) % groups) for i in range(groups)]
        )

    def mine_of(value):
        return lax.dynamic_slice_in_dim(value, vis * part_rows, part_rows, axis=0)

    def halves_of(mine, value):
        if pair and value is None:
            return [mine, shifted(mine, "vis", 1)]
        if pair:
            return [mine, lax.dynamic_slice_in_dim(value, (1 - vis) * part_rows, part_rows, axis=0)]
        if value is None:
            value = lax.all_gather(mine, "vis", axis=0, tiled=True)
        return [value[: rows // 2], value[rows // 2 :]]

    token = []

    def gated(value):
        return value + token[0][0, 0].astype(value.dtype) if token else value

    words = wide(captions)
    word_power = summed(jnp.sum(words * words, axis=-1), "vis")
    tokens = wide(image_tokens[0])
    row_total, row_squares = summed(
        jnp.stack([jnp.sum(tokens, axis=-1), jnp.sum(tokens * tokens, axis=-1)]), "enc"
    )
    mean = row_total / all_features
    spread = row_squares / all_features - mean * mean
    normed = slim(
        (tokens - mean[:, None]) * lax.rsqrt(spread + EPSILON)[:, None] * vision_gain
    )
    my_tokens = mine_of(image_tokens[0])
    my_normed = mine_of(normed)

    inner = qkv_weight.shape[2]
    heads = inner // DH
    shares = vis_count if heads % vis_count == 0 else 1
    share = inner // shares
    fast = pair and shares == 2 and cores == 2 and enc_count == 2
    spots = jnp.stack([vis, place, core, lax.axis_index("enc"), group])
    word_normed = slim(words * lax.rsqrt(word_power / width + EPSILON)[..., None] * encoder_gain)
    all_words = joined(word_normed, "enc", 1)
    cand_local = all_words.shape[0]
    word_rows = cand_local * CAP
    flat_words = all_words.reshape(word_rows, all_words.shape[2])

    def head_weights(which):
        return lax.dynamic_slice_in_dim(qkv_weight, which * share, share, axis=2)

    def heads_of(block, weight):
        return jnp.einsum("rd,kdh->rkh", block, weight, preferred_element_type=jnp.float32)

    def head_sum(values):
        if shares == 1:
            return lax.psum(values, "vis")
        return lax.psum_scatter(values, "vis", scatter_dimension=2, tiled=True)

    arrived, blocks, pres, outs, backs = {}, {}, {}, {}, {}

    def forwarded(step):
        if step < places:
            here = passed(arrived[step], token[0]) if step > 1 and token else arrived[step]
            if step + 1 < places:
                arrived[step + 1] = to_place(here, 1)
            blocks[step] = halves_of(here, None)

    def up(step, *after):
        if step < places:
            pre, token[:] = (lambda got: (got[0], [got[1]]))(
                up_call(blocks[step], up_weights, [*token, *after])
            )
            if enc_count == 2:
                pres[step] = pre, shifted(pre, "enc", 1)
            else:
                pres[step] = pre, slim(lax.psum(wide(pre), "enc") - wide(pre))

    def down(step, *after):
        if step < places:
            kept, sent, next_token = down_call(*pres[step], down_weights, [*token, *after])
            token[:] = [next_token]
            if pair:
                outs[step] = kept, shifted(sent, "vis", 1)
            else:
                out = jnp.concatenate([kept, wide(sent)])
                kept = lax.psum_scatter(out, "vis", scatter_dimension=0, tiled=True)
                outs[step] = kept, jnp.zeros_like(kept, jnp.bfloat16)

    def back(step):
        if 0 < step < places:
            parts = [*outs[step], *([backs[step - 1]] if step > 1 else [])]
            total, next_token = add_call(parts, token)
            token[:] = [next_token]
            backs[step] = to_place(total, 1)

    if places > 1:
        arrived[1] = to_place(my_normed, 1)
    if fast:
        word_sent, word_kept, word_token = heads_call(
            flat_words, qkv_weight, spots, [my_normed, my_tokens]
        )
        token[:] = [word_token]
        word_other = shifted(word_sent, "vis", 1)
    else:
        word_kept = head_sum(heads_of(flat_words, qkv_weight)).reshape(word_rows, 3 * share)
        word_other = jnp.zeros_like(word_kept, jnp.bfloat16)
    forwarded(1)
    messages = []

    def hops():
        for step in range(1, places):
            back_one = step > 1 and step == places - 1
            messages.append(
                to_place(messages[0], -1) if back_one else to_place(messages[-1], 1)
            )

    blocks[0] = halves_of(my_normed, normed)
    if fast:
        up_weights[-1] = held_call(up_weights[-1], token)
        token[:] = [up_weights[-1]]
    forwarded(2)
    messages.append(message_call(caption_lengths, word_kept, word_other, token))
    up(1, messages[0])
    hops()
    if fast:
        down_weights[-1] = held_call(down_weights[-1], token)
    forwarded(3)
    up(2, blocks[places - 1][0], *messages[1:2])
    down(1)
    up(3)
    back(1)
    down(2, *messages[2:])
    up(0, *[backs[step] for step in backs])
    for step in range(4, places):
        forwarded(step)
        up(step)
        down(step - 1)
    down(places - 1)
    for step in range(2, places - 1):
        back(step)
    down(0)
    word_block = stack_call(messages)
    if cores == 2:
        word_blocks = [word_block, lax.ppermute(word_block, "grp", core_swap)]
    else:
        word_blocks = [word_block]
    if places > 2:
        back(places - 1)

    home = [my_tokens, *outs[0], *([backs[places - 1]] if places > 1 else [])]
    cands = groups * cand_local
    most = min(MOSTC, cands)
    if fast:
        near, near_token = near_call(
            spots, cand_counts, *word_blocks, places, most * CAP, token
        )
        final_weight = held_call(out_weight, [near_token])
        my_vision, _ = add_call(home, [near_token, final_weight])
        other_vision = shifted(my_vision, "vis", 1)
        pieces = []
        for block in (my_vision, other_vision):
            partial = project_call(block, project_weight, [])
            full = shifted(partial, "enc", 1)
            pieces.append(image_call(partial, full, encoder_gain, qkv_weight, spots))
        got = [shifted(sent, "vis", 1) for _, sent, _ in pieces]
        parts = []
        for here, there in ((0, 1), (1, 0)):
            parts += [pieces[here][0], got[there], pieces[here][2]]
        placed = attend_call(spots, cand_counts, near, parts, places, word_rows, width)
        landed = [to_place(part, step) if step else part for step, part in enumerate(placed)]
        kept, given = land_call(landed)
        across_both = [
            (v * groups + i, (1 - v) * groups + (i ^ 1)) for v in range(2) for i in range(groups)
        ]
        from_core = lax.ppermute(given, "grp", core_swap)
        from_both = lax.ppermute(given, ("vis", "grp"), across_both)
        from_vis = shifted(kept, "vis", 1)
        mine, sent = output_call(spots, [kept, from_core, from_vis, from_both], final_weight)
        words_out = (mine + wide(shifted(sent, "enc", 1))).reshape(words.shape)
        vision_rows = jnp.where(
            vis == 0,
            jnp.concatenate([my_vision, other_vision]),
            jnp.concatenate([other_vision, my_vision]),
        )
        return (vision_rows[None], slim(words + words_out))
    my_vision = slim(sum([wide(part) for part in home]))

    ends = jnp.cumsum(cand_counts)
    start = ends[group] - cand_counts[group]
    near_ids = start * CAP + jnp.arange(most * CAP, dtype=jnp.int32)
    owned = near_ids < ends[group] * CAP

    def ids_of(core_at, sign):
        steps = jnp.arange(places, dtype=jnp.int32)[:, None]
        first = ((place + sign * steps) % places * cores + core_at) * word_rows
        return (first + jnp.arange(word_rows, dtype=jnp.int32)[None]).reshape(-1)

    core_order = [core, 1 - core][:cores]
    near = 0.0
    for core_at, block in zip(core_order, word_blocks):
        pick = near_ids[:, None] == ids_of(core_at, -1)[None, :]
        near = near + dot(pick.astype(jnp.bfloat16), block)
    near = slim(near)
    place_ids = jnp.concatenate(
        [ids_of(core_at, 1).reshape(places, word_rows) for core_at in core_order], axis=1
    ).reshape(-1)
    put = slim((place_ids[:, None] == near_ids[None, :]) & owned[None, :])
    def embed(block):
        partial = dot(block, project_weight)
        if enc_count == 2:
            full = partial + wide(shifted(slim(partial), "enc", 1))
        else:
            full = lax.psum(partial, "enc")
        return slim(full * encoder_gain), jnp.sum(full * full, axis=-1)

    vision_rows = joined(my_vision, "vis", 0)
    scaled, power = embed(vision_rows)
    total = head_sum(heads_of(scaled, qkv_weight[1:]))
    power = lax.psum(power, "vis")
    image_kv = slim(total * lax.rsqrt(power / width + EPSILON)[:, None, None])

    live = near[:, 3 * share] > 0
    near = near[:, : 3 * share].reshape(most * CAP, 3, share // DH, DH)
    row_cand = jnp.arange(most * CAP, dtype=jnp.int32) // CAP
    own_allowed = (row_cand[:, None] == row_cand[None, :]) & live[None, :]
    image_kv = image_kv.reshape(rows, 2, share // DH, DH)
    query = near[:, 0]

    def scores_of(keys):
        return jnp.einsum(
            "qhd,khd->hqk", query, keys, preferred_element_type=jnp.float32
        ) * DH ** (-0.5)

    def mixed(weights, values):
        return jnp.einsum(
            "hqk,khd->hqd", slim(weights), values, preferred_element_type=jnp.float32
        )

    image_scores = scores_of(image_kv[:, 0])
    own_scores = jnp.where(own_allowed[None], scores_of(near[:, 1]), FLOOR)
    top = jnp.maximum(
        jnp.max(image_scores, axis=-1, keepdims=True), jnp.max(own_scores, axis=-1, keepdims=True)
    )
    image_weights = jnp.exp(image_scores - top)
    own_weights = jnp.where(own_allowed[None], jnp.exp(own_scores - top), 0.0)
    total = jnp.sum(image_weights, axis=-1, keepdims=True) + jnp.sum(
        own_weights, axis=-1, keepdims=True
    )
    result = (mixed(image_weights, image_kv[:, 1]) + mixed(own_weights, near[:, 2])) / total
    result = slim(result).transpose(1, 0, 2).reshape(most * CAP, share)
    spread_out = slim(dot(put, result)).reshape(places, cores * word_rows, share)
    landed = spread_out[0]
    for step in range(1, places):
        landed = landed + to_place(spread_out[step], step)
    kept = landed[:word_rows]
    attended = kept
    if cores == 2:
        given = landed[word_rows:]
        attended = kept + lax.ppermute(given, "grp", core_swap)
    if shares > 1:
        attended = lax.all_gather(attended, "vis", axis=1, tiled=True)
    partial_words = dot(attended, out_weight).reshape(cand_local, CAP, out_weight.shape[1])
    words_out = lax.psum_scatter(partial_words, "enc", scatter_dimension=1, tiled=True)
    caption_out = slim(words + words_out)
    return (vision_rows[None], caption_out)


def solution(mesh):
    return jax.shard_map(
        on_device,
        mesh=mesh,
        in_specs=(
            P("grp", None, "enc"),
            P("enc"),
            P("enc", ("vis", "grp")),
            P(("vis", "grp"), "enc"),
            P("enc", "vis"),
            P("vis"),
            P(None, "vis", "enc"),
            P("enc", "vis"),
            P("grp", "enc", "vis"),
            P(),
            P("grp"),
        ),
        out_specs=(P("grp", None, "enc"), P("grp", "enc", "vis")),
        check_vma=False,
    )
```

```python
import functools

import jax
import jax.numpy as jnp
from jax import lax
from jax.experimental import pallas as pl
from jax.experimental.pallas import tpu as pltpu
from jax.sharding import PartitionSpec as P

DH = 256
CAP = 16
MOSTC = 12


EPSILON = 1e-06
FLOOR = -1e30


def dot(a, b):
    return jnp.dot(a, b, preferred_element_type=jnp.float32)


def wide(a):
    return a.astype(jnp.float32)


def slim(a):
    return a.astype(jnp.bfloat16)


def shifted(value, axis, step):
    count = lax.axis_size(axis)
    return lax.ppermute(value, axis, [(i, (i + step) % count) for i in range(count)])


def summed(value, axis):
    if lax.axis_size(axis) != 2:
        return lax.psum(value, axis)
    return value + shifted(value, axis, 1)


def joined(value, axis, dim):
    if lax.axis_size(axis) != 2:
        return lax.all_gather(value, axis, axis=dim, tiled=True)
    other = shifted(value, axis, 1)
    first = lax.axis_index(axis) == 0
    return jnp.concatenate(
        [jnp.where(first, value, other), jnp.where(first, other, value)], axis=dim
    )


TOKEN = (8, 128)
HBM = pl.BlockSpec(memory_space=pl.ANY)
VMEM = pl.BlockSpec(memory_space=pltpu.VMEM)
SMEM = pl.BlockSpec(memory_space=pltpu.SMEM)
LIGHT = pl.CostEstimate(flops=1024, bytes_accessed=1024, transcendentals=0)
PARAMS = pltpu.CompilerParams(vmem_limit_bytes=12 * 1024 * 1024)


def tile_of(size, most):
    return most if size % most == 0 else size


def pass_kernel(value_ref, token_ref, out_ref):
    pass


def passed(value, token):
    return pl.pallas_call(
        pass_kernel,
        in_specs=[HBM, HBM],
        out_specs=HBM,
        out_shape=jax.ShapeDtypeStruct(value.shape, value.dtype),
        input_output_aliases={0: 0},
        compiler_params=PARAMS,
        cost_estimate=LIGHT,
    )(value, token)


def hold_kernel(value_ref, *refs):
    out_ref, sem = refs[-2:]
    copy = pltpu.make_async_copy(value_ref, out_ref, sem)
    copy.start()
    copy.wait()


def held_call(value, after):
    return pl.pallas_call(
        hold_kernel,
        in_specs=[HBM] * (1 + len(after)),
        out_specs=VMEM,
        out_shape=jax.ShapeDtypeStruct(value.shape, value.dtype),
        scratch_shapes=[pltpu.SemaphoreType.DMA],
        compiler_params=PARAMS,
        cost_estimate=LIGHT,
    )(value, *after)


def up_kernel(cores, mine_ref, theirs_ref, *refs):
    weights, (out_ref, token_ref, rows_ref) = refs[:cores], refs[-3:]
    half = mine_ref.shape[0]
    units = weights[0].shape[1]
    tile = tile_of(units, 256)
    rows_ref[:half] = mine_ref[...]
    rows_ref[half:] = theirs_ref[...]
    token_ref[...] = jnp.zeros(TOKEN, jnp.float32)
    for core in range(cores):
        for first in range(0, units, tile):
            out_ref[:, core * units + first : core * units + first + tile] = slim(
                dot(rows_ref[...], weights[core][:, first : first + tile])
            )


def up_call(halves, weights, after):
    cores = len(weights)
    depth, units = weights[0].shape
    rows = 2 * halves[0].shape[0]
    return pl.pallas_call(
        functools.partial(up_kernel, cores),
        in_specs=[VMEM] * (2 + cores) + [HBM] * len(after),
        out_specs=[VMEM, VMEM],
        out_shape=[
            jax.ShapeDtypeStruct((rows, cores * units), jnp.bfloat16),
            jax.ShapeDtypeStruct(TOKEN, jnp.float32),
        ],
        scratch_shapes=[pltpu.VMEM((rows, depth), jnp.bfloat16)],
        compiler_params=PARAMS,
        cost_estimate=LIGHT,
    )(*halves, *weights, *after)


def down_kernel(cores, own_ref, other_ref, *refs):
    weights, (kept_ref, sent_ref, token_ref, total_ref) = refs[:cores], refs[-6:-2]
    hidden = refs[-2:]
    units, columns = weights[0].shape
    tile = tile_of(units, 256)
    half = kept_ref.shape[0]
    part = tile_of(columns, 1536)
    token_ref[...] = jnp.zeros(TOKEN, jnp.float32)
    order = [(core, first) for core in range(cores) for first in range(0, units, tile)]

    def fill(at):
        core, first = order[at]
        columns_at = slice(core * units + first, core * units + first + tile)
        total = wide(own_ref[:, columns_at]) + wide(other_ref[:, columns_at])
        hidden[at % 2][...] = slim(0.5 * total * (1.0 + lax.erf(total * 0.5**0.5)))

    fill(0)
    for at, (core, first) in enumerate(order):
        for start in range(0, columns, part):
            term = dot(hidden[at % 2][...], weights[core][first : first + tile, start : start + part])
            if at:
                term = total_ref[:, start : start + part] + term
            if at + 1 < len(order):
                total_ref[:, start : start + part] = term
            else:
                kept_ref[:, start : start + part] = slim(term[:half])
                sent_ref[:, start : start + part] = slim(term[half:])
        if at + 1 < len(order):
            fill(at + 1)


def down_call(own, other, weights, after):
    cores = len(weights)
    units, columns = weights[0].shape
    tile = tile_of(units, 256)
    rows = own.shape[0]
    half = jax.ShapeDtypeStruct((rows // 2, columns), jnp.bfloat16)
    return pl.pallas_call(
        functools.partial(down_kernel, cores),
        in_specs=[VMEM] * (2 + cores) + [HBM] * len(after),
        out_specs=[VMEM, VMEM, VMEM],
        out_shape=[half, half, jax.ShapeDtypeStruct(TOKEN, jnp.float32)],
        scratch_shapes=[pltpu.VMEM((rows, columns), jnp.float32)]
        + [pltpu.VMEM((rows, tile), jnp.bfloat16)] * 2,
        compiler_params=PARAMS,
        cost_estimate=LIGHT,
    )(own, other, *weights, *after)


def project_kernel(rows_ref, weight_ref, *refs):
    out_ref = refs[-1]
    columns = weight_ref.shape[1]
    part = tile_of(columns, 512)
    for first in range(0, columns, part):
        out_ref[:, first : first + part] = slim(
            dot(rows_ref[...], weight_ref[:, first : first + part])
        )


def project_call(rows, weight, after):
    return pl.pallas_call(
        project_kernel,
        in_specs=[VMEM, VMEM] + [HBM] * len(after),
        out_specs=VMEM,
        out_shape=jax.ShapeDtypeStruct((rows.shape[0], weight.shape[1]), jnp.bfloat16),
        compiler_params=PARAMS,
        cost_estimate=LIGHT,
    )(rows, weight, *after)


def image_kernel(vis_ref, own_ref, other_ref, gain_ref, weight_ref, kept_ref, sent_ref, power_ref):
    share = weight_ref.shape[2] // 2
    full = wide(own_ref[...]) + wide(other_ref[...])
    power = jnp.sum(full * full, axis=1, keepdims=True)
    scaled = slim(full * gain_ref[...])
    power_ref[...] = jnp.broadcast_to(power, power_ref.shape)
    high = slim(power)
    middle = slim(power - wide(high))
    low = slim(power - wide(high) - wide(middle))
    lane = lax.broadcasted_iota(jnp.int32, (power.shape[0], 128), 1)
    parts = jnp.where(lane == 0, wide(high), jnp.where(lane == 1, wide(middle), wide(low)))
    sent_ref[:, 2 * share :] = slim(jnp.where(lane < 3, parts, 0.0))
    vis = vis_ref[0]
    for kind in range(2):
        columns = slice(kind * share, (kind + 1) * share)
        other = pl.ds(pl.multiple_of((1 - vis) * share, share), share)
        sent_ref[:, columns] = slim(dot(scaled, weight_ref[kind + 1, :, other]))
    for kind in range(2):
        columns = slice(kind * share, (kind + 1) * share)
        mine = pl.ds(pl.multiple_of(vis * share, share), share)
        kept_ref[:, columns] = dot(scaled, weight_ref[kind + 1, :, mine])


def image_call(own, other, gain, weight, spots):
    rows = own.shape[0]
    share = weight.shape[2] // 2
    return pl.pallas_call(
        image_kernel,
        in_specs=[pl.BlockSpec(memory_space=pltpu.SMEM)] + [VMEM] * 4,
        out_specs=[VMEM] * 3,
        out_shape=[
            jax.ShapeDtypeStruct((rows, 2 * share), jnp.float32),
            jax.ShapeDtypeStruct((rows, 2 * share + 128), jnp.bfloat16),
            jax.ShapeDtypeStruct((rows, 128), jnp.float32),
        ],
        compiler_params=PARAMS,
        cost_estimate=LIGHT,
    )(spots, own, other, gain[None], weight)


def heads_kernel(vis_ref, rows_ref, weight_ref, *refs):
    sent_ref, kept_ref, token_ref = refs[-3:]
    kinds, _, inner = weight_ref.shape
    share = inner // 2
    vis = vis_ref[0]
    token_ref[...] = jnp.zeros(TOKEN, jnp.float32)
    for which, out_ref in ((1 - vis, sent_ref), (vis, kept_ref)):
        for kind in range(kinds):
            heads = pl.ds(pl.multiple_of(which * share, share), share)
            term = dot(rows_ref[...], weight_ref[kind, :, heads])
            out_ref[:, kind * share : (kind + 1) * share] = term.astype(out_ref.dtype)


def heads_call(block, weight, spots, after):
    shape = (block.shape[0], weight.shape[0] * weight.shape[2] // 2)
    return pl.pallas_call(
        heads_kernel,
        in_specs=[pl.BlockSpec(memory_space=pltpu.SMEM), VMEM, VMEM] + [HBM] * len(after),
        out_specs=[VMEM, VMEM, VMEM],
        out_shape=[
            jax.ShapeDtypeStruct(shape, jnp.bfloat16),
            jax.ShapeDtypeStruct(shape, jnp.float32),
            jax.ShapeDtypeStruct(TOKEN, jnp.float32),
        ],
        compiler_params=PARAMS,
        cost_estimate=LIGHT,
    )(spots, block, weight, *after)


def add_kernel(count, *refs):
    out_ref, token_ref = refs[-2:]
    rows = out_ref.shape[0]
    step = tile_of(rows, 32)

    def body(at, carry):
        part = pl.ds(pl.multiple_of(at * step, step), step)
        total = wide(refs[0][part])
        for ref in refs[1:count]:
            total = total + wide(ref[part])
        out_ref[part] = slim(total)
        return carry

    lax.fori_loop(0, rows // step, body, 0)
    token_ref[...] = jnp.zeros(TOKEN, jnp.float32)


def add_call(values, after):
    return pl.pallas_call(
        functools.partial(add_kernel, len(values)),
        in_specs=[VMEM] * len(values) + [HBM] * len(after),
        out_specs=[VMEM, VMEM],
        out_shape=[
            jax.ShapeDtypeStruct(values[0].shape, jnp.bfloat16),
            jax.ShapeDtypeStruct(TOKEN, jnp.float32),
        ],
        compiler_params=PARAMS,
        cost_estimate=LIGHT,
    )(*values, *after)


def message_kernel(lengths_ref, kept_ref, other_ref, *refs):
    out_ref = refs[-1]
    rows, columns = kept_ref.shape
    out_ref[:, :columns] = slim(kept_ref[...] + wide(other_ref[...]))
    row = lax.broadcasted_iota(jnp.int32, (rows, 128), 0)
    live = jnp.zeros((rows, 128), jnp.float32)
    for cand in range(rows // CAP):
        inside = (row >= cand * CAP) & (row < cand * CAP + lengths_ref[cand])
        live = jnp.where(inside, 1.0, live)
    out_ref[:, columns:] = slim(live)


def message_call(lengths, kept, other, after):
    rows, columns = kept.shape
    return pl.pallas_call(
        message_kernel,
        in_specs=[SMEM, VMEM, VMEM] + [HBM] * len(after),
        out_specs=VMEM,
        out_shape=jax.ShapeDtypeStruct((rows, columns + 128), jnp.bfloat16),
        compiler_params=PARAMS,
        cost_estimate=LIGHT,
    )(lengths, kept, other, *after)


def stack_kernel(count, *refs):
    out_ref = refs[-1]
    rows = refs[0].shape[0]
    for at in range(count):
        out_ref[at * rows : (at + 1) * rows] = refs[at][...]


def stack_call(values):
    rows, columns = values[0].shape
    return pl.pallas_call(
        functools.partial(stack_kernel, len(values)),
        in_specs=[VMEM] * len(values),
        out_specs=VMEM,
        out_shape=jax.ShapeDtypeStruct((rows * len(values), columns), values[0].dtype),
        compiler_params=PARAMS,
        cost_estimate=LIGHT,
    )(*values)


def span_of(counts_ref, group, images):
    first, end = jnp.int32(0), jnp.int32(0)
    for image in range(images):
        first = first + jnp.where(image < group, counts_ref[image], 0)
        end = end + jnp.where(image <= group, counts_ref[image], 0)
    return first, end


def row_ids(index, place, core, places, word_rows, sign):
    step = index // word_rows
    at = lax.rem(place + sign * step + places, places)
    return (at * 2 + core) * word_rows + lax.rem(index, word_rows)


def near_kernel(places, spots_ref, counts_ref, own_ref, other_ref, *refs):
    out_ref, token_ref = refs[-2:]
    near_rows = out_ref.shape[0]
    rows = own_ref.shape[0]
    place, core, group = spots_ref[1], spots_ref[2], spots_ref[4]
    first, _ = span_of(counts_ref, group, counts_ref.shape[0])
    near_id = first * CAP + lax.broadcasted_iota(jnp.int32, (near_rows, rows), 0)
    column = lax.broadcasted_iota(jnp.int32, (near_rows, rows), 1)
    total = 0.0
    for core_at, ref in ((core, own_ref), (1 - core, other_ref)):
        pick = near_id == row_ids(column, place, core_at, places, rows // places, -1)
        total = total + dot(slim(jnp.where(pick, 1.0, 0.0)), ref[...])
    out_ref[...] = slim(total)
    token_ref[...] = jnp.zeros(TOKEN, jnp.float32)


def near_call(spots, counts, own, other, places, near_rows, after):
    return pl.pallas_call(
        functools.partial(near_kernel, places),
        in_specs=[SMEM, SMEM, VMEM, VMEM] + [HBM] * len(after),
        out_specs=[VMEM, VMEM],
        out_shape=[
            jax.ShapeDtypeStruct((near_rows, own.shape[1]), jnp.bfloat16),
            jax.ShapeDtypeStruct(TOKEN, jnp.float32),
        ],
        compiler_params=PARAMS,
        cost_estimate=LIGHT,
    )(spots, counts, own, other, *after)


def across(a, b):
    return lax.dot_general(a, b, (((1,), (1,)), ((), ())), preferred_element_type=jnp.float32)


def attend_kernel(places, word_rows, width, spots_ref, counts_ref, near_ref, *refs):
    parts, outs, result_ref = refs[:6], refs[-1 - places : -1], refs[-1]
    near_rows = near_ref.shape[0]
    share = result_ref.shape[1]
    place, core, group = spots_ref[1], spots_ref[2], spots_ref[4]
    first, end = span_of(counts_ref, group, counts_ref.shape[0])
    sources = []
    for kept_ref, got_ref, power_ref in (parts[:3], parts[3:]):
        power = power_ref[:, :1] + jnp.sum(
            wide(got_ref[:, 2 * share : 2 * share + 128]), axis=1, keepdims=True
        )
        scale = lax.rsqrt(power / width + EPSILON)
        total = slim((kept_ref[...] + wide(got_ref[:, : 2 * share])) * scale)
        sources.append((total[:, :share], total[:, share:], None))
    lane = lax.broadcasted_iota(jnp.int32, (16, 128), 1)
    pick = slim(jnp.where(lane == 0, 1.0, 0.0))
    live = across(pick, near_ref[:, 3 * share :])[:1]
    shape = (near_rows, near_rows)
    own = lax.broadcasted_iota(jnp.int32, shape, 0) // CAP == lax.broadcasted_iota(jnp.int32, shape, 1) // CAP
    allowed = own & (live > 0.5)
    sources.append((near_ref[:, share : 2 * share], near_ref[:, 2 * share : 3 * share], allowed))
    for head in range(share // DH):
        columns = slice(head * DH, (head + 1) * DH)
        query = near_ref[:, columns]
        scores = []
        for keys, _, mask in sources:
            score = across(query, keys[:, columns]) * DH ** (-0.5)
            scores.append(score if mask is None else jnp.where(mask, score, FLOOR))
        top = functools.reduce(
            jnp.maximum, [jnp.max(score, axis=1, keepdims=True) for score in scores]
        )
        total, mixed = 0.0, 0.0
        for score, (_, values, mask) in zip(scores, sources):
            weights = jnp.exp(score - top)
            if mask is not None:
                weights = jnp.where(mask, weights, 0.0)
            total = total + jnp.sum(weights, axis=1, keepdims=True)
            mixed = mixed + dot(slim(weights), values[:, columns])
        result_ref[:, columns] = slim(mixed / total)
    block = 2 * word_rows
    row = lax.broadcasted_iota(jnp.int32, (block, near_rows), 0)
    near_id = first * CAP + lax.broadcasted_iota(jnp.int32, (block, near_rows), 1)
    core_at = jnp.where(row < word_rows, core, 1 - core)
    for step, out_ref in enumerate(outs):
        home = lax.rem(place + step, places)
        ids = (home * 2 + core_at) * word_rows + lax.rem(row, word_rows)
        put = (ids == near_id) & (near_id < end * CAP)
        out_ref[...] = slim(dot(slim(jnp.where(put, 1.0, 0.0)), result_ref[...]))


def attend_call(spots, counts, near, pieces, places, word_rows, width, after):
    share = pieces[0].shape[1] // 2
    return pl.pallas_call(
        functools.partial(attend_kernel, places, word_rows, width),
        in_specs=[SMEM, SMEM] + [VMEM] * (1 + len(pieces)) + [HBM] * len(after),
        out_specs=[VMEM] * places,
        out_shape=[jax.ShapeDtypeStruct((2 * word_rows, share), jnp.bfloat16)] * places,
        scratch_shapes=[pltpu.VMEM((near.shape[0], share), jnp.bfloat16)],
        compiler_params=PARAMS,
        cost_estimate=LIGHT,
    )(spots, counts, near, *pieces, *after)


def land_kernel(*refs):
    kept_ref, given_ref = refs[-2:]
    rows = kept_ref.shape[0]
    total = wide(refs[0][...])
    for ref in refs[1:-2]:
        total = total + wide(ref[...])
    kept_ref[...] = slim(total[:rows])
    given_ref[...] = slim(total[rows:])


def land_call(values):
    rows, columns = values[0].shape
    return pl.pallas_call(
        land_kernel,
        in_specs=[VMEM] * len(values),
        out_specs=[VMEM, VMEM],
        out_shape=[jax.ShapeDtypeStruct((rows // 2, columns), jnp.bfloat16)] * 2,
        compiler_params=PARAMS,
        cost_estimate=LIGHT,
    )(*values)


def output_kernel(spots_ref, kept_ref, core_ref, vis_ref, both_ref, weight_ref, mine_ref, sent_ref):
    vis, enc = spots_ref[0], spots_ref[3]
    share = kept_ref.shape[1]
    own = slim(wide(kept_ref[...]) + wide(core_ref[...]))
    other = slim(wide(vis_ref[...]) + wide(both_ref[...]))
    slots = CAP // 2
    columns = weight_ref.shape[1]
    part = tile_of(columns, 512)
    for start in range(0, columns, part):
        span = slice(start, start + part)
        total = dot(own, weight_ref[pl.ds(pl.multiple_of(vis * share, share), share), span])
        total = total + dot(other, weight_ref[pl.ds(pl.multiple_of((1 - vis) * share, share), share), span])
        firsts = range(0, total.shape[0], CAP)
        low = jnp.concatenate([total[at : at + slots] for at in firsts])
        high = jnp.concatenate([total[at + slots : at + CAP] for at in firsts])
        mine_ref[:, span] = jnp.where(enc == 0, low, high)
        sent_ref[:, span] = slim(jnp.where(enc == 0, high, low))


def output_call(spots, pieces, weight):
    shape = (pieces[0].shape[0] // 2, weight.shape[1])
    return pl.pallas_call(
        output_kernel,
        in_specs=[SMEM] + [VMEM] * 5,
        out_specs=[VMEM, VMEM],
        out_shape=[
            jax.ShapeDtypeStruct(shape, jnp.float32),
            jax.ShapeDtypeStruct(shape, jnp.bfloat16),
        ],
        compiler_params=PARAMS,
        cost_estimate=LIGHT,
    )(spots, *pieces, weight)


def on_device(
    image_tokens,
    vision_gain,
    up_weight,
    down_weight,
    project_weight,
    encoder_gain,
    qkv_weight,
    out_weight,
    captions,
    cand_counts,
    caption_lengths,
):
    vis_count = lax.axis_size("vis")
    enc_count = lax.axis_size("enc")
    groups = lax.axis_size("grp")
    vis = lax.axis_index("vis")
    group = lax.axis_index("grp")
    rows, features = image_tokens.shape[1:]
    all_features = features * enc_count
    width = captions.shape[2] * vis_count
    pair = vis_count == 2
    part_rows = rows // vis_count

    cores = 2 if groups % 2 == 0 else 1
    places = groups // cores
    place, core = group // cores, group % cores
    core_swap = [(i, i ^ 1) for i in range(groups)]
    up_weights, down_weights = [up_weight], [down_weight]
    if cores == 2:
        up_weights.append(lax.ppermute(up_weight, "grp", core_swap))
        down_weights.append(lax.ppermute(down_weight, "grp", core_swap))
        if up_weight.shape[1] % 128:
            up_weights = [jnp.concatenate(up_weights, axis=1)]
            down_weights = [jnp.concatenate(down_weights)]

    def to_place(value, step):
        return lax.ppermute(
            value, "grp", [(i, (i + step * cores) % groups) for i in range(groups)]
        )

    def mine_of(value):
        return lax.dynamic_slice_in_dim(value, vis * part_rows, part_rows, axis=0)

    def halves_of(mine, value):
        if pair and value is None:
            return [mine, shifted(mine, "vis", 1)]
        if pair:
            return [mine, lax.dynamic_slice_in_dim(value, (1 - vis) * part_rows, part_rows, axis=0)]
        if value is None:
            value = lax.all_gather(mine, "vis", axis=0, tiled=True)
        return [value[: rows // 2], value[rows // 2 :]]

    token = []

    def gated(value):
        return value + token[0][0, 0].astype(value.dtype) if token else value

    words = wide(captions)
    word_power = summed(jnp.sum(words * words, axis=-1), "vis")
    tokens = wide(image_tokens[0])
    row_total, row_squares = summed(
        jnp.stack([jnp.sum(tokens, axis=-1), jnp.sum(tokens * tokens, axis=-1)]), "enc"
    )
    mean = row_total / all_features
    spread = row_squares / all_features - mean * mean
    normed = slim(
        (tokens - mean[:, None]) * lax.rsqrt(spread + EPSILON)[:, None] * vision_gain
    )
    my_tokens = mine_of(image_tokens[0])
    my_normed = mine_of(normed)

    inner = qkv_weight.shape[2]
    heads = inner // DH
    shares = vis_count if heads % vis_count == 0 else 1
    share = inner // shares
    fast = pair and shares == 2 and cores == 2 and enc_count == 2
    spots = jnp.stack([vis, place, core, lax.axis_index("enc"), group])
    word_normed = slim(words * lax.rsqrt(word_power / width + EPSILON)[..., None] * encoder_gain)
    all_words = joined(word_normed, "enc", 1)
    cand_local = all_words.shape[0]
    word_rows = cand_local * CAP
    flat_words = all_words.reshape(word_rows, all_words.shape[2])

    def head_weights(which):
        return lax.dynamic_slice_in_dim(qkv_weight, which * share, share, axis=2)

    def heads_of(block, weight):
        return jnp.einsum("rd,kdh->rkh", block, weight, preferred_element_type=jnp.float32)

    def head_sum(values):
        if shares == 1:
            return lax.psum(values, "vis")
        return lax.psum_scatter(values, "vis", scatter_dimension=2, tiled=True)

    arrived, blocks, pres, outs, backs = {}, {}, {}, {}, {}

    def forwarded(step):
        if step < places:
            here = passed(arrived[step], token[0]) if step > 1 and token else arrived[step]
            if step + 1 < places:
                arrived[step + 1] = to_place(here, 1)
            blocks[step] = halves_of(here, None)

    def up(step, *after):
        if step < places:
            pre, token[:] = (lambda got: (got[0], [got[1]]))(
                up_call(blocks[step], up_weights, [*token, *after])
            )
            if enc_count == 2:
                pres[step] = pre, shifted(pre, "enc", 1)
            else:
                pres[step] = pre, slim(lax.psum(wide(pre), "enc") - wide(pre))

    def down(step, *after):
        if step < places:
            kept, sent, next_token = down_call(*pres[step], down_weights, [*token, *after])
            token[:] = [next_token]
            if pair:
                outs[step] = kept, shifted(sent, "vis", 1)
            else:
                out = jnp.concatenate([kept, wide(sent)])
                kept = lax.psum_scatter(out, "vis", scatter_dimension=0, tiled=True)
                outs[step] = kept, jnp.zeros_like(kept, jnp.bfloat16)

    def back(step):
        if 0 < step < places:
            parts = [*outs[step], *([backs[step - 1]] if step > 1 else [])]
            total, next_token = add_call(parts, token)
            token[:] = [next_token]
            backs[step] = to_place(total, 1)

    if places > 1:
        arrived[1] = to_place(my_normed, 1)
    if fast:
        word_sent, word_kept, word_token = heads_call(
            flat_words, qkv_weight, spots, [my_normed, my_tokens]
        )
        token[:] = [word_token]
        word_other = shifted(word_sent, "vis", 1)
    else:
        word_kept = head_sum(heads_of(flat_words, qkv_weight)).reshape(word_rows, 3 * share)
        word_other = jnp.zeros_like(word_kept, jnp.bfloat16)
    forwarded(1)
    messages = []

    def hops():
        for step in range(1, places):
            back_one = step > 1 and step == places - 1
            messages.append(
                to_place(messages[0], -1) if back_one else to_place(messages[-1], 1)
            )

    blocks[0] = halves_of(my_normed, normed)
    if fast:
        up_weights[-1] = held_call(up_weights[-1], token)
    up(0)
    forwarded(2)
    messages.append(message_call(caption_lengths, word_kept, word_other, token))
    up(1, messages[0])
    hops()
    if fast:
        down_weights[-1] = held_call(down_weights[-1], token)
    down(0)
    forwarded(3)
    up(2, blocks[places - 1][0], *messages[1:2])
    down(1)
    up(3)
    down(2, *messages[2:])
    back(1)
    for step in range(4, places):
        forwarded(step)
        up(step)
        down(step - 1)
    down(places - 1)
    word_block = stack_call(messages)
    if cores == 2:
        word_blocks = [word_block, lax.ppermute(word_block, "grp", core_swap)]
    else:
        word_blocks = [word_block]
    for step in range(2, places):
        back(step)

    home = [my_tokens, *outs[0], *([backs[places - 1]] if places > 1 else [])]
    cands = groups * cand_local
    most = min(MOSTC, cands)
    if fast:
        near, near_token = near_call(
            spots, cand_counts, *word_blocks, places, most * CAP, token
        )
        my_vision, _ = add_call(home, [near_token])
        other_vision = shifted(my_vision, "vis", 1)
        pieces = []
        for block in (my_vision, other_vision):
            partial = project_call(block, project_weight, [])
            full = shifted(partial, "enc", 1)
            pieces.append(image_call(partial, full, encoder_gain, qkv_weight, spots))
        got = [shifted(sent, "vis", 1) for _, sent, _ in pieces]
        parts = []
        for here, there in ((0, 1), (1, 0)):
            parts += [pieces[here][0], got[there], pieces[here][2]]
        final_weight = held_call(out_weight, [pieces[1][1]])
        placed = attend_call(
            spots, cand_counts, near, parts, places, word_rows, width, [final_weight]
        )
        landed = [to_place(part, step) if step else part for step, part in enumerate(placed)]
        kept, given = land_call(landed)
        across_both = [
            (v * groups + i, (1 - v) * groups + (i ^ 1)) for v in range(2) for i in range(groups)
        ]
        from_core = lax.ppermute(given, "grp", core_swap)
        from_both = lax.ppermute(given, ("vis", "grp"), across_both)
        from_vis = shifted(kept, "vis", 1)
        mine, sent = output_call(spots, [kept, from_core, from_vis, from_both], final_weight)
        words_out = (mine + wide(shifted(sent, "enc", 1))).reshape(words.shape)
        vision_rows = jnp.where(
            vis == 0,
            jnp.concatenate([my_vision, other_vision]),
            jnp.concatenate([other_vision, my_vision]),
        )
        return (vision_rows[None], slim(words + words_out))
    my_vision = slim(sum([wide(part) for part in home]))

    ends = jnp.cumsum(cand_counts)
    start = ends[group] - cand_counts[group]
    near_ids = start * CAP + jnp.arange(most * CAP, dtype=jnp.int32)
    owned = near_ids < ends[group] * CAP

    def ids_of(core_at, sign):
        steps = jnp.arange(places, dtype=jnp.int32)[:, None]
        first = ((place + sign * steps) % places * cores + core_at) * word_rows
        return (first + jnp.arange(word_rows, dtype=jnp.int32)[None]).reshape(-1)

    core_order = [core, 1 - core][:cores]
    near = 0.0
    for core_at, block in zip(core_order, word_blocks):
        pick = near_ids[:, None] == ids_of(core_at, -1)[None, :]
        near = near + dot(pick.astype(jnp.bfloat16), block)
    near = slim(near)
    place_ids = jnp.concatenate(
        [ids_of(core_at, 1).reshape(places, word_rows) for core_at in core_order], axis=1
    ).reshape(-1)
    put = slim((place_ids[:, None] == near_ids[None, :]) & owned[None, :])
    def embed(block):
        partial = dot(block, project_weight)
        if enc_count == 2:
            full = partial + wide(shifted(slim(partial), "enc", 1))
        else:
            full = lax.psum(partial, "enc")
        return slim(full * encoder_gain), jnp.sum(full * full, axis=-1)

    vision_rows = joined(my_vision, "vis", 0)
    scaled, power = embed(vision_rows)
    total = head_sum(heads_of(scaled, qkv_weight[1:]))
    power = lax.psum(power, "vis")
    image_kv = slim(total * lax.rsqrt(power / width + EPSILON)[:, None, None])

    live = near[:, 3 * share] > 0
    near = near[:, : 3 * share].reshape(most * CAP, 3, share // DH, DH)
    row_cand = jnp.arange(most * CAP, dtype=jnp.int32) // CAP
    own_allowed = (row_cand[:, None] == row_cand[None, :]) & live[None, :]
    image_kv = image_kv.reshape(rows, 2, share // DH, DH)
    query = near[:, 0]

    def scores_of(keys):
        return jnp.einsum(
            "qhd,khd->hqk", query, keys, preferred_element_type=jnp.float32
        ) * DH ** (-0.5)

    def mixed(weights, values):
        return jnp.einsum(
            "hqk,khd->hqd", slim(weights), values, preferred_element_type=jnp.float32
        )

    image_scores = scores_of(image_kv[:, 0])
    own_scores = jnp.where(own_allowed[None], scores_of(near[:, 1]), FLOOR)
    top = jnp.maximum(
        jnp.max(image_scores, axis=-1, keepdims=True), jnp.max(own_scores, axis=-1, keepdims=True)
    )
    image_weights = jnp.exp(image_scores - top)
    own_weights = jnp.where(own_allowed[None], jnp.exp(own_scores - top), 0.0)
    total = jnp.sum(image_weights, axis=-1, keepdims=True) + jnp.sum(
        own_weights, axis=-1, keepdims=True
    )
    result = (mixed(image_weights, image_kv[:, 1]) + mixed(own_weights, near[:, 2])) / total
    result = slim(result).transpose(1, 0, 2).reshape(most * CAP, share)
    spread_out = slim(dot(put, result)).reshape(places, cores * word_rows, share)
    landed = spread_out[0]
    for step in range(1, places):
        landed = landed + to_place(spread_out[step], step)
    kept = landed[:word_rows]
    attended = kept
    if cores == 2:
        given = landed[word_rows:]
        attended = kept + lax.ppermute(given, "grp", core_swap)
    if shares > 1:
        attended = lax.all_gather(attended, "vis", axis=1, tiled=True)
    partial_words = dot(attended, out_weight).reshape(cand_local, CAP, out_weight.shape[1])
    words_out = lax.psum_scatter(partial_words, "enc", scatter_dimension=1, tiled=True)
    caption_out = slim(words + words_out)
    return (vision_rows[None], caption_out)


def solution(mesh):
    return jax.shard_map(
        on_device,
        mesh=mesh,
        in_specs=(
            P("grp", None, "enc"),
            P("enc"),
            P("enc", ("vis", "grp")),
            P(("vis", "grp"), "enc"),
            P("enc", "vis"),
            P("vis"),
            P(None, "vis", "enc"),
            P("enc", "vis"),
            P("grp", "enc", "vis"),
            P(),
            P("grp"),
        ),
        out_specs=(P("grp", None, "enc"), P("grp", "enc", "vis")),
        check_vma=False,
    )
```
